32 devices in a mesh: var: 16 (over z, y, core), win: 2 (over x).
Axes of the slice: x: 2, y: 2, z: 4, core: 2. Of those that a mesh axis runs over, the one named last changes fastest.
Arguments:
- series: float32 [64, 896, 96], P('var', 'win'), may hold values from -30 to 30
- target: float32 [64, 896, 96], P('var', 'win'), may hold values from -30 to 30
- valid_slots: int32 [896], P('win'), may hold values 0 or 1
- observed: int32 [64, 896, 96], P('var', 'win'), may hold values from 0 to 1
- embed_weight: float32 [96, 512], P(None, 'var'), may hold values from -0.625 to 0.625
- joint_proj: float32 [1, 512, 1536], P(None, 'var'), may hold values from -0.25 to 0.25
- out_proj: float32 [1, 512, 512], P(None, 'var'), may hold values from -1.5 to 1.5
- up_proj: float32 [1, 512, 2048], P(None, 'var'), may hold values from -0.25 to 0.25
- down_proj: float32 [1, 2048, 512], P(None, 'var'), may hold values from -0.125 to 0.125
- head_weight: float32 [512, 96], P('var'), may hold values from -0.25 to 0.25
- norm_params: float32 [1, 4, 512], P(None, None, 'var'), may hold values from -0.6 to 1.3
- embed_mean: float32 [96, 512], P(None, 'var'), may hold values from -0.001953125 to 0.001953125
- joint_mean: float32 [1, 512, 1536], P(None, 'var'), may hold values from -0.00048828125 to 0.00048828125
- out_mean: float32 [1, 512, 512], P(None, 'var'), may hold values from -0.00048828125 to 0.00048828125
- up_mean: float32 [1, 512, 2048], P(None, 'var'), may hold values from -0.00048828125 to 0.00048828125
- down_mean: float32 [1, 2048, 512], P(None, 'var'), may hold values from -0.00048828125 to 0.00048828125
- head_mean: float32 [512, 96], P('var'), may hold values from -0.001953125 to 0.001953125
- norm_mean: float32 [1, 4, 512], P(None, None, 'var'), may hold values from -0.00390625 to 0.00390625
- embed_square: float32 [96, 512], P(None, 'var'), may hold values from 4.045759e-09 to 6.417411e-08
- joint_square: float32 [1, 512, 1536], P(None, 'var'), may hold values from 2.5285993e-10 to 4.010882e-09
- out_square: float32 [1, 512, 512], P(None, 'var'), may hold values from 2.5285993e-10 to 4.010882e-09
- up_square: float32 [1, 512, 2048], P(None, 'var'), may hold values from 2.5285993e-10 to 4.010882e-09
- down_square: float32 [1, 2048, 512], P(None, 'var'), may hold values from 2.5285993e-10 to 4.010882e-09
- head_square: float32 [512, 96], P('var'), may hold values from 4.045759e-09 to 6.417411e-08
- norm_square: float32 [1, 4, 512], P(None, None, 'var'), may hold values from 1.6183035e-08 to 2.5634765e-07
Outputs:
- loss: float32 [1], replicated
- new_embed: float32 [96, 512], P(None, 'var')
- new_joint: float32 [1, 512, 1536], P(None, 'var')
- new_out: float32 [1, 512, 512], P(None, 'var')
- new_up: float32 [1, 512, 2048], P(None, 'var')
- new_down: float32 [1, 2048, 512], P(None, 'var')
- new_head: float32 [512, 96], P('var')
- norm_grad: float32 [1, 4, 512], P(None, None, 'var')
- next_embed_mean: float32 [96, 512], P(None, 'var')
- next_joint_mean: float32 [1, 512, 1536], P(None, 'var')
- next_out_mean: float32 [1, 512, 512], P(None, 'var')
- next_up_mean: float32 [1, 512, 2048], P(None, 'var')
- next_down_mean: float32 [1, 2048, 512], P(None, 'var')
- next_head_mean: float32 [512, 96], P('var')
- next_norm_mean: float32 [1, 4, 512], P(None, None, 'var')
- next_embed_square: float32 [96, 512], P(None, 'var')
- next_joint_square: float32 [1, 512, 1536], P(None, 'var')
- next_out_square: float32 [1, 512, 512], P(None, 'var')
- next_up_square: float32 [1, 512, 2048], P(None, 'var')
- next_down_square: float32 [1, 2048, 512], P(None, 'var')
- next_head_square: float32 [512, 96], P('var')
- next_norm_square: float32 [1, 4, 512], P(None, None, 'var')
The draws below stay inside these ranges and needn't reach their ends.
All inputs are finite; a program needn't handle non-finite values. No bound on the sum of `valid_slots` on one device may be relied on, other than what follows from the above.
Results may differ from the reference program's by a relative error of at most 0.018.
Values may be sent and summed in bfloat16 or wider, within the bound.
No kernel may reach another device: no remote copies, remote signals or barrier semaphores. Data moves between devices by JAX's collectives and lax.ppermute only.
A program may use at most 320 MiB of HBM per device.

```python
import math
import jax
import jax.numpy as jnp
from jax import lax

D = 512
HEADS = 8
HEAD_SIZE = 64
FF = 2048
LOOK = 96
HORIZON = 96
VARS = 896
LAYERS = 1
STEP_NUMBER = 10
WINDOWS = 64


def variate_law(key):
    base = jax.random.fold_in(key, 11)
    first_key, second_key = jax.random.split(base)
    scales = jnp.exp(jax.random.uniform(first_key, (WINDOWS, VARS, 1), jnp.float32, jnp.log(0.5), jnp.log(4.0)))
    offsets = 2.0 * jnp.clip(jax.random.normal(second_key, (WINDOWS, VARS, 1), jnp.float32), -3.0, 3.0)
    return (scales, offsets)


def draw_series(key, part):
    scales, offsets = variate_law(key)
    noise_key = jax.random.fold_in(key, 21)
    noise = jnp.clip(jax.random.normal(noise_key, (WINDOWS, VARS, LOOK), jnp.float32), -6.0, 6.0)
    return offsets + scales * noise


def draw_target(key, part):
    scales, offsets = variate_law(key)
    noise_key = jax.random.fold_in(key, 22)
    noise = jnp.clip(jax.random.normal(noise_key, (WINDOWS, VARS, HORIZON), jnp.float32), -6.0, 6.0)
    return offsets + scales * noise


def draw_observed(key, part):
    window_index = jnp.arange(WINDOWS, dtype=jnp.int32)[:, None, None]
    slot_index = jnp.arange(VARS, dtype=jnp.int32)[None, :, None]
    level = 250 + 500 * window_index // max(WINDOWS - 1, 1) + 250 * slot_index // max(VARS - 1, 1)
    rolled = jax.random.randint(jax.random.fold_in(key, 41), (WINDOWS, VARS, HORIZON), 0, 1000)
    return (rolled < level).astype(jnp.int32)


def draw_norm_params(key, part):
    raw = jnp.clip(jax.random.normal(jax.random.fold_in(key, 31), (LAYERS, 4, D), jnp.float32), -3.0, 3.0)
    centres = jnp.array([1.0, 0.0, 1.0, 0.0], jnp.float32)[None, :, None]
    widths = jnp.array([0.1, 0.2, 0.1, 0.2], jnp.float32)[None, :, None]
    return centres + widths * raw


def with_ends(drawn, key, low, high):
    longest = drawn.shape.index(max(drawn.shape))
    spots = []
    for shift in (0, 1):
        where = [jax.random.randint(jax.random.fold_in(key, axis), (), 0, length) for axis, length in enumerate(drawn.shape)]
        where[longest] = (where[longest] + shift) % drawn.shape[longest]
        spots.append(tuple(where))
    return drawn.at[spots[0]].set(low).at[spots[1]].set(high)


def block_scale(rng, dims, cuts, least, top_value):
    factor_of = 1.0
    for position, parts in cuts:
        heights = jax.random.uniform(jax.random.fold_in(jax.random.fold_in(rng, 6), position), (parts,), jnp.float32, least / len(cuts), top_value / len(cuts))
        factor_of = factor_of * jnp.repeat(jnp.exp(heights), dims[position] // parts).reshape((-1,) + (1,) * (len(dims) - 1 - position))
    return factor_of


def bell_draw(rng, dims, width, reach, pieces=(), held_as=jnp.bfloat16):
    values = jax.random.normal(rng, dims, jnp.float32) * width
    if len(pieces) > 0:
        values = block_scale(rng, dims, pieces, -0.22, 0.18) * values
    return jnp.clip(values, min=-reach, max=reach).astype(held_as)


def setup_inputs(seed: int = 0) -> dict:
    arg_keys = jax.random.split(jax.random.key(seed), 26)
    series = draw_series(jax.random.fold_in(arg_keys[25], 71), 0)
    target = draw_target(jax.random.fold_in(arg_keys[25], 71), 0)
    valid_slots = with_ends((jax.random.randint(arg_keys[2], (VARS,), 0, 32) < 31).astype(jnp.int32), jax.random.fold_in(arg_keys[2], 1), 0, 1)
    observed = draw_observed(jax.random.fold_in(arg_keys[25], 71), 0)
    embed_weight = bell_draw(arg_keys[4], (LOOK, D), LOOK ** -0.5, 0.625, ((1, 16),), jnp.float32)
    joint_proj = bell_draw(arg_keys[5], (LAYERS, D, 3 * D), D ** -0.5, 0.25, ((1, 16),), jnp.float32)
    out_proj = bell_draw(arg_keys[6], (LAYERS, D, D), (D // 32) ** -0.5, 1.5, ((1, 16),), jnp.float32)
    up_proj = bell_draw(arg_keys[7], (LAYERS, D, FF), D ** -0.5, 0.25, ((1, 16),), jnp.float32)
    down_proj = bell_draw(arg_keys[8], (LAYERS, FF, D), FF ** -0.5, 0.125, ((1, 16),), jnp.float32)
    head_weight = bell_draw(arg_keys[9], (D, HORIZON), D ** -0.5, 0.25, ((0, 16),), jnp.float32)
    norm_params = draw_norm_params(jax.random.fold_in(arg_keys[25], 71), 0)
    embed_mean = bell_draw(arg_keys[11], (LOOK, D), (0.076 * (WINDOWS * VARS) ** -0.5), 0.001953125, ((1, 16),), jnp.float32)
    joint_mean = bell_draw(arg_keys[12], (LAYERS, D, 3 * D), (0.019 * (WINDOWS * VARS) ** -0.5), 0.00048828125, ((1, 16),), jnp.float32)
    out_mean = bell_draw(arg_keys[13], (LAYERS, D, D), (0.019 * (WINDOWS * VARS) ** -0.5), 0.00048828125, ((1, 16),), jnp.float32)
    up_mean = bell_draw(arg_keys[14], (LAYERS, D, FF), (0.019 * (WINDOWS * VARS) ** -0.5), 0.00048828125, ((1, 16),), jnp.float32)
    down_mean = bell_draw(arg_keys[15], (LAYERS, FF, D), (0.019 * (WINDOWS * VARS) ** -0.5), 0.00048828125, ((1, 16),), jnp.float32)
    head_mean = bell_draw(arg_keys[16], (D, HORIZON), (0.076 * (WINDOWS * VARS) ** -0.5), 0.001953125, ((0, 16),), jnp.float32)
    norm_mean = bell_draw(arg_keys[17], (LAYERS, 4, D), (0.152 * (WINDOWS * VARS) ** -0.5), 0.00390625, ((2, 16),), jnp.float32)
    embed_square = jnp.clip(jnp.exp(math.log(6.417410958192704e-08) - 2.7639307 * jax.random.uniform(arg_keys[18], (LOOK, D), jnp.float32) ** block_scale(arg_keys[18], (LOOK, D), ((1, 16),), -0.2, 0.2)), 4.045758839055225e-09, 6.417410958192704e-08)
    joint_square = jnp.clip(jnp.exp(math.log(4.01088184887044e-09) - 2.7639307 * jax.random.uniform(arg_keys[19], (LAYERS, D, 3 * D), jnp.float32) ** block_scale(arg_keys[19], (LAYERS, D, 3 * D), ((1, 16),), -0.2, 0.2)), 2.5285992744095154e-10, 4.01088184887044e-09)
    out_square = jnp.clip(jnp.exp(math.log(4.01088184887044e-09) - 2.7639307 * jax.random.uniform(arg_keys[20], (LAYERS, D, D), jnp.float32) ** block_scale(arg_keys[20], (LAYERS, D, D), ((1, 16),), -0.2, 0.2)), 2.5285992744095154e-10, 4.01088184887044e-09)
    up_square = jnp.clip(jnp.exp(math.log(4.01088184887044e-09) - 2.7639307 * jax.random.uniform(arg_keys[21], (LAYERS, D, FF), jnp.float32) ** block_scale(arg_keys[21], (LAYERS, D, FF), ((1, 16),), -0.2, 0.2)), 2.5285992744095154e-10, 4.01088184887044e-09)
    down_square = jnp.clip(jnp.exp(math.log(4.01088184887044e-09) - 2.7639307 * jax.random.uniform(arg_keys[22], (LAYERS, FF, D), jnp.float32) ** block_scale(arg_keys[22], (LAYERS, FF, D), ((1, 16),), -0.2, 0.2)), 2.5285992744095154e-10, 4.01088184887044e-09)
    head_square = jnp.clip(jnp.exp(math.log(6.417410958192704e-08) - 2.7639307 * jax.random.uniform(arg_keys[23], (D, HORIZON), jnp.float32) ** block_scale(arg_keys[23], (D, HORIZON), ((0, 16),), -0.2, 0.2)), 4.045758839055225e-09, 6.417410958192704e-08)
    norm_square = jnp.clip(jnp.exp(math.log(2.5634764710957825e-07) - 2.762571 * jax.random.uniform(arg_keys[24], (LAYERS, 4, D), jnp.float32) ** block_scale(arg_keys[24], (LAYERS, 4, D), ((2, 16),), -0.2, 0.2)), 1.61830353562209e-08, 2.5634764710957825e-07)
    return dict(series=series, target=target, valid_slots=valid_slots, observed=observed, embed_weight=embed_weight, joint_proj=joint_proj, out_proj=out_proj, up_proj=up_proj, down_proj=down_proj, head_weight=head_weight, norm_params=norm_params, embed_mean=embed_mean, joint_mean=joint_mean, out_mean=out_mean, up_mean=up_mean, down_mean=down_mean, head_mean=head_mean, norm_mean=norm_mean, embed_square=embed_square, joint_square=joint_square, out_square=out_square, up_square=up_square, down_square=down_square, head_square=head_square, norm_square=norm_square)


highest = lax.Precision.HIGHEST

@jax.custom_vjp
def low(v):
    return lax.optimization_barrier(v.astype(jnp.bfloat16)).astype(jnp.float32)

@jax.custom_vjp
def low_back(v):
    return v

def low_keep(v):
    return (low(v), None)

def low_pass(kept, grad):
    return (grad,)

def back_keep(v):
    return (v, None)

def back_low(kept, grad):
    return (low(grad),)
low.defvjp(low_keep, low_pass)
low_back.defvjp(back_keep, back_low)

def matmul(left, right):
    return jnp.dot(left, right, precision=highest, preferred_element_type=jnp.float32)

def layer_norm(resid, gain, shift):
    centre = lax.optimization_barrier(jnp.mean(resid, -1, keepdims=True))
    offset = resid - centre
    spread = lax.optimization_barrier(jnp.mean(offset * offset, -1, keepdims=True))
    return offset * lax.rsqrt(spread + 1e-05) * gain + shift

def attention(query_rows, key_portion, value_rows, allowed):
    score_matrix = low_back(jnp.einsum('hqd,hkd->hqk', query_rows, key_portion, precision=highest) * 0.125)
    score_matrix = jnp.where(allowed[None], score_matrix, -1e+30)
    weights = low(jax.nn.softmax(score_matrix, axis=-1))
    return jnp.einsum('hqk,hkd->hqd', weights, value_rows, precision=highest)

def window_loss(params, history, future, weighting, allowed):
    embed_weight, joint_proj, out_proj, up_proj, down_proj, head_weight, norm_params = params
    centre = lax.optimization_barrier(jnp.mean(history, -1, keepdims=True))
    offset = history - centre
    spread = jnp.sqrt(lax.optimization_barrier(jnp.mean(offset * offset, -1, keepdims=True)) + 1e-05)
    hidden = low_back(matmul(low(offset / spread), embed_weight))
    for layer in range(LAYERS):
        split = matmul(low(hidden), joint_proj[layer]).reshape(VARS, 3, HEADS, HEAD_SIZE).transpose(1, 2, 0, 3)
        query_rows = low_back(low(split[0]))
        key_portion = low_back(low(split[1]))
        value_rows = low_back(low(split[2]))
        mixed = attention(query_rows, key_portion, value_rows, allowed).transpose(1, 0, 2).reshape(VARS, D)
        mixed = low_back(mixed)
        branch = low_back(matmul(low(mixed), out_proj[layer]))
        middle = layer_norm(hidden + branch, norm_params[layer, 0], norm_params[layer, 1])
        pre_gelu = low_back(matmul(low(middle), up_proj[layer]))
        activated = low(jax.nn.gelu(pre_gelu, approximate=False))
        branch = low_back(matmul(activated, down_proj[layer]))
        hidden = layer_norm(middle + branch, norm_params[layer, 2], norm_params[layer, 3])
    guess = low_back(matmul(low(hidden), head_weight)) * spread + centre
    error = guess - future
    return jnp.sum(weighting * error * error)

def adamw(weight, mean, square, grad, count_step):
    mean_next = 0.9 * mean + 0.1 * grad
    square_next = 0.999 * square + 0.001 * grad * grad
    mean_hat = mean_next / (1.0 - 0.9 ** count_step)
    square_hat = square_next / (1.0 - 0.999 ** count_step)
    weight_next = weight - 0.1 * (mean_hat / (jnp.sqrt(square_hat) + 1e-08) + 0.1 * weight)
    return (weight_next, mean_next, square_next)

def reference(series, target, valid_slots, observed, embed_weight, joint_proj, out_proj, up_proj, down_proj, head_weight, norm_params, embed_mean, joint_mean, out_mean, up_mean, down_mean, head_mean, norm_mean, embed_square, joint_square, out_square, up_square, down_square, head_square, norm_square):
    weights = (embed_weight, joint_proj, out_proj, up_proj, down_proj, head_weight, norm_params)
    means = (embed_mean, joint_mean, out_mean, up_mean, down_mean, head_mean, norm_mean)
    squares = (embed_square, joint_square, out_square, up_square, down_square, head_square, norm_square)
    valid_float = valid_slots.astype(jnp.float32)
    weight_mask = observed.astype(jnp.float32) * valid_float[None, :, None]
    count = jnp.maximum(jnp.sum(weight_mask), 1.0)
    slot_index = jnp.arange(VARS, dtype=jnp.int32)
    allowed = (valid_slots[None, :] > 0) | (slot_index[:, None] == slot_index[None, :])

    def total_loss(params):
        lowered = tuple((low(p) for p in params))

        def one_window(history, future, weighting):
            return window_loss(lowered, history, future, weighting, allowed)
        checked = jax.checkpoint(one_window)

        def add_window(carry, item):
            return (carry + checked(item[0], item[1], item[2]), None)
        summed, _ = lax.scan(add_window, jnp.zeros((), jnp.float32), (series, target, weight_mask))
        return summed / count
    loss, pull = jax.vjp(total_loss, weights)
    grads = pull(jnp.ones_like(loss))[0]
    count_step = float(STEP_NUMBER)
    results = [adamw(weights[i], means[i], squares[i], grads[i], count_step) for i in range(7)]
    return (loss.reshape(1), results[0][0], results[1][0], results[2][0], results[3][0], results[4][0], results[5][0], grads[6], results[0][1], results[1][1], results[2][1], results[3][1], results[4][1], results[5][1], results[6][1], results[0][2], results[1][2], results[2][2], results[3][2], results[4][2], results[5][2], results[6][2])
```

```python
from functools import partial

import jax
import jax.numpy as jnp
from jax import lax
from jax.experimental import pallas as pl
from jax.experimental.pallas import tpu as pltpu
from jax.sharding import PartitionSpec as P

HEADS = 8
HEAD_SIZE = 64
LAYERS = 1
STEP_NUMBER = 10

F32 = jnp.float32
BF16 = jnp.bfloat16
LANES = 128
D = HEADS * HEAD_SIZE
PARTS = 16
ROWS = D // PARTS
MIB = 1 << 20

OUT_AT, UP_AT, DOWN_AT, HEAD_AT, LOSS_AT, BUNDLE = 0, 128, 640, 1152, 1184, 1200
EMBED_AT, FIRST = 384, 416


def dot_nn(a, b):
    return lax.dot_general(a, b, (((1,), (0,)), ((), ())), preferred_element_type=F32)


def dot_nt(a, b):
    return lax.dot_general(a, b, (((1,), (1,)), ((), ())), preferred_element_type=F32)


def dot_tn(a, b):
    return lax.dot_general(a, b, (((0,), (0,)), ((), ())), preferred_element_type=F32)


def offset_of(slot):
    return (slot % 4) * 4 + (slot // 4 % 2) * 2 + slot // 8


def slot_of(offset):
    return (offset & 1) * 8 + ((offset >> 1) & 1) * 4 + (offset >> 2)


def lane_index(shape):
    return lax.broadcasted_iota(jnp.int32, shape, len(shape) - 1)


def params(limit=56, **more):
    return pltpu.CompilerParams(vmem_limit_bytes=limit * MIB, **more)


def cost(flops, moved):
    return pl.CostEstimate(flops=int(flops), bytes_accessed=int(moved), transcendentals=0)


def swapped(block, axis, distance):
    count = lax.axis_size(axis)
    return lax.ppermute(block, axis, [(i, i ^ distance) for i in range(count)])


def gathered(block):
    along_z = [block] + [swapped(block, "var", 4 * i) for i in (1, 2, 3)]
    plane = jnp.stack(along_z)
    across = swapped(plane, "var", 2)
    return (plane, across, swapped(plane, "var", 1), swapped(across, "var", 1))


def added(*terms):
    total = terms[0].astype(F32)
    for term in terms[1:]:
        total = total + term.astype(F32)
    return total.astype(BF16)


def scattered(kept, leaving):
    plane = added(kept, swapped(leaving, "var", 1))
    row = added(plane[:4], swapped(plane[4:], "var", 2))
    mine = added(row[0], *[swapped(row[i], "var", 4 * i) for i in (1, 2, 3)])
    return (mine, swapped(mine, "win", 1))


def prep_kernel(pos_ref, series, target, observed, valid, kept_n, sent_n, kept_t, sent_t, count, total):
    step = pl.program_id(0)
    steps = pl.num_programs(0)
    half = steps // 2
    local = series.shape[1]
    rows = series[0]
    centre = jnp.mean(rows, -1, keepdims=True)
    offset = rows - centre
    spread = jnp.sqrt(jnp.mean(offset * offset, -1, keepdims=True) + 1e-05)
    normed = offset / spread
    mark = valid[...].astype(F32)
    weight = observed[0].astype(F32) * mark

    @pl.when(step == 0)
    def _():
        total[...] = jnp.zeros_like(total)

    total[...] += jnp.sum(jnp.sum(weight, 0, keepdims=True), 1, keepdims=True)
    spare = (local, LANES - rows.shape[-1])
    lane = lane_index(spare)
    extra_n = jnp.where(lane == 0, mark, 0.0)
    extra_t = jnp.where(
        lane == 0,
        centre,
        jnp.where(lane == 1, spread, jnp.where(lane == 2, total[0:1, 0:1], 0.0)),
    )
    look = rows.shape[-1]

    def write(n_ref, t_ref):
        n_ref[0, :, 0:look] = normed.astype(BF16)
        n_ref[0, :, look:LANES] = extra_n.astype(BF16)
        t_ref[0, :, 0:look] = target[0]
        t_ref[0, :, look:LANES] = extra_t
        t_ref[0, :, LANES : LANES + look] = weight
        t_ref[0, :, LANES + look :] = jnp.zeros(spare, F32)

    @pl.when(step < half)
    def _():
        write(kept_n, kept_t)

    @pl.when(step >= half)
    def _():
        write(sent_n, sent_t)

    count[...] = total[...]


def prep(pos, series, target, observed, valid):
    windows, local, look = series.shape
    half = windows // 2

    def source(i, pos_ref):
        return (lax.rem(pos_ref[0] * half + i, windows), 0, 0)

    def kept(i, pos_ref):
        return (jnp.minimum(i, half - 1), 0, 0)

    def sent(i, pos_ref):
        return (jnp.maximum(i - half, 0), 0, 0)

    block = pl.BlockSpec((1, local, look), source)
    return pl.pallas_call(
        prep_kernel,
        grid_spec=pltpu.PrefetchScalarGridSpec(
            num_scalar_prefetch=1,
            grid=(windows,),
            in_specs=[block, block, block, pl.BlockSpec((local, 1), lambda i, p: (0, 0))],
            out_specs=[
                pl.BlockSpec((1, local, LANES), kept),
                pl.BlockSpec((1, local, LANES), sent),
                pl.BlockSpec((1, local, 2 * LANES), kept),
                pl.BlockSpec((1, local, 2 * LANES), sent),
                pl.BlockSpec((8, LANES), lambda i, p: (0, 0)),
            ],
            scratch_shapes=[pltpu.VMEM((8, LANES), F32)],
        ),
        out_shape=[
            jax.ShapeDtypeStruct((half, local, LANES), BF16),
            jax.ShapeDtypeStruct((half, local, LANES), BF16),
            jax.ShapeDtypeStruct((half, local, 2 * LANES), F32),
            jax.ShapeDtypeStruct((half, local, 2 * LANES), F32),
            jax.ShapeDtypeStruct((8, LANES), F32),
        ],
        compiler_params=params(),
        cost_estimate=cost(0, 8 * MIB),
        name="prep",
    )(pos, series, target, observed, valid)


def pack_first_kernel(joint, embed, out):
    for c in range(12):
        out[c * ROWS : (c + 1) * ROWS, :] = joint[0, :, c * LANES : (c + 1) * LANES].astype(BF16)
    look = embed.shape[-1]
    out[EMBED_AT:FIRST, 0:look] = embed[...].astype(BF16)
    out[EMBED_AT:FIRST, look:] = jnp.zeros((ROWS, LANES - look), BF16)


def pack_first(joint, embed):
    return pl.pallas_call(
        pack_first_kernel,
        out_shape=jax.ShapeDtypeStruct((FIRST, LANES), BF16),
        compiler_params=params(),
        cost_estimate=cost(0, MIB // 2),
        name="pack_first",
    )(joint, embed)


def pack_second_kernel(own, other, out_w, up, down, head, norm, out):
    for c in range(4):
        out[OUT_AT + c * ROWS : OUT_AT + (c + 1) * ROWS, :] = out_w[
            0, :, c * LANES : (c + 1) * LANES
        ].astype(BF16)
    for c in range(16):
        out[UP_AT + c * ROWS : UP_AT + (c + 1) * ROWS, :] = up[
            0, :, c * LANES : (c + 1) * LANES
        ].astype(BF16)
    for c in range(4):
        out[DOWN_AT + c * LANES : DOWN_AT + (c + 1) * LANES, :] = down[
            0, :, c * LANES : (c + 1) * LANES
        ].astype(BF16)
    horizon = head.shape[-1]
    spare = (ROWS, LANES - horizon)
    lane = lane_index(spare)
    count = own[0:1, 0:1] + other[...]
    high = count.astype(BF16).astype(F32)
    middle = (count - high).astype(BF16).astype(F32)
    low = (count - high - middle).astype(BF16).astype(F32)
    extra = jnp.zeros(spare, F32)
    for i in range(4):
        extra = jnp.where(lane == i, norm[:, i : i + 1], extra)
    for i, piece in enumerate((high, middle, low)):
        extra = jnp.where(lane == 4 + i, piece, extra)
    out[HEAD_AT:LOSS_AT, 0:horizon] = head[...].astype(BF16)
    out[HEAD_AT:LOSS_AT, horizon:] = extra.astype(BF16)
    out[LOSS_AT:BUNDLE, :] = jnp.zeros((BUNDLE - LOSS_AT, LANES), BF16)


def pack_second(own, other, out_w, up, down, head, norm):
    return pl.pallas_call(
        pack_second_kernel,
        out_shape=jax.ShapeDtypeStruct((BUNDLE, LANES), BF16),
        compiler_params=params(),
        cost_estimate=cost(0, MIB),
        name="pack_second",
    )(own, other, out_w, up, down, head, norm)


def project_kernel(me_ref, g0, g1, g2, g3, kept, came, qkv, hid, joint, embed):
    @pl.when(pl.program_id(0) == 0)
    def _():
        me = me_ref[0]
        for slot in range(PARTS):
            block = (g0, g1, g2, g3)[slot // 4]
            owner = me ^ offset_of(slot)
            for c in range(12):
                joint[owner, :, c * LANES : (c + 1) * LANES] = block[
                    slot % 4, c * ROWS : (c + 1) * ROWS, :
                ]
            embed[owner] = block[slot % 4, EMBED_AT:FIRST, :]

    normed = jnp.concatenate([kept[0], came[0]], axis=0)
    low = dot_nt(embed[...].reshape(D, LANES), normed).astype(BF16)
    hid[...] = low
    for part in range(3):
        weights = joint[:, :, part * D : (part + 1) * D].reshape(D, D)
        rows = dot_tn(weights, low)
        if part == 0:
            rows = rows.astype(BF16).astype(F32) * 0.125
        qkv[part * D : (part + 1) * D, :] = rows.astype(BF16)


def project(me, bundle, kept, came):
    half, local, _ = kept.shape
    slots = 2 * local
    whole = pl.BlockSpec((4, FIRST, LANES), lambda w, m: (0, 0, 0))
    mine = pl.BlockSpec((1, local, LANES), lambda w, m: (w, 0, 0))
    return pl.pallas_call(
        project_kernel,
        grid_spec=pltpu.PrefetchScalarGridSpec(
            num_scalar_prefetch=1,
            grid=(half,),
            in_specs=[whole] * 4 + [mine] * 2,
            out_specs=[
                pl.BlockSpec((3 * D, slots), lambda w, m: (0, w)),
                pl.BlockSpec((D, slots), lambda w, m: (0, w)),
                pl.BlockSpec((PARTS, ROWS, 3 * D), lambda w, m: (0, 0, 0)),
                pl.BlockSpec((PARTS, ROWS, LANES), lambda w, m: (0, 0, 0)),
            ],
        ),
        out_shape=[
            jax.ShapeDtypeStruct((3 * D, half * slots), BF16),
            jax.ShapeDtypeStruct((D, half * slots), BF16),
            jax.ShapeDtypeStruct((PARTS, ROWS, 3 * D), BF16),
            jax.ShapeDtypeStruct((PARTS, ROWS, LANES), BF16),
        ],
        compiler_params=params(),
        cost_estimate=cost(3e9, 12 * MIB),
        name="project",
    )(me, *bundle, kept, came)


def tiles_of(length, size):
    return [(at, min(size, length - at)) for at in range(0, length, size)]


def attend_kernel(kept, came, q, k, v, weights, mixed, scale, bias):
    slots = q.shape[1]
    local = slots // 2

    @pl.when((pl.program_id(0) == 0) & (pl.program_id(1) == 0))
    def _():
        for part, marks in enumerate((kept, came)):
            rows = slice(part * local, (part + 1) * local)
            mark = marks[0, :, 96:97].astype(F32)
            key = part * local + lax.broadcasted_iota(jnp.int32, (local, slots), 0)
            query = lane_index((local, slots))
            bias[rows, :] = jnp.where((mark > 0.5) | (key == query), 0.0, -1e30)

    keys = k[...].T
    for at, size in tiles_of(slots, 256):
        cols = slice(at, at + size)
        score = dot_nn(keys, q[:, cols]) + bias[:, cols]
        top = jnp.max(score, 0, keepdims=True)
        weight = jnp.exp(score - top)
        low = weight.astype(BF16)
        weights[0, :, cols] = low
        inverse = 1.0 / jnp.sum(weight, 0, keepdims=True)
        scale[0, :, cols] = inverse
        mixed[:, cols] = (dot_nn(v[...], low) * inverse).astype(BF16)


def attend(first, count, kept, came, qkv):
    half, local, _ = kept.shape
    slots = 2 * local
    marks = pl.BlockSpec((1, local, LANES), lambda h, w: (0, 0, 0))

    def head(part):
        return pl.BlockSpec((HEAD_SIZE, slots), lambda h, w: (part * HEADS + first + h, w))

    return pl.pallas_call(
        attend_kernel,
        grid=(count, half),
        in_specs=[marks, marks, head(0), head(1), head(2)],
        out_specs=[
            pl.BlockSpec((1, slots, slots), lambda h, w: (h * half + w, 0, 0)),
            pl.BlockSpec((HEAD_SIZE, slots), lambda h, w: (h, w)),
            pl.BlockSpec((1, 1, slots), lambda h, w: (h * half + w, 0, 0)),
        ],
        out_shape=[
            jax.ShapeDtypeStruct((count * half, slots, slots), BF16),
            jax.ShapeDtypeStruct((count * HEAD_SIZE, half * slots), BF16),
            jax.ShapeDtypeStruct((count * half, 1, slots), F32),
        ],
        scratch_shapes=[pltpu.VMEM((slots, slots), F32)],
        compiler_params=params(),
        cost_estimate=cost(count * half * 1.2e9, count * half * 2 * MIB),
        name="attend",
    )(kept, came, qkv, qkv, qkv)


def unattend_kernel(
    me_ref, weights, scale, mixed, dmixed, q, k, v, hid, dproj, kept, leaving, rows, packed, sems
):
    head, window = pl.program_id(0), pl.program_id(1)
    slots = q.shape[1]
    dmix = dmixed[...].astype(F32) * scale[0]
    low = dmix.astype(BF16)
    delta = jnp.sum(low.astype(F32) * mixed[...].astype(F32), 0, keepdims=True)
    values = v[...].T
    keys = k[...]
    dval = jnp.zeros((HEAD_SIZE, slots), F32)
    dkey = jnp.zeros((HEAD_SIZE, slots), F32)
    for at, size in tiles_of(slots, 256):
        cols = slice(at, at + size)
        weight = weights[0, :, cols]
        dweight = dot_nn(values, low[:, cols])
        dscore = (weight.astype(F32) * (dweight - delta[:, cols])).astype(BF16)
        dproj[0, :, cols] = (dot_nn(keys, dscore) * 0.125).astype(BF16)
        dkey = dkey + dot_nt(q[:, cols], dscore)
        dval = dval + dot_nt(low[:, cols], weight)
    dproj[1] = dkey.astype(BF16)
    dproj[2] = dval.astype(BF16)
    start = pl.multiple_of(window * slots, LANES)
    for part in range(3):
        rows[part, head, :, pl.ds(start, slots)] = dproj[part]

    count = pl.num_programs(0)

    @pl.when((head == count - 1) & (window == pl.num_programs(1) - 1))
    def _():
        me = me_ref[0]
        width = rows.shape[1] * HEAD_SIZE
        for part in range(3):
            grad = dot_nt(hid[...], rows[part].reshape(width, rows.shape[-1])).astype(BF16)
            for b in range(PARTS):
                slot = slot_of(b ^ me)
                for c in range(width // LANES):
                    at = (part * (width // LANES) + c) * ROWS
                    packed[slot, at : at + ROWS, :] = grad[
                        b * ROWS : (b + 1) * ROWS, c * LANES : (c + 1) * LANES
                    ]
        send_packed(packed, kept, leaving, sems)


def send_packed(packed, kept, leaving, sems):
    half = PARTS // 2
    copies = [
        pltpu.make_async_copy(packed.at[pl.ds(0, half)], kept, sems.at[0]),
        pltpu.make_async_copy(packed.at[pl.ds(half, half)], leaving, sems.at[1]),
    ]
    for copy in copies:
        copy.start()
    for copy in copies:
        copy.wait()


def unattend(me, first, count, weights, scale, mixed, dmixed, qkv, hid):
    slots = weights.shape[-1]
    tokens = qkv.shape[1]
    half = tokens // slots
    height = 3 * count * HEAD_SIZE // LANES * ROWS

    def head(part):
        return pl.BlockSpec((HEAD_SIZE, slots), lambda h, w, m: (part * HEADS + first + h, w))

    return pl.pallas_call(
        unattend_kernel,
        grid_spec=pltpu.PrefetchScalarGridSpec(
            num_scalar_prefetch=1,
            grid=(count, half),
            in_specs=[
                pl.BlockSpec((1, slots, slots), lambda h, w, m: (h * half + w, 0, 0)),
                pl.BlockSpec((1, 1, slots), lambda h, w, m: (h * half + w, 0, 0)),
                pl.BlockSpec((HEAD_SIZE, slots), lambda h, w, m: (h, w)),
                pl.BlockSpec((HEAD_SIZE, slots), lambda h, w, m: (first + h, w)),
                head(0),
                head(1),
                head(2),
                pl.BlockSpec((D, tokens), lambda h, w, m: (0, 0)),
            ],
            out_specs=[
                pl.BlockSpec((3, HEAD_SIZE, slots), lambda h, w, m: (0, h, w)),
                pl.BlockSpec(memory_space=pl.ANY),
                pl.BlockSpec(memory_space=pl.ANY),
            ],
            scratch_shapes=[
                pltpu.VMEM((3, count, HEAD_SIZE, tokens), BF16),
                pltpu.VMEM((PARTS, height, LANES), BF16),
                pltpu.SemaphoreType.DMA((2,)),
            ],
        ),
        out_shape=[
            jax.ShapeDtypeStruct((3, count * HEAD_SIZE, tokens), BF16),
            jax.ShapeDtypeStruct((PARTS // 2, height, LANES), BF16),
            jax.ShapeDtypeStruct((PARTS // 2, height, LANES), BF16),
        ],
        compiler_params=params(),
        cost_estimate=cost(count * half * 2.5e9, count * half * 2 * MIB),
        name="unattend",
    )(me, weights, scale, mixed, dmixed, qkv, qkv, qkv, hid)


def gelu_parts(pre):
    bell = jnp.exp(pre * pre * -0.5)
    size = jnp.abs(pre)
    t = 1.0 / (1.0 + 0.23164190 * size)
    poly = t * (
        0.127414796
        + t * (-0.142248368 + t * (0.7107068705 + t * (-0.7265760135 + t * 0.5307027145)))
    )
    tail = poly * bell
    phi = jnp.where(pre >= 0.0, 1.0 - tail, tail)
    return (pre * phi, phi + pre * bell * 0.3989422804014327)


def norm_forward(resid, gain, shift):
    centre = jnp.mean(resid, 0, keepdims=True)
    offset = resid - centre
    inverse = lax.rsqrt(jnp.mean(offset * offset, 0, keepdims=True) + 1e-05)
    unit = offset * inverse
    return (unit * gain + shift, unit, inverse)


def norm_backward(grad, unit, inverse, gain):
    scaled = grad * gain
    first = jnp.mean(scaled, 0, keepdims=True)
    second = jnp.mean(scaled * unit, 0, keepdims=True)
    return (scaled - first - unit * second) * inverse


def middle_kernel(
    me_ref,
    g0,
    g1,
    g2,
    g3,
    embed,
    normed,
    future,
    mixed_a,
    mixed_b,
    dmixed,
    dattn,
    counted,
    kept,
    leaving,
    w_out,
    w_up,
    w_down,
    w_head,
    t_out,
    t_up,
    t_down,
    norms,
    slope,
    mixed_s,
    middle_s,
    active_s,
    dbranch_s,
    dpre_s,
    dattn_s,
    final_s,
    dguess_s,
    norm_sums,
    loss_sum,
    packed,
    sems,
):
    step = pl.program_id(0)
    size = dmixed.shape[1]
    ff = active_s.shape[0]
    chunks = ff // D

    @pl.when(step == 0)
    def _():
        me = me_ref[0]
        total = jnp.zeros((1, 1), F32)
        for slot in range(PARTS):
            block = (g0, g1, g2, g3)[slot // 4]
            i = slot % 4
            owner = me ^ offset_of(slot)
            for c in range(4):
                cols = slice(c * LANES, (c + 1) * LANES)
                at = OUT_AT + c * ROWS
                w_out[owner, :, cols] = block[i, at : at + ROWS, :]
                at = DOWN_AT + c * LANES
                w_down[owner, :, cols] = block[i, at : at + LANES, :]
            for c in range(16):
                at = UP_AT + c * ROWS
                w_up[owner, :, c * LANES : (c + 1) * LANES] = block[i, at : at + ROWS, :]
            head = block[i, HEAD_AT:LOSS_AT, :]
            w_head[owner] = head
            pieces = head[0:1, 100:103].astype(F32)
            total = total + jnp.sum(pieces, 1, keepdims=True)
        counted[...] = jnp.broadcast_to(jnp.maximum(total, 1.0), counted.shape)
        t_out[...] = w_out[...].reshape(D, D).T
        for c in range(chunks):
            rows = slice(c * D, (c + 1) * D)
            t_up[rows, :] = w_up[:, :, rows].reshape(D, D).T
            t_down[:, rows] = w_down[c * 4 : (c + 1) * 4].reshape(D, D).T
        extra = w_head[...].reshape(D, LANES)
        for i in range(4):
            column = extra[:, 96 + i : 97 + i].astype(F32)
            norms[i] = jnp.broadcast_to(column, (D, size))
        norm_sums[...] = jnp.zeros_like(norm_sums)
        loss_sum[...] = jnp.zeros_like(loss_sum)

    cols = pl.ds(pl.multiple_of(step * size, size), size)
    unit_of = normed[...]
    mixed = jnp.concatenate([mixed_a[...], mixed_b[...]], axis=0)
    mixed_s[:, cols] = mixed
    resid = dot_nt(embed[...].reshape(D, LANES), unit_of) + dot_nn(t_out[...], mixed)
    middle, unit_one, inverse_one = norm_forward(resid, norms[0], norms[1])
    middle_low = middle.astype(BF16)
    middle_s[:, cols] = middle_low
    resid = middle
    for c in range(chunks):
        rows = slice(c * D, (c + 1) * D)
        active, gradient = gelu_parts(dot_nn(t_up[rows, :], middle_low))
        active = active.astype(BF16)
        active_s[rows, cols] = active
        slope[rows, :] = gradient
        resid = resid + dot_nn(t_down[:, rows], active)
    final, unit_two, inverse_two = norm_forward(resid, norms[2], norms[3])
    final_low = final.astype(BF16)
    final_s[:, cols] = final_low
    w_h = w_head[...].reshape(D, LANES)
    guess = dot_tn(final_low, w_h)
    ahead = future[:, 0:LANES]
    weighting = future[:, LANES:]
    centre = future[:, 96:97]
    spread = future[:, 97:98]
    error = guess * spread + centre - ahead
    loss_sum[...] += jnp.sum(weighting * error * error, 0, keepdims=True)
    dguess = (2.0 * weighting * error / counted[0:1, 0:1] * spread).astype(BF16)
    dguess_s[cols, :] = dguess
    dfinal = dot_nt(w_h, dguess)
    norm_sums[2] += dfinal * unit_two
    norm_sums[3] += dfinal
    dresid = norm_backward(dfinal, unit_two, inverse_two, norms[2])
    dbranch = dresid.astype(BF16)
    dbranch_s[:, cols] = dbranch
    for c in range(chunks):
        rows = slice(c * D, (c + 1) * D)
        w_d = w_down[c * 4 : (c + 1) * 4].reshape(D, D)
        dpre = (dot_nn(w_d, dbranch) * slope[rows, :]).astype(BF16)
        dpre_s[rows, cols] = dpre
        dresid = dresid + dot_nn(w_up[:, :, rows].reshape(D, D), dpre)
    norm_sums[0] += dresid * unit_one
    norm_sums[1] += dresid
    dfirst = norm_backward(dresid, unit_one, inverse_one, norms[0]).astype(BF16)
    dattn[...] = dfirst
    dattn_s[:, cols] = dfirst
    dmixed[...] = dot_nn(w_out[...].reshape(D, D), dfirst).astype(BF16)

    @pl.when(step == pl.num_programs(0) - 1)
    def _():
        me = me_ref[0]

        def place(grad, first_row, blocks, base):
            height = grad.shape[0] // blocks
            for b in range(blocks):
                slot = slot_of((first_row + b) ^ me)
                for c in range(grad.shape[1] // LANES):
                    at = base + c * height
                    packed[slot, at : at + height, :] = grad[
                        b * height : (b + 1) * height, c * LANES : (c + 1) * LANES
                    ]

        for c in range(chunks):
            rows = slice(c * D, (c + 1) * D)
            place(dot_nt(active_s[rows, :], dbranch_s[...]).astype(BF16), c * 4, 4, DOWN_AT)
            place(
                dot_nt(middle_s[...], dpre_s[rows, :]).astype(BF16),
                0,
                PARTS,
                UP_AT + c * (D // LANES) * ROWS,
            )
        place(dot_nt(mixed_s[...], dattn_s[...]).astype(BF16), 0, PARTS, OUT_AT)
        head = dot_nn(final_s[...], dguess_s[...])
        lane = lane_index(head.shape)
        for i in range(4):
            head = jnp.where(lane == 96 + i, jnp.sum(norm_sums[i], 1, keepdims=True), head)
        place(head.astype(BF16), 0, PARTS, HEAD_AT)
        row = lax.broadcasted_iota(jnp.int32, (BUNDLE - LOSS_AT, LANES), 0)
        losses = jnp.where(row == 0, loss_sum[...], 0.0).astype(BF16)
        for slot in range(PARTS):
            packed[slot, LOSS_AT:BUNDLE, :] = losses
        send_packed(packed, kept, leaving, sems)


def middle_pass(me, bundle, embed, normed, future, mixed, ff):
    tokens = normed.shape[0]
    size = 256
    whole = pl.BlockSpec((4, BUNDLE, LANES), lambda t, m: (0, 0, 0), pipeline_mode=pl.Buffered(1))
    return pl.pallas_call(
        middle_kernel,
        grid_spec=pltpu.PrefetchScalarGridSpec(
            num_scalar_prefetch=1,
            grid=(tokens // size,),
            in_specs=[whole] * 4
            + [
                pl.BlockSpec((PARTS, ROWS, LANES), lambda t, m: (0, 0, 0)),
                pl.BlockSpec((size, LANES), lambda t, m: (t, 0)),
                pl.BlockSpec((size, 2 * LANES), lambda t, m: (t, 0)),
                pl.BlockSpec((D // 2, size), lambda t, m: (0, t)),
                pl.BlockSpec((D // 2, size), lambda t, m: (0, t)),
            ],
            out_specs=[
                pl.BlockSpec((D, size), lambda t, m: (0, t)),
                pl.BlockSpec((D, size), lambda t, m: (0, t)),
                pl.BlockSpec((8, LANES), lambda t, m: (0, 0)),
                pl.BlockSpec(memory_space=pl.ANY),
                pl.BlockSpec(memory_space=pl.ANY),
            ],
            scratch_shapes=[
                pltpu.VMEM((PARTS, ROWS, D), BF16),
                pltpu.VMEM((PARTS, ROWS, ff), BF16),
                pltpu.VMEM((PARTS, ff // PARTS, D), BF16),
                pltpu.VMEM((PARTS, ROWS, LANES), BF16),
                pltpu.VMEM((D, D), BF16),
                pltpu.VMEM((ff, D), BF16),
                pltpu.VMEM((D, ff), BF16),
                pltpu.VMEM((4, D, size), F32),
                pltpu.VMEM((ff, size), F32),
                pltpu.VMEM((D, tokens), BF16),
                pltpu.VMEM((D, tokens), BF16),
                pltpu.VMEM((ff, tokens), BF16),
                pltpu.VMEM((D, tokens), BF16),
                pltpu.VMEM((ff, tokens), BF16),
                pltpu.VMEM((D, tokens), BF16),
                pltpu.VMEM((D, tokens), BF16),
                pltpu.VMEM((tokens, LANES), BF16),
                pltpu.VMEM((4, D, size), F32),
                pltpu.VMEM((1, LANES), F32),
                pltpu.VMEM((PARTS, BUNDLE, LANES), BF16),
                pltpu.SemaphoreType.DMA((2,)),
            ],
        ),
        out_shape=[
            jax.ShapeDtypeStruct((D, tokens), BF16),
            jax.ShapeDtypeStruct((D, tokens), BF16),
            jax.ShapeDtypeStruct((8, LANES), F32),
            jax.ShapeDtypeStruct((PARTS // 2, BUNDLE, LANES), BF16),
            jax.ShapeDtypeStruct((PARTS // 2, BUNDLE, LANES), BF16),
        ],
        compiler_params=params(60),
        cost_estimate=cost(35e9, 20 * MIB),
        name="middle",
    )(me, *bundle, embed, normed, future, *mixed)


def last_kernel(me_ref, joint, dproj_a, dproj_b, dattn, normed, kept, leaving, total, packed, sems):
    step = pl.program_id(0)

    @pl.when(step == 0)
    def _():
        total[...] = jnp.zeros_like(total)

    dhidden = dattn[...].astype(F32)
    for part in range(3):
        rows = jnp.concatenate([dproj_a[part], dproj_b[part]], axis=0)
        weights = joint[:, :, part * D : (part + 1) * D].reshape(D, D)
        dhidden = dhidden + dot_nn(weights, rows)
    total[...] += dot_nn(dhidden.astype(BF16), normed[...])

    @pl.when(step == pl.num_programs(0) - 1)
    def _():
        me = me_ref[0]
        for b in range(PARTS):
            packed[slot_of(b ^ me)] = total[b * ROWS : (b + 1) * ROWS, :].astype(BF16)
        send_packed(packed, kept, leaving, sems)


def last_pass(me, joint, dprojs, dattn, normed):
    tokens = normed.shape[0]
    size = 256
    return pl.pallas_call(
        last_kernel,
        grid_spec=pltpu.PrefetchScalarGridSpec(
            num_scalar_prefetch=1,
            grid=(tokens // size,),
            in_specs=[
                pl.BlockSpec((PARTS, ROWS, 3 * D), lambda t, m: (0, 0, 0)),
                pl.BlockSpec((3, D // 2, size), lambda t, m: (0, 0, t)),
                pl.BlockSpec((3, D // 2, size), lambda t, m: (0, 0, t)),
                pl.BlockSpec((D, size), lambda t, m: (0, t)),
                pl.BlockSpec((size, LANES), lambda t, m: (t, 0)),
            ],
            out_specs=[pl.BlockSpec(memory_space=pl.ANY), pl.BlockSpec(memory_space=pl.ANY)],
            scratch_shapes=[
                pltpu.VMEM((D, LANES), F32),
                pltpu.VMEM((PARTS, ROWS, LANES), BF16),
                pltpu.SemaphoreType.DMA((2,)),
            ],
        ),
        out_shape=[
            jax.ShapeDtypeStruct((PARTS // 2, ROWS, LANES), BF16),
            jax.ShapeDtypeStruct((PARTS // 2, ROWS, LANES), BF16),
        ],
        compiler_params=params(),
        cost_estimate=cost(3e9, 10 * MIB),
        name="last",
    )(me, joint, *dprojs, dattn, normed)


def adamw(weight, mean, square, grad, count_step):
    mean_next = 0.9 * mean + 0.1 * grad
    square_next = 0.999 * square + 0.001 * grad * grad
    mean_hat = mean_next / (1.0 - 0.9**count_step)
    square_hat = square_next / (1.0 - 0.999**count_step)
    weight_next = weight - 0.1 * (mean_hat / (jnp.sqrt(square_hat) + 1e-08) + 0.1 * weight)
    return (weight_next, mean_next, square_next)


def step_second_kernel(mine, other, counted, *refs):
    held, results = refs[:15], refs[15:]
    grad = mine[...].astype(F32) + other[...].astype(F32)

    def update(which, at, value):
        states = [held[which * 3 + j] for j in range(3)]
        news = adamw(*[state[at] for state in states], value, float(STEP_NUMBER))
        for j in range(3):
            results[which * 3 + j][at] = news[j]

    def block(c):
        return slice(c * LANES, (c + 1) * LANES)

    for c in range(4):
        base = OUT_AT + c * ROWS
        update(0, (0, slice(None), block(c)), grad[base : base + ROWS])
    for c in range(16):
        base = UP_AT + c * ROWS
        update(1, (0, slice(None), block(c)), grad[base : base + ROWS])
    for c in range(4):
        base = DOWN_AT + c * LANES
        update(2, (0, slice(None), block(c)), grad[base : base + LANES])
    horizon = held[9].shape[-1]
    head = grad[HEAD_AT:LOSS_AT]
    update(3, (slice(None), slice(None)), head[:, 0:horizon])
    norm = head[:, 96:100]
    update(4, (slice(None), slice(None)), norm)
    results[15][...] = norm
    losses = jnp.sum(grad[LOSS_AT : LOSS_AT + 1], 1, keepdims=True)
    results[16][...] = losses / counted[0:1, 0:1]


def step_second(mine, other, counted, states):
    shapes = [jax.ShapeDtypeStruct(a.shape, F32) for a in states]
    return pl.pallas_call(
        step_second_kernel,
        out_shape=shapes
        + [jax.ShapeDtypeStruct(states[12].shape, F32), jax.ShapeDtypeStruct((1, 1), F32)],
        compiler_params=params(),
        cost_estimate=cost(0, 5 * MIB),
        name="step_second",
    )(mine, other, counted, *states)


def step_first_kernel(mine_a, other_a, mine_b, other_b, *refs):
    held, results = refs[:6], refs[6:]
    halves = [
        mine_a[...].astype(F32) + other_a[...].astype(F32),
        mine_b[...].astype(F32) + other_b[...].astype(F32),
    ]

    def update(which, at, value):
        states = [held[which * 3 + j] for j in range(3)]
        news = adamw(*[state[at] for state in states], value, float(STEP_NUMBER))
        for j in range(3):
            results[which * 3 + j][at] = news[j]

    for part in range(3):
        for side in range(2):
            for c in range(2):
                at = (part * 2 + c) * ROWS
                start = part * D + side * (D // 2) + c * LANES
                update(0, (0, slice(None), slice(start, start + LANES)), halves[side][at : at + ROWS])
    look = held[3].shape[-1]
    update(1, (slice(None), slice(None)), halves[1][6 * ROWS : 7 * ROWS, 0:look])


def step_first(pair_a, pair_b, states):
    shapes = [jax.ShapeDtypeStruct(a.shape, F32) for a in states]
    return pl.pallas_call(
        step_first_kernel,
        out_shape=shapes,
        compiler_params=params(),
        cost_estimate=cost(0, 2 * MIB),
        name="step_first",
    )(*pair_a, *pair_b, *states)


def whole_windows_body(
    series,
    target,
    valid_slots,
    observed,
    embed_weight,
    joint_proj,
    out_proj,
    up_proj,
    down_proj,
    head_weight,
    norm_params,
    embed_mean,
    joint_mean,
    out_mean,
    up_mean,
    down_mean,
    head_mean,
    norm_mean,
    embed_square,
    joint_square,
    out_square,
    up_square,
    down_square,
    head_square,
    norm_square,
):
    me = lax.axis_index("var").astype(jnp.int32).reshape(1)
    pos = lax.axis_index("win").astype(jnp.int32).reshape(1)
    ff = up_proj.shape[-1]
    first = gathered(pack_first(joint_proj, embed_weight.T))
    valid = valid_slots.reshape(-1, 1)
    kept_n, sent_n, kept_t, sent_t, own = prep(pos, series, target, observed, valid)
    came_n = swapped(sent_n, "win", 1)
    came_t = swapped(sent_t, "win", 1)
    half, local, _ = kept_n.shape
    tokens = half * 2 * local
    second = gathered(
        pack_second(
            own,
            came_t[half - 1, 0:1, 98:99],
            out_proj,
            up_proj,
            down_proj,
            head_weight,
            norm_params[0].T,
        )
    )
    normed = jnp.concatenate([kept_n, came_n], axis=1).reshape(tokens, LANES)
    future = jnp.concatenate([kept_t, came_t], axis=1).reshape(tokens, 2 * LANES)
    qkv, hid, joint, embed = project(me, first, kept_n, came_n)
    count = HEADS // 2
    sides = [attend(side * count, count, kept_n, came_n, qkv) for side in range(2)]
    dmixed, dattn, counted, kept, leaving = middle_pass(
        me, second, embed, normed, future, [side[1] for side in sides], ff
    )
    second_pair = scattered(kept, leaving)
    grads = [
        unattend(me, side * count, count, sides[side][0], sides[side][2], sides[side][1], dmixed, qkv, hid)
        for side in range(2)
    ]
    pair_a = scattered(grads[0][1], grads[0][2])
    last = last_pass(me, joint, [g[0] for g in grads], dattn, normed)
    pair_b = scattered(
        *[jnp.concatenate([grads[1][1 + i], last[i]], axis=1) for i in range(2)]
    )
    states = []
    for group in (
        (out_proj, out_mean, out_square),
        (up_proj, up_mean, up_square),
        (down_proj, down_mean, down_square),
        (head_weight, head_mean, head_square),
        (norm_params[0].T, norm_mean[0].T, norm_square[0].T),
    ):
        states.extend(group)
    new = step_second(*second_pair, counted, states)
    fresh = step_first(
        pair_a,
        pair_b,
        [joint_proj, joint_mean, joint_square, embed_weight.T, embed_mean.T, embed_square.T],
    )
    outs, ups, downs, heads, norms = [new[3 * i : 3 * i + 3] for i in range(5)]
    norms = [n.T[None] for n in norms]
    embeds = [e.T for e in fresh[3:6]]
    return (
        new[16].reshape(1),
        embeds[0],
        fresh[0],
        outs[0],
        ups[0],
        downs[0],
        heads[0],
        new[15].T[None],
        embeds[1],
        fresh[1],
        outs[1],
        ups[1],
        downs[1],
        heads[1],
        norms[1],
        embeds[2],
        fresh[2],
        outs[2],
        ups[2],
        downs[2],
        heads[2],
        norms[2],
    )


def passed_along(block, axis, distance):
    devices = range(lax.axis_size(axis))
    route = [((i - distance) % len(devices), i) for i in devices]
    return lax.ppermute(block, axis, route)


def layer_norm(resid, gain, shift):
    centre = jnp.mean(resid, -1, keepdims=True)
    offset = resid - centre
    spread = jnp.mean(offset * offset, -1, keepdims=True)
    return offset * lax.rsqrt(spread + 1e-05) * gain + shift


def to_items(matrix, windows, local, parts):
    shaped = matrix.reshape(windows, local, parts, HEADS, HEAD_SIZE).transpose(0, 3, 1, 2, 4)
    return shaped.reshape(windows * HEADS, local, parts * HEAD_SIZE)


def from_items(items, windows, local, parts):
    shaped = items.reshape(windows, HEADS, local, parts, HEAD_SIZE).transpose(0, 2, 3, 1, 4)
    return shaped.reshape(windows * local, parts * HEADS * HEAD_SIZE)


def masked_scores(query_rows, key_portion, markers, query_pos, key_pos):
    score_matrix = (
        jnp.einsum("acn,azn->acz", query_rows, key_portion, preferred_element_type=jnp.float32)
        * 0.125
    )
    allowed = (markers[None, :] > 0.5) | (query_pos[:, None] == key_pos[None, :])
    return jnp.where(allowed[None], score_matrix, -1e30)


def absorb(state, query_rows, paired_keys, markers, query_pos, key_pos):
    peak, totals, accum = state
    score_matrix = masked_scores(
        query_rows, paired_keys[..., :HEAD_SIZE], markers, query_pos, key_pos
    )
    top_new = jnp.maximum(peak, jnp.max(score_matrix, -1))
    rescale = jnp.exp(peak - top_new)
    weights = jnp.exp(score_matrix - top_new[..., None])
    totals = totals * rescale + jnp.sum(weights, -1)
    reduced_weights = weights.astype(jnp.bfloat16)
    accum = accum * rescale[..., None] + jnp.einsum(
        "zsx,zxj->zsj",
        reduced_weights,
        paired_keys[..., HEAD_SIZE:],
        preferred_element_type=jnp.float32,
    )
    return (top_new, totals, accum)


def release(
    dquery, query_rows, paired_keys, markers, query_pos, key_pos, log_total, mixed_gradient, deltas
):
    key_portion = paired_keys[..., :HEAD_SIZE]
    value_rows = paired_keys[..., HEAD_SIZE:]
    score_matrix = masked_scores(query_rows, key_portion, markers, query_pos, key_pos)
    weights = jnp.exp(score_matrix - log_total[..., None])
    weight_gradient = jnp.einsum(
        "acn,azn->acz", mixed_gradient, value_rows, preferred_element_type=jnp.float32
    )
    score_gradient = (weights * (weight_gradient - deltas[..., None])).astype(jnp.bfloat16)
    reduced_weights = weights.astype(jnp.bfloat16)
    dquery = (
        dquery
        + jnp.einsum(
            "zsx,zxj->zsj", score_gradient, key_portion, preferred_element_type=jnp.float32
        )
        * 0.125
    )
    key_gradient = (
        jnp.einsum("fov,foc->fvc", score_gradient, query_rows, preferred_element_type=jnp.float32)
        * 0.125
    )
    value_gradient = jnp.einsum(
        "fov,foc->fvc", reduced_weights, mixed_gradient, preferred_element_type=jnp.float32
    )
    return (dquery, key_gradient, value_gradient)


def empty_state(blocks, length):
    return (
        jnp.full((blocks, length), -1e30, jnp.float32),
        jnp.zeros((blocks, length), jnp.float32),
        jnp.zeros((blocks, length, HEAD_SIZE), jnp.float32),
    )


def attend_forward(items, markers, position, group, local):
    blocks = items.shape[0]
    query_rows = items[..., :HEAD_SIZE]
    paired_keys = items[..., HEAD_SIZE:]
    query_pos = position * local + jnp.arange(local, dtype=jnp.int32)
    state = absorb(
        empty_state(blocks, local), query_rows, paired_keys, markers, query_pos, query_pos
    )

    def turn(counter, carry):
        moving, moving_marks, state = carry
        moving, moving_marks = passed_along((moving, moving_marks), "win", 1)
        key_pos = (position - counter) % group * local + jnp.arange(local, dtype=jnp.int32)
        return (
            moving,
            moving_marks,
            absorb(state, query_rows, moving, moving_marks, query_pos, key_pos),
        )

    _, _, state = lax.fori_loop(1, group, turn, (paired_keys, markers, state))
    peak, totals, accum = state
    mixed_full = accum / totals[..., None]
    return (mixed_full.astype(jnp.bfloat16), (mixed_full, peak + jnp.log(totals)))


def attend_backward(items, markers, mixed_gradient, kept, position, group, local):
    blocks = items.shape[0]
    mixed_full, log_total = kept
    query_rows = items[..., :HEAD_SIZE]
    deltas = jnp.sum(mixed_gradient.astype(jnp.float32) * mixed_full, -1)
    query_pos = position * local + jnp.arange(local, dtype=jnp.int32)

    def turn(counter, carry):
        moving, moving_marks, dquery, dpairs = carry
        key_pos = (position - counter) % group * local + jnp.arange(local, dtype=jnp.int32)
        dquery, key_gradient, value_gradient = release(
            dquery,
            query_rows,
            moving,
            moving_marks,
            query_pos,
            key_pos,
            log_total,
            mixed_gradient,
            deltas,
        )
        dpairs = passed_along(
            (dpairs + jnp.concatenate([key_gradient, value_gradient], -1)).astype(jnp.bfloat16),
            "win",
            1,
        ).astype(jnp.float32)
        moving, moving_marks = passed_along((moving, moving_marks), "win", 1)
        return (moving, moving_marks, dquery, dpairs)

    start = (
        items[..., HEAD_SIZE:],
        markers,
        jnp.zeros((blocks, local, HEAD_SIZE), jnp.float32),
        jnp.zeros((blocks, local, 2 * HEAD_SIZE), jnp.float32),
    )
    _, _, dquery, dpairs = lax.fori_loop(0, group, turn, start)
    return jnp.concatenate([dquery, dpairs], -1).astype(jnp.bfloat16)


def layer_forward(hidden, layer_weights, markers, position, group, windows, local):
    joint, out_mat, up_mat, down_mat, norms = layer_weights
    hidden_low = hidden.astype(jnp.bfloat16)
    items = to_items(
        jnp.dot(hidden_low, joint, preferred_element_type=jnp.float32).astype(jnp.bfloat16),
        windows,
        local,
        3,
    )
    mixed_items, kept_attn = attend_forward(items, markers, position, group, local)
    mixed_low = from_items(mixed_items, windows, local, 1)
    resid_one = hidden + jnp.dot(mixed_low, out_mat, preferred_element_type=jnp.float32)
    middle = layer_norm(resid_one, norms[0], norms[1])
    middle_low = middle.astype(jnp.bfloat16)
    pre_gelu = jnp.dot(middle_low, up_mat, preferred_element_type=jnp.float32)
    activated = jax.nn.gelu(pre_gelu, approximate=False).astype(jnp.bfloat16)
    resid_two = middle + jnp.dot(activated, down_mat, preferred_element_type=jnp.float32)
    result = layer_norm(resid_two, norms[2], norms[3])
    return (
        result,
        (
            hidden_low,
            items,
            kept_attn,
            mixed_low,
            resid_one,
            middle_low,
            pre_gelu,
            activated,
            resid_two,
        ),
    )


def layer_backward(dresult, layer_weights, kept, markers, position, group, windows, local):
    joint, out_mat, up_mat, down_mat, norms = layer_weights
    (
        hidden_low,
        items,
        kept_attn,
        mixed_low,
        resid_one,
        middle_low,
        pre_gelu,
        activated,
        resid_two,
    ) = kept
    _, pull_two = jax.vjp(layer_norm, resid_two, norms[2], norms[3])
    dresid_two, dgain_two, dshift_two = pull_two(dresult)
    dbranch = dresid_two.astype(jnp.bfloat16)
    grad_down = jnp.dot(activated.T, dbranch, preferred_element_type=jnp.float32)
    dactive = jnp.dot(dbranch, down_mat.T, preferred_element_type=jnp.float32)
    _, pull_gelu = jax.vjp(partial(jax.nn.gelu, approximate=False), pre_gelu)
    dpre = pull_gelu(dactive)[0].astype(jnp.bfloat16)
    grad_up = jnp.dot(middle_low.T, dpre, preferred_element_type=jnp.float32)
    dmiddle = dresid_two + jnp.dot(dpre, up_mat.T, preferred_element_type=jnp.float32)
    _, pull_one = jax.vjp(layer_norm, resid_one, norms[0], norms[1])
    dresid_one, dgain_one, dshift_one = pull_one(dmiddle)
    dattn = dresid_one.astype(jnp.bfloat16)
    grad_out = jnp.dot(mixed_low.T, dattn, preferred_element_type=jnp.float32)
    mixed_gradient = jnp.dot(dattn, out_mat.T, preferred_element_type=jnp.float32).astype(
        jnp.bfloat16
    )
    ditems = attend_backward(
        items,
        markers,
        to_items(mixed_gradient, windows, local, 1),
        kept_attn,
        position,
        group,
        local,
    )
    dproj = from_items(ditems, windows, local, 3)
    grad_joint = jnp.dot(hidden_low.T, dproj, preferred_element_type=jnp.float32)
    dhidden = dresid_one + jnp.dot(dproj, joint.T, preferred_element_type=jnp.float32)
    grad_norm = jnp.stack([dgain_one, dshift_one, dgain_two, dshift_two])
    return (dhidden, (grad_joint, grad_out, grad_up, grad_down, grad_norm))


def sliced_windows_body(
    series,
    target,
    valid_slots,
    observed,
    embed_weight,
    joint_proj,
    out_proj,
    up_proj,
    down_proj,
    head_weight,
    norm_params,
    embed_mean,
    joint_mean,
    out_mean,
    up_mean,
    down_mean,
    head_mean,
    norm_mean,
    embed_square,
    joint_square,
    out_square,
    up_square,
    down_square,
    head_square,
    norm_square,
):
    windows = series.shape[0]
    local = series.shape[1]
    row_count = windows * local
    group = lax.axis_size("win")
    position = lax.axis_index("win")
    embed, joint, out_mat, up_mat, down_mat, head_mat, norms_low = (
        lax.all_gather(embed_weight.astype(jnp.bfloat16), "var", axis=1, tiled=True),
        lax.all_gather(joint_proj.astype(jnp.bfloat16), "var", axis=1, tiled=True),
        lax.all_gather(out_proj.astype(jnp.bfloat16), "var", axis=1, tiled=True),
        lax.all_gather(up_proj.astype(jnp.bfloat16), "var", axis=1, tiled=True),
        lax.all_gather(down_proj.astype(jnp.bfloat16), "var", axis=1, tiled=True),
        lax.all_gather(head_weight.astype(jnp.bfloat16), "var", axis=0, tiled=True),
        lax.all_gather(norm_params.astype(jnp.bfloat16), "var", axis=2, tiled=True),
    )
    norms = norms_low.astype(jnp.float32)
    weight_mask = observed.astype(jnp.float32) * valid_slots.astype(jnp.float32)[None, :, None]
    count = jnp.maximum(lax.psum(jnp.sum(weight_mask), ("var", "win")), 1.0)
    markers = valid_slots.astype(jnp.bfloat16)
    centre = jnp.mean(series, -1, keepdims=True)
    offset = series - centre
    spread = jnp.sqrt(jnp.mean(offset * offset, -1, keepdims=True) + 1e-05)
    normed = (offset / spread).astype(jnp.bfloat16).reshape(row_count, -1)
    hidden = jnp.dot(normed, embed, preferred_element_type=jnp.float32)
    layer = 0
    layer_weights = (joint[layer], out_mat[layer], up_mat[layer], down_mat[layer], norms[layer])
    hidden, kept = layer_forward(hidden, layer_weights, markers, position, group, windows, local)
    kept_layers = [kept]
    final_low = hidden.astype(jnp.bfloat16)
    guess = (
        jnp.dot(final_low, head_mat, preferred_element_type=jnp.float32).reshape(windows, local, -1)
        * spread
        + centre
    )
    error = guess - target
    loss_part = jnp.sum(weight_mask * error * error)
    dguess = (
        (2.0 * weight_mask * error / count * spread).reshape(row_count, -1).astype(jnp.bfloat16)
    )
    grad_head = jnp.dot(final_low.T, dguess, preferred_element_type=jnp.float32)
    dhidden = jnp.dot(dguess, head_mat.T, preferred_element_type=jnp.float32)
    layer_grads = [None] * LAYERS
    for layer in reversed(range(LAYERS)):
        layer_weights = (joint[layer], out_mat[layer], up_mat[layer], down_mat[layer], norms[layer])
        dhidden, layer_grads[layer] = layer_backward(
            dhidden, layer_weights, kept_layers[layer], markers, position, group, windows, local
        )
    grad_embed = jnp.dot(normed.T, dhidden.astype(jnp.bfloat16), preferred_element_type=jnp.float32)
    stacked = [jnp.stack([grads[i] for grads in layer_grads]) for i in range(5)]
    summed = (
        lax.psum_scatter(
            grad_embed.astype(jnp.bfloat16), "var", scatter_dimension=1, tiled=True
        ).astype(jnp.float32),
        lax.psum_scatter(
            stacked[0].astype(jnp.bfloat16), "var", scatter_dimension=1, tiled=True
        ).astype(jnp.float32),
        lax.psum_scatter(
            stacked[1].astype(jnp.bfloat16), "var", scatter_dimension=1, tiled=True
        ).astype(jnp.float32),
        lax.psum_scatter(
            stacked[2].astype(jnp.bfloat16), "var", scatter_dimension=1, tiled=True
        ).astype(jnp.float32),
        lax.psum_scatter(
            stacked[3].astype(jnp.bfloat16), "var", scatter_dimension=1, tiled=True
        ).astype(jnp.float32),
        lax.psum_scatter(
            grad_head.astype(jnp.bfloat16), "var", scatter_dimension=0, tiled=True
        ).astype(jnp.float32),
        lax.psum_scatter(
            stacked[4].astype(jnp.bfloat16), "var", scatter_dimension=2, tiled=True
        ).astype(jnp.float32),
    )
    totals = (
        lax.psum(summed[0].astype(jnp.bfloat16), "win").astype(jnp.float32),
        lax.psum(summed[1].astype(jnp.bfloat16), "win").astype(jnp.float32),
        lax.psum(summed[2].astype(jnp.bfloat16), "win").astype(jnp.float32),
        lax.psum(summed[3].astype(jnp.bfloat16), "win").astype(jnp.float32),
        lax.psum(summed[4].astype(jnp.bfloat16), "win").astype(jnp.float32),
        lax.psum(summed[5].astype(jnp.bfloat16), "win").astype(jnp.float32),
        lax.psum(summed[6].astype(jnp.bfloat16), "win").astype(jnp.float32),
    )
    loss = lax.psum(loss_part, ("var", "win")) / count
    count_step = float(STEP_NUMBER)
    weights = (embed_weight, joint_proj, out_proj, up_proj, down_proj, head_weight, norm_params)
    means = (embed_mean, joint_mean, out_mean, up_mean, down_mean, head_mean, norm_mean)
    squares = (
        embed_square,
        joint_square,
        out_square,
        up_square,
        down_square,
        head_square,
        norm_square,
    )
    results = [adamw(weights[i], means[i], squares[i], totals[i], count_step) for i in range(7)]
    return (
        loss.reshape(1),
        results[0][0],
        results[1][0],
        results[2][0],
        results[3][0],
        results[4][0],
        results[5][0],
        totals[6],
        results[0][1],
        results[1][1],
        results[2][1],
        results[3][1],
        results[4][1],
        results[5][1],
        results[6][1],
        results[0][2],
        results[1][2],
        results[2][2],
        results[3][2],
        results[4][2],
        results[5][2],
        results[6][2],
    )


def solution(mesh):
    swaps = mesh.shape["var"] == PARTS and mesh.shape["win"] == 2
    body = whole_windows_body if swaps else sliced_windows_body
    placed = (
        P("var", "win", None),
        P("var", "win", None),
        P("win"),
        P("var", "win", None),
        P(None, "var"),
        P(None, "var", None),
        P(None, "var", None),
        P(None, "var", None),
        P(None, "var", None),
        P("var", None),
        P(None, None, "var"),
        P(None, "var"),
        P(None, "var", None),
        P(None, "var", None),
        P(None, "var", None),
        P(None, "var", None),
        P("var", None),
        P(None, None, "var"),
        P(None, "var"),
        P(None, "var", None),
        P(None, "var", None),
        P(None, "var", None),
        P(None, "var", None),
        P("var", None),
        P(None, None, "var"),
    )
    return jax.shard_map(
        body,
        mesh=mesh,
        in_specs=placed,
        out_specs=(
            P(),
            P(None, "var"),
            P(None, "var", None),
            P(None, "var", None),
            P(None, "var", None),
            P(None, "var", None),
            P("var", None),
            P(None, None, "var"),
            P(None, "var"),
            P(None, "var", None),
            P(None, "var", None),
            P(None, "var", None),
            P(None, "var", None),
            P("var", None),
            P(None, None, "var"),
            P(None, "var"),
            P(None, "var", None),
            P(None, "var", None),
            P(None, "var", None),
            P(None, "var", None),
            P("var", None),
            P(None, None, "var"),
        ),
        check_vma=False,
    )
```

```python
from functools import partial

import jax
import jax.numpy as jnp
from jax import lax
from jax.experimental import pallas as pl
from jax.experimental.pallas import tpu as pltpu
from jax.sharding import PartitionSpec as P

HEADS = 8
HEAD_SIZE = 64
LAYERS = 1
STEP_NUMBER = 10

F32 = jnp.float32
BF16 = jnp.bfloat16
LANES = 128
D = HEADS * HEAD_SIZE
PARTS = 16
ROWS = D // PARTS
MIB = 1 << 20

OUT_AT, UP_AT, DOWN_AT, HEAD_AT, LOSS_AT, BUNDLE = 0, 128, 640, 1152, 1184, 1200
CUT = 896
EMBED_AT, FIRST = 384, 416


def dot_nn(a, b):
    return lax.dot_general(a, b, (((1,), (0,)), ((), ())), preferred_element_type=F32)


def dot_nt(a, b):
    return lax.dot_general(a, b, (((1,), (1,)), ((), ())), preferred_element_type=F32)


def dot_tn(a, b):
    return lax.dot_general(a, b, (((0,), (0,)), ((), ())), preferred_element_type=F32)


def offset_of(slot):
    return (slot % 4) * 4 + (slot // 4 % 2) * 2 + slot // 8


def slot_of(offset):
    return (offset & 1) * 8 + ((offset >> 1) & 1) * 4 + (offset >> 2)


def lane_index(shape):
    return lax.broadcasted_iota(jnp.int32, shape, len(shape) - 1)


IN_HBM = pl.BlockSpec(memory_space=pltpu.HBM)
ANYWHERE = pl.BlockSpec(memory_space=pl.ANY)


def ignoring(kernel, reads, ignored):
    def run(*refs):
        kernel(*refs[:reads], *refs[reads + ignored :])

    return run


def params(limit=63, **more):
    return pltpu.CompilerParams(vmem_limit_bytes=limit * MIB, **more)


def cost(flops, moved):
    return pl.CostEstimate(flops=int(flops), bytes_accessed=int(moved), transcendentals=0)


def swapped(block, axis, distance):
    count = lax.axis_size(axis)
    return lax.ppermute(block, axis, [(i, i ^ distance) for i in range(count)])


def sent_along_z(blocks):
    return [swapped(block, "var", 4 * i) for i, block in zip((1, 2, 3), blocks)]


def stacked_kernel(counts, *refs):
    ins, outs, sems = sum(counts), len(counts), refs[-1]
    blocks, results = refs[:ins], refs[ins : ins + outs]
    copies, at = [], 0
    for count, result in zip(counts, results):
        row = 0
        for block in blocks[at : at + count]:
            if len(block.shape) == 2:
                target, height = result.at[row], 1
            else:
                height = block.shape[0]
                target = result.at[pl.ds(row, height)]
            copies.append(pltpu.make_async_copy(block, target, sems.at[len(copies)]))
            row += height
        at += count
    for copy in copies:
        copy.start()
    for copy in copies:
        copy.wait()


def stacked(groups, after=()):
    counts = tuple(len(group) for group in groups)
    blocks = [block for group in groups for block in group]
    shapes = []
    for group in groups:
        rows = sum(1 if block.ndim == 2 else block.shape[0] for block in group)
        shapes.append(jax.ShapeDtypeStruct((rows, *group[0].shape[-2:]), BF16))
    vmem = pl.BlockSpec(memory_space=pltpu.VMEM)
    return pl.pallas_call(
        ignoring(partial(stacked_kernel, counts), len(blocks), len(after)),
        in_specs=[ANYWHERE] * (len(blocks) + len(after)),
        out_specs=[vmem] * len(shapes),
        out_shape=shapes,
        scratch_shapes=[pltpu.SemaphoreType.DMA((len(blocks),))],
        compiler_params=params(6),
        cost_estimate=cost(0, MIB),
        name="stacked",
    )(*blocks, *after)


def summed_kernel(groups, *refs):
    at, to = 0, sum(terms for terms, _ in groups)
    for terms, outs in groups:
        total = refs[at][...].astype(F32)
        for ref in refs[at + 1 : at + terms]:
            total = total + ref[...].astype(F32)
        total = total.astype(BF16)
        for i, ref in enumerate(refs[to : to + outs]):
            height = total.shape[0] // outs
            ref[...] = total[i * height : (i + 1) * height].reshape(ref.shape)
        at, to = at + terms, to + outs


def summed(groups, after=()):
    counts = tuple((len(terms), parts) for terms, parts in groups)
    arrays = [term for terms, _ in groups for term in terms]
    shapes = []
    for terms, parts in groups:
        first, *rest = terms[0].shape
        shape = tuple(rest) if parts == 4 else (first // parts, *rest)
        shapes += [jax.ShapeDtypeStruct(shape, BF16)] * parts
    moved = sum(array.size for array in arrays) * 3
    vmem = pl.BlockSpec(memory_space=pltpu.VMEM)
    return pl.pallas_call(
        ignoring(partial(summed_kernel, counts), len(arrays), len(after)),
        in_specs=[vmem] * len(arrays) + [ANYWHERE] * len(after),
        out_specs=[vmem] * len(shapes),
        out_shape=shapes,
        compiler_params=params(12),
        cost_estimate=cost(0, moved),
        name="summed",
    )(*arrays, *after)


def core_terms(kept, leaving):
    return ([kept, swapped(leaving, "var", 1)], 2)


def y_terms(near, far):
    return ([near, swapped(far, "var", 2)], 4)


def z_terms(mine, *others):
    return ([mine, *sent_along_z(others)], 1)


def with_other(mine):
    return (mine, swapped(mine, "win", 1))


def three_pieces(value):
    high = value.astype(BF16).astype(F32)
    middle = (value - high).astype(BF16).astype(F32)
    return (high, middle, value - high - middle)


def prep_kernel(
    pos_ref, series, target, observed, valid, kept_n, sent_n, kept_t, sent_t, count, total
):
    step = pl.program_id(0)
    half = pl.num_programs(0) // 2
    rows = series[0]
    look, local = rows.shape
    centre = jnp.mean(rows, 0, keepdims=True)
    offset = rows - centre
    spread = jnp.sqrt(jnp.mean(offset * offset, 0, keepdims=True) + 1e-05)
    normed = offset / spread
    mark = valid[...].astype(F32)
    weight = observed[0].astype(F32) * mark

    @pl.when(step == 0)
    def _():
        total[...] = jnp.zeros_like(total)

    total[...] += jnp.sum(jnp.sum(weight, 0, keepdims=True), 1, keepdims=True)
    spare = LANES - look
    row = lax.broadcasted_iota(jnp.int32, (spare, local), 0)
    extra = jnp.where(row == 0, mark, 0.0)
    for i, piece in enumerate(three_pieces(total[0:1, 0:1])):
        extra = jnp.where(row == 1 + i, piece, extra)
    normed = jnp.concatenate([normed, extra], axis=0).T.astype(BF16)
    extra = jnp.where(row == 0, centre, jnp.where(row == 1, spread, 0.0))
    future = jnp.concatenate([target[0], extra], axis=0).T
    weight = jnp.concatenate([weight, jnp.zeros((spare, local), F32)], axis=0).T

    @pl.when(step < half)
    def _():
        kept_n[0] = normed
        kept_t[0, :, 0:LANES] = future
        kept_t[0, :, LANES:] = weight

    @pl.when(step >= half)
    def _():
        sent_n[0] = normed
        sent_t[0, :, 0:LANES] = future
        sent_t[0, :, LANES:] = weight

    count[...] = total[...]


def prep(pos, series, target, observed, valid, after):
    windows, look, local = series.shape
    half = windows // 2

    def source(i, pos_ref):
        return (lax.rem(pos_ref[0] * half + i, windows), 0, 0)

    def kept(i, pos_ref):
        return (jnp.minimum(i, half - 1), 0, 0)

    def sent(i, pos_ref):
        return (jnp.maximum(i - half, 0), 0, 0)

    block = pl.BlockSpec((1, look, local), source)
    out_shape, out_specs = [], []
    for dtype, width in ((BF16, LANES), (F32, 2 * LANES)):
        for index in (kept, sent):
            out_shape.append(jax.ShapeDtypeStruct((half, local, width), dtype))
            out_specs.append(pl.BlockSpec((1, local, width), index))
    return pl.pallas_call(
        ignoring(prep_kernel, 5, len(after)),
        grid_spec=pltpu.PrefetchScalarGridSpec(
            num_scalar_prefetch=1,
            grid=(windows,),
            in_specs=[block, block, block, pl.BlockSpec((1, local), lambda i, p: (0, 0))]
            + [ANYWHERE] * len(after),
            out_specs=out_specs + [pl.BlockSpec((8, LANES), lambda i, p: (0, 0))],
            scratch_shapes=[pltpu.VMEM((8, LANES), F32)],
        ),
        out_shape=out_shape + [jax.ShapeDtypeStruct((8, LANES), F32)],
        compiler_params=params(8),
        cost_estimate=cost(0, 8 * MIB),
        name="prep",
    )(pos, series, target, observed, valid, *after)


def pack_first_kernel(joint, embed, out):
    for c in range(12):
        out[c * ROWS : (c + 1) * ROWS, :] = joint[0, :, c * LANES : (c + 1) * LANES].astype(BF16)
    look = embed.shape[-1]
    out[EMBED_AT:FIRST, 0:look] = embed[...].astype(BF16)
    out[EMBED_AT:FIRST, look:] = jnp.zeros((ROWS, LANES - look), BF16)


def pack_first(joint, embed):
    return pl.pallas_call(
        pack_first_kernel,
        out_shape=jax.ShapeDtypeStruct((FIRST, LANES), BF16),
        compiler_params=params(4),
        cost_estimate=cost(0, MIB // 2),
        name="pack_first",
    )(joint, embed)


def pack_second_kernel(own, came, out_w, up, down, head, norm, one, two):
    for c in range(4):
        one[OUT_AT + c * ROWS : OUT_AT + (c + 1) * ROWS, :] = out_w[
            0, :, c * LANES : (c + 1) * LANES
        ].astype(BF16)
    for c in range(16):
        one[UP_AT + c * ROWS : UP_AT + (c + 1) * ROWS, :] = up[
            0, :, c * LANES : (c + 1) * LANES
        ].astype(BF16)
    for c in range(4):
        two[c * LANES : (c + 1) * LANES, :] = down[0, :, c * LANES : (c + 1) * LANES].astype(BF16)
    horizon = head.shape[-1]
    spare = (ROWS, LANES - horizon)
    lane = lane_index(spare)
    count = own[0:1, 0:1] + jnp.sum(came[0, 0:1, 97:100].astype(F32), 1, keepdims=True)
    square = jnp.concatenate([norm[0], jnp.zeros((LANES - 4, ROWS), F32)], axis=0)
    square = jnp.concatenate([square] * (LANES // ROWS), axis=1).T
    extra = square[0:ROWS, 0 : LANES - horizon]
    for i, piece in enumerate(three_pieces(count)):
        extra = jnp.where(lane == 4 + i, piece, extra)
    two[HEAD_AT - DOWN_AT : LOSS_AT - DOWN_AT, 0:horizon] = head[...].astype(BF16)
    two[HEAD_AT - DOWN_AT : LOSS_AT - DOWN_AT, horizon:] = extra.astype(BF16)
    two[LOSS_AT - DOWN_AT :, :] = jnp.zeros((BUNDLE - LOSS_AT, LANES), BF16)


def pack_second(own, came, out_w, up, down, head, norm, after):
    half = came.shape[0]
    arrays = (own, came, out_w, up, down, head, norm)
    specs = [pl.BlockSpec(a.shape, lambda i, n=a.ndim: (0,) * n) for a in arrays]
    specs[1] = pl.BlockSpec((1, 16, LANES), lambda i: (half - 1, 0, 0))
    shapes = [(DOWN_AT, LANES), (BUNDLE - DOWN_AT, LANES)]
    return pl.pallas_call(
        ignoring(pack_second_kernel, len(arrays), len(after)),
        grid=(1,),
        in_specs=specs + [ANYWHERE] * len(after),
        out_specs=[pl.BlockSpec(shape, lambda i: (0, 0)) for shape in shapes],
        out_shape=[jax.ShapeDtypeStruct(shape, BF16) for shape in shapes],
        compiler_params=params(8),
        cost_estimate=cost(0, 2 * MIB),
        name="pack_second",
    )(*arrays, *after)


def project_kernel(me_ref, g0, g1, kept, came, qkv, hid, joint, embed):
    @pl.when(pl.program_id(0) == 0)
    def _():
        me = me_ref[0]
        for slot in range(PARTS):
            block = (g0, g1)[slot // 8]
            owner = me ^ offset_of(slot)
            for c in range(12):
                joint[owner, :, c * LANES : (c + 1) * LANES] = block[
                    slot % 8, c * ROWS : (c + 1) * ROWS, :
                ]
            embed[owner] = block[slot % 8, EMBED_AT:FIRST, :]

    normed = jnp.concatenate([kept[0], came[0]], axis=0)
    low = dot_nt(embed[...].reshape(D, LANES), normed).astype(BF16)
    hid[...] = low
    for part in range(3):
        weights = joint[:, :, part * D : (part + 1) * D].reshape(D, D)
        rows = dot_tn(weights, low)
        if part == 0:
            rows = rows * 0.18033688011112042
        qkv[part * D : (part + 1) * D, :] = rows.astype(BF16)


def project(me, bundle, kept, came):
    half, local, _ = kept.shape
    slots = 2 * local
    whole = pl.BlockSpec((8, FIRST, LANES), lambda w, m: (0, 0, 0))
    mine = pl.BlockSpec((1, local, LANES), lambda w, m: (w, 0, 0))
    return pl.pallas_call(
        project_kernel,
        grid_spec=pltpu.PrefetchScalarGridSpec(
            num_scalar_prefetch=1,
            grid=(half,),
            in_specs=[whole] * 2 + [mine] * 2,
            out_specs=[
                pl.BlockSpec((3 * D, slots), lambda w, m: (0, w)),
                pl.BlockSpec((D, slots), lambda w, m: (0, w)),
                pl.BlockSpec((PARTS, ROWS, 3 * D), lambda w, m: (0, 0, 0)),
                pl.BlockSpec((PARTS, ROWS, LANES), lambda w, m: (0, 0, 0)),
            ],
        ),
        out_shape=[
            jax.ShapeDtypeStruct((3 * D, half * slots), BF16),
            jax.ShapeDtypeStruct((D, half * slots), BF16),
            jax.ShapeDtypeStruct((PARTS, ROWS, 3 * D), BF16),
            jax.ShapeDtypeStruct((PARTS, ROWS, LANES), BF16),
        ],
        compiler_params=params(18),
        cost_estimate=cost(3e9, 12 * MIB),
        name="project",
    )(me, *bundle, kept, came)


def tiles_of(length, size):
    return [(at, min(size, length - at)) for at in range(0, length, size)]


PAIR = 2


def head_rows(i):
    return slice(i * HEAD_SIZE, (i + 1) * HEAD_SIZE)


def attend_kernel(kept, came, q, k, v, weights, mixed, scale, bias):
    slots = q.shape[1]
    local = slots // 2

    @pl.when((pl.program_id(0) == 0) & (pl.program_id(1) == 0))
    def _():
        for part, marks in enumerate((kept, came)):
            rows = slice(part * local, (part + 1) * local)
            mark = marks[0, :, 96:97].astype(F32)
            key = part * local + lax.broadcasted_iota(jnp.int32, (local, slots), 0)
            query = lane_index((local, slots))
            bias[rows, :] = jnp.where((mark > 0.5) | (key == query), 0.0, -1e30)

    def score_of(i):
        return dot_tn(k[head_rows(i), :], q[head_rows(i), :]) + bias[...]

    def weigh(i, score):
        weight = jnp.exp2(score - jnp.max(score, 0, keepdims=True))
        low = weight.astype(BF16)
        weights[i] = low
        return (low, jnp.sum(weight, 0, keepdims=True))

    def mix(i, low, total):
        inverse = 1.0 / total
        scale[i] = inverse
        mixed[head_rows(i), :] = (dot_nn(v[head_rows(i), :], low) * inverse).astype(BF16)

    score = score_of(0)
    pending = None
    for i in range(PAIR):
        coming = score_of(i + 1) if i + 1 < PAIR else None
        weighed = weigh(i, score)
        if pending is not None:
            mix(*pending)
        pending = (i, *weighed)
        score = coming
    mix(*pending)


def attend(first, count, kept, came, qkv, after=()):
    half, local, _ = kept.shape
    slots = 2 * local
    marks = pl.BlockSpec((1, local, LANES), lambda h, w: (0, 0, 0))

    def heads(part):
        return pl.BlockSpec(
            (PAIR * HEAD_SIZE, slots), lambda h, w: ((part * HEADS + first) // PAIR + h, w)
        )

    return pl.pallas_call(
        ignoring(attend_kernel, 5, len(after)),
        grid=(count // PAIR, half),
        in_specs=[marks, marks, heads(0), heads(1), heads(2)] + [ANYWHERE] * len(after),
        out_specs=[
            pl.BlockSpec((PAIR, slots, slots), lambda h, w: (h * half + w, 0, 0)),
            pl.BlockSpec((PAIR * HEAD_SIZE, slots), lambda h, w: (h, w)),
            pl.BlockSpec((PAIR, 1, slots), lambda h, w: (h * half + w, 0, 0)),
        ],
        out_shape=[
            jax.ShapeDtypeStruct((count * half, slots, slots), BF16),
            jax.ShapeDtypeStruct((count * HEAD_SIZE, half * slots), BF16),
            jax.ShapeDtypeStruct((count * half, 1, slots), F32),
        ],
        scratch_shapes=[pltpu.VMEM((slots, slots), F32)],
        compiler_params=params(52),
        cost_estimate=cost(count * half * 2e9, count * half * 2 * MIB),
        name="attend",
    )(kept, came, qkv, qkv, qkv, *after)


def unattend_kernel(
    me_ref, weights, scale, mixed, dmixed, q, k, v, hid, dproj, kept, leaving, rows, packed, sems
):
    head, window = pl.program_id(0), pl.program_id(1)
    slots = q.shape[1]

    def prepared(i):
        low = (dmixed[head_rows(i), :].astype(F32) * scale[i]).astype(BF16)
        share = low.astype(F32) * mixed[head_rows(i), :].astype(F32)
        return (low, jnp.sum(share, 0, keepdims=True))

    def dweight_of(i, low, delta):
        return dot_tn(v[head_rows(i), :], low) - delta

    ready = [prepared(i) for i in range(PAIR)]
    dweight = dweight_of(0, *ready[0])
    for i in range(PAIR):
        coming = dweight_of(i + 1, *ready[i + 1]) if i + 1 < PAIR else None
        dscore = (weights[i].astype(F32) * dweight).astype(BF16)
        dquery = dot_nn(k[head_rows(i), :], dscore) * 0.125
        dkey = dot_nt(q[head_rows(i), :], dscore) * 0.6931471805599453
        dvalue = dot_nt(ready[i][0], weights[i])
        for part, grad in enumerate((dquery, dkey, dvalue)):
            dproj[part, head_rows(i), :] = grad.astype(BF16)
        dweight = coming
    start = pl.multiple_of(window * slots, LANES)
    for part in range(3):
        rows[part, head, :, pl.ds(start, slots)] = dproj[part]

    count = pl.num_programs(0)

    @pl.when((head == count - 1) & (window == pl.num_programs(1) - 1))
    def _():
        me = me_ref[0]
        width = rows.shape[1] * rows.shape[2]
        for part in range(3):
            grad = dot_nt(hid[...], rows[part].reshape(width, rows.shape[-1])).astype(BF16)
            for b in range(PARTS):
                slot = slot_of(b ^ me)
                for c in range(width // LANES):
                    at = (part * (width // LANES) + c) * ROWS
                    packed[slot, at : at + ROWS, :] = grad[
                        b * ROWS : (b + 1) * ROWS, c * LANES : (c + 1) * LANES
                    ]
        send_packed(packed, kept, leaving, sems)


def send_packed(packed, kept, leaving, sems, rows=None):
    half = PARTS // 2
    start, height = rows or (0, packed.shape[1])
    copies = [
        pltpu.make_async_copy(
            packed.at[pl.ds(i * half, half), pl.ds(start, height)], target, sems.at[i]
        )
        for i, target in enumerate((kept, leaving))
    ]
    for copy in copies:
        copy.start()
    for copy in copies:
        copy.wait()


def unattend(me, first, count, weights, scale, mixed, dmixed, qkv, hid, after=()):
    slots = weights.shape[-1]
    tokens = qkv.shape[1]
    half = tokens // slots
    height = 3 * count * HEAD_SIZE // LANES * ROWS
    lead = first // PAIR

    def heads(part):
        return pl.BlockSpec(
            (PAIR * HEAD_SIZE, slots), lambda h, w, m: (part * HEADS // PAIR + lead + h, w)
        )

    return pl.pallas_call(
        ignoring(unattend_kernel, 9, len(after)),
        grid_spec=pltpu.PrefetchScalarGridSpec(
            num_scalar_prefetch=1,
            grid=(count // PAIR, half),
            in_specs=[
                pl.BlockSpec((PAIR, slots, slots), lambda h, w, m: (h * half + w, 0, 0)),
                pl.BlockSpec((PAIR, 1, slots), lambda h, w, m: (h * half + w, 0, 0)),
                pl.BlockSpec((PAIR * HEAD_SIZE, slots), lambda h, w, m: (h, w)),
                pl.BlockSpec((PAIR * HEAD_SIZE, slots), lambda h, w, m: (lead + h, w)),
                heads(0),
                heads(1),
                heads(2),
                pl.BlockSpec((D, tokens), lambda h, w, m: (0, 0)),
            ]
            + [ANYWHERE] * len(after),
            out_specs=[
                pl.BlockSpec((3, PAIR * HEAD_SIZE, slots), lambda h, w, m: (0, h, w)),
                ANYWHERE,
                ANYWHERE,
            ],
            scratch_shapes=[
                pltpu.VMEM((3, count // PAIR, PAIR * HEAD_SIZE, tokens), BF16),
                pltpu.VMEM((PARTS, height, LANES), BF16),
                pltpu.SemaphoreType.DMA((2,)),
            ],
        ),
        out_shape=[
            jax.ShapeDtypeStruct((3, count * HEAD_SIZE, tokens), BF16),
            jax.ShapeDtypeStruct((PARTS // 2, height, LANES), BF16),
            jax.ShapeDtypeStruct((PARTS // 2, height, LANES), BF16),
        ],
        compiler_params=params(52),
        cost_estimate=cost(count * half * 2.8e9, count * half * 2 * MIB),
        name="unattend",
    )(me, weights, scale, mixed, dmixed, qkv, qkv, qkv, hid, *after)


def gelu_parts(pre):
    bell = jnp.exp(pre * pre * -0.5)
    size = jnp.abs(pre)
    t = 1.0 / (1.0 + 0.23164190 * size)
    poly = t * (
        0.127414796
        + t * (-0.142248368 + t * (0.7107068705 + t * (-0.7265760135 + t * 0.5307027145)))
    )
    tail = poly * bell
    phi = jnp.where(pre >= 0.0, 1.0 - tail, tail)
    return (pre * phi, phi + pre * bell * 0.3989422804014327)


def norm_forward(resid, gain, shift):
    centre = jnp.mean(resid, 0, keepdims=True)
    offset = resid - centre
    inverse = lax.rsqrt(jnp.mean(offset * offset, 0, keepdims=True) + 1e-05)
    unit = offset * inverse
    return (unit * gain + shift, unit, inverse)


def norm_backward(grad, unit, inverse, gain):
    scaled = grad * gain
    first = jnp.mean(scaled, 0, keepdims=True)
    second = jnp.mean(scaled * unit, 0, keepdims=True)
    return (scaled - first - unit * second) * inverse


def wide(block, size):
    return jnp.concatenate([block] * (size // LANES), axis=1)


def folded(block):
    total = block[:, 0:LANES]
    for at in range(LANES, block.shape[1], LANES):
        total = total + block[:, at : at + LANES]
    return total


def middle_kernel(
    me_ref,
    a0,
    a1,
    b0,
    b1,
    *refs,
):
    fetched, (dmixed_out, dattn_out), refs = refs[:7], refs[7:9], refs[9:]
    spaces, (dmixed, dattn), refs = refs[-10:-3], refs[-3:-1], (*refs[:-10], refs[-1])
    arrivals = [
        pltpu.make_async_copy(array, space, refs[-1].at[i])
        for i, (array, space) in enumerate(zip(fetched, spaces))
    ]
    for arrival in arrivals:
        arrival.start()
    results = [
        pltpu.make_async_copy(space, array, refs[-1].at[len(arrivals) + i])
        for i, (space, array) in enumerate(((dmixed, dmixed_out), (dattn, dattn_out)))
    ]
    middle_body(me_ref, a0, a1, b0, b1, *spaces, dmixed, dattn, *refs[:-1], arrivals, results)


def middle_body(
    me_ref,
    a0,
    a1,
    b0,
    b1,
    embed,
    kept_n,
    came_n,
    kept_t,
    came_t,
    mixed_a,
    mixed_b,
    dmixed,
    dattn,
    counted,
    kept_a,
    leaving_a,
    kept_b,
    leaving_b,
    w_out,
    w_up,
    w_down,
    w_head,
    t_out,
    t_up,
    t_down,
    norms,
    middle_s,
    active_s,
    dbranch_s,
    dpre_s,
    final_s,
    dguess_s,
    norm_sums,
    loss_sum,
    packed,
    sems,
    arrivals,
    results,
):
    ff = active_s.shape[0]
    chunks = ff // D
    me = me_ref[0]
    windows, local, _ = kept_n.shape
    slots = 2 * local

    def set_up():
        copies = [
            pltpu.make_async_copy(
                block, packed.at[pl.ds(i % 2 * 8, 8), pl.ds(at, block.shape[1])], sems.at[i]
            )
            for i, (at, block) in enumerate(((0, a0), (0, a1), (DOWN_AT, b0), (DOWN_AT, b1)))
        ]
        for copy in copies:
            copy.start()
        for copy in copies:
            copy.wait()
        total = jnp.zeros((1, 1), F32)
        for slot in range(PARTS):
            owner = me ^ offset_of(slot)
            for c in range(4):
                cols = slice(c * LANES, (c + 1) * LANES)
                at = OUT_AT + c * ROWS
                w_out[owner, :, cols] = packed[slot, at : at + ROWS, :]
                at = DOWN_AT + c * LANES
                w_down[owner, :, cols] = packed[slot, at : at + LANES, :]
            for c in range(16):
                at = UP_AT + c * ROWS
                w_up[owner, :, c * LANES : (c + 1) * LANES] = packed[slot, at : at + ROWS, :]
            head = packed[slot, HEAD_AT:LOSS_AT, :]
            w_head[owner] = head
            pieces = head[0:1, 100:103].astype(F32)
            total = total + jnp.sum(pieces, 1, keepdims=True)
        counted[...] = jnp.broadcast_to(jnp.maximum(total, 1.0), counted.shape)
        t_out[...] = w_out[...].reshape(D, D).T
        for c in range(chunks):
            rows = slice(c * D, (c + 1) * D)
            t_up[rows, :] = w_up[:, :, rows].reshape(D, D).T
            t_down[:, rows] = w_down[c * 4 : (c + 1) * 4].reshape(D, D).T
        extra = w_head[...].reshape(D, LANES)
        for i in range(4):
            column = extra[:, 96 + i : 97 + i].astype(F32)
            norms[i] = jnp.broadcast_to(column, (D, LANES))
        norm_sums[...] = jnp.zeros_like(norm_sums)
        loss_sum[...] = jnp.zeros_like(loss_sum)

    set_up()
    for arrival in arrivals:
        arrival.wait()
    tiles = [
        middle_tile(
            window * slots,
            slots,
            jnp.concatenate([kept_n[window], came_n[window]], axis=0),
            jnp.concatenate([kept_t[window], came_t[window]], axis=0),
            *(embed, mixed_a, mixed_b, dmixed, dattn, counted),
            *(w_out, w_up, w_down, w_head, t_out, t_up, t_down, norms),
            *(middle_s, active_s, dbranch_s, dpre_s, final_s, dguess_s, norm_sums, loss_sum),
        )
        for window in range(windows)
    ]
    in_turn(tiles, LAG)
    for result in results:
        result.start()

    def place(grad, first_row, blocks, base):
        height = grad.shape[0] // blocks
        for b in range(blocks):
            slot = slot_of((first_row + b) ^ me)
            for c in range(grad.shape[1] // LANES):
                at = base + c * height
                packed[slot, at : at + height, :] = grad[
                    b * height : (b + 1) * height, c * LANES : (c + 1) * LANES
                ]

    for c in range(chunks):
        rows = slice(c * D, (c + 1) * D)
        place(dot_nt(active_s[rows, :], dbranch_s[...]).astype(BF16), c * 4, 4, DOWN_AT)
        place(
            dot_nt(middle_s[...], dpre_s[rows, :]).astype(BF16),
            0,
            PARTS,
            UP_AT + c * (D // LANES) * ROWS,
        )
    for i, side in enumerate((mixed_a, mixed_b)):
        grad = dot_nt(side[...], dattn[...]).astype(BF16)
        place(grad, i * (PARTS // 2), PARTS // 2, OUT_AT)
    head = dot_nn(final_s[...], dguess_s[...])
    lane = lane_index(head.shape)
    for i in range(4):
        head = jnp.where(lane == 96 + i, jnp.sum(norm_sums[i], 1, keepdims=True), head)
    place(head.astype(BF16), 0, PARTS, HEAD_AT)
    row = lax.broadcasted_iota(jnp.int32, (BUNDLE - LOSS_AT, LANES), 0)
    losses = jnp.where(row == 0, loss_sum[...], 0.0).astype(BF16)
    for slot in range(PARTS):
        packed[slot, LOSS_AT:BUNDLE, :] = losses
    send_packed(packed, kept_a, leaving_a, sems, (0, CUT))
    send_packed(packed, kept_b, leaving_b, sems, (CUT, BUNDLE - CUT))
    for result in results:
        result.wait()


def in_turn(streams, lag):
    waiting = [lag * i for i in range(len(streams))]
    live = [True] * len(streams)
    while any(live):
        for i, stream in enumerate(streams):
            if waiting[i] > 0:
                waiting[i] -= 1
            elif live[i]:
                live[i] = next(stream, stream) is not stream


def middle_tile(
    at,
    size,
    normed,
    future,
    embed,
    mixed_a,
    mixed_b,
    dmixed,
    dattn,
    counted,
    w_out,
    w_up,
    w_down,
    w_head,
    t_out,
    t_up,
    t_down,
    norms,
    middle_s,
    active_s,
    dbranch_s,
    dpre_s,
    final_s,
    dguess_s,
    norm_sums,
    loss_sum,
):
    ff = active_s.shape[0]
    height = FF_ROWS
    cols = slice(at, at + size)
    mixed = jnp.concatenate([mixed_a[:, cols], mixed_b[:, cols]], axis=0)
    resid = dot_nt(embed[...].reshape(D, LANES), normed) + dot_nn(t_out[...], mixed)
    yield
    gain_one, gain_two = wide(norms[0], size), wide(norms[2], size)
    middle, unit_one, inverse_one = norm_forward(resid, gain_one, wide(norms[1], size))
    middle_low = middle.astype(BF16)
    middle_s[:, cols] = middle_low
    yield
    for row in range(0, ff, height):
        rows = slice(row, row + height)
        active, gradient = gelu_parts(dot_nn(t_up[rows, :], middle_low))
        active_s[rows, cols] = active.astype(BF16)
        dpre_s[rows, cols] = gradient.astype(BF16)
        yield
    yield
    resid = middle + dot_nn(t_down[...], active_s[:, cols])
    yield
    final, unit_two, inverse_two = norm_forward(resid, gain_two, wide(norms[3], size))
    final_low = final.astype(BF16)
    final_s[:, cols] = final_low
    w_h = w_head[...].reshape(D, LANES)
    yield
    guess = dot_tn(final_low, w_h)
    yield
    ahead = future[:, 0:LANES]
    weighting = future[:, LANES:]
    centre = future[:, 96:97]
    spread = future[:, 97:98]
    error = guess * spread + centre - ahead
    loss_sum[...] += jnp.sum(weighting * error * error, 0, keepdims=True)
    dguess = (2.0 * weighting * error / counted[0:1, 0:1] * spread).astype(BF16)
    dguess_s[cols, :] = dguess
    yield
    dfinal = dot_nt(w_h, dguess)
    yield
    norm_sums[2] += folded(dfinal * unit_two)
    norm_sums[3] += folded(dfinal)
    dresid = norm_backward(dfinal, unit_two, inverse_two, gain_two)
    dbranch = dresid.astype(BF16)
    dbranch_s[:, cols] = dbranch
    yield
    w_d = w_down[...].reshape(ff, D)
    for row in range(0, ff, height):
        rows = slice(row, row + height)
        dpre = (dot_nn(w_d[rows], dbranch) * dpre_s[rows, cols].astype(F32)).astype(BF16)
        dpre_s[rows, cols] = dpre
        yield
    yield
    dresid = dresid + dot_nn(w_up[...].reshape(D, ff), dpre_s[:, cols])
    yield
    norm_sums[0] += folded(dresid * unit_one)
    norm_sums[1] += folded(dresid)
    dfirst = norm_backward(dresid, unit_one, inverse_one, gain_one).astype(BF16)
    dattn[:, cols] = dfirst
    yield
    dmixed[:, cols] = dot_nn(w_out[...].reshape(D, D), dfirst).astype(BF16)


LAG = 2
FF_ROWS = 512


def middle_pass(me, bundle, embed, kept, came, mixed, ff):
    tokens = mixed[0].shape[1]
    fetched = (embed, kept[0], came[0], kept[1], came[1], *mixed)
    vmem = pl.BlockSpec(memory_space=pltpu.VMEM)
    return pl.pallas_call(
        middle_kernel,
        in_specs=[pl.BlockSpec(memory_space=pltpu.SMEM)] + [ANYWHERE] * 4 + [IN_HBM] * 7,
        out_specs=[IN_HBM, IN_HBM, vmem] + [IN_HBM] * 4,
        scratch_shapes=[
            pltpu.VMEM((PARTS, ROWS, D), BF16),
            pltpu.VMEM((PARTS, ROWS, ff), BF16),
            pltpu.VMEM((PARTS, ff // PARTS, D), BF16),
            pltpu.VMEM((PARTS, ROWS, LANES), BF16),
            pltpu.VMEM((D, D), BF16),
            pltpu.VMEM((ff, D), BF16),
            pltpu.VMEM((D, ff), BF16),
            pltpu.VMEM((4, D, LANES), F32),
            pltpu.VMEM((D, tokens), BF16),
            pltpu.VMEM((ff, tokens), BF16),
            pltpu.VMEM((D, tokens), BF16),
            pltpu.VMEM((ff, tokens), BF16),
            pltpu.VMEM((D, tokens), BF16),
            pltpu.VMEM((tokens, LANES), BF16),
            pltpu.VMEM((4, D, LANES), F32),
            pltpu.VMEM((1, LANES), F32),
            pltpu.VMEM((PARTS, BUNDLE, LANES), BF16),
            pltpu.SemaphoreType.DMA((4,)),
        ]
        + [pltpu.VMEM(array.shape, array.dtype) for array in fetched]
        + [pltpu.VMEM((D, tokens), BF16)] * 2
        + [pltpu.SemaphoreType.DMA((len(fetched) + 2,))],
        out_shape=[
            jax.ShapeDtypeStruct((D, tokens), BF16),
            jax.ShapeDtypeStruct((D, tokens), BF16),
            jax.ShapeDtypeStruct((8, LANES), F32),
            jax.ShapeDtypeStruct((PARTS // 2, CUT, LANES), BF16),
            jax.ShapeDtypeStruct((PARTS // 2, CUT, LANES), BF16),
            jax.ShapeDtypeStruct((PARTS // 2, BUNDLE - CUT, LANES), BF16),
            jax.ShapeDtypeStruct((PARTS // 2, BUNDLE - CUT, LANES), BF16),
        ],
        compiler_params=params(63),
        cost_estimate=cost(35e9, 20 * MIB),
        name="middle",
    )(me, *bundle, *fetched)


def last_kernel(
    me_ref, joint, dproj_a, dproj_b, dattn, kept_n, came_n, near, far, kept, leaving, *scratch
):
    joint_s, dproj_s, dattn_s, normed, packed, sems = scratch
    me = me_ref[0]
    windows, local, _ = kept_n.shape
    slots = 2 * local
    rows = near.shape[1]
    half = PARTS // 2
    copies = [pltpu.make_async_copy(joint, joint_s, sems.at[0])]
    for w in range(windows):
        cols = pl.ds(w * slots, slots)
        for source, target in (
            (dproj_a.at[:, :, cols], dproj_s.at[w, :, pl.ds(0, D // 2)]),
            (dproj_b.at[:, :, cols], dproj_s.at[w, :, pl.ds(D // 2, D // 2)]),
            (dattn.at[:, cols], dattn_s.at[w]),
            (kept_n.at[w], normed.at[w, pl.ds(0, local)]),
            (came_n.at[w], normed.at[w, pl.ds(local, local)]),
        ):
            copies.append(pltpu.make_async_copy(source, target, sems.at[len(copies)]))
    per_window = (len(copies) - 1) // windows
    for i, side in enumerate((near, far)):
        target = packed.at[pl.ds(i * half, half), pl.ds(0, rows)]
        copies.append(pltpu.make_async_copy(side, target, sems.at[len(copies)]))
    for copy in copies:
        copy.start()
    copies[0].wait()
    total = jnp.zeros((D, LANES), F32)
    for w in range(windows):
        for copy in copies[1 + w * per_window : 1 + (w + 1) * per_window]:
            copy.wait()
        dhidden = dattn_s[w].astype(F32)
        for part in range(3):
            weights = joint_s[:, :, part * D : (part + 1) * D].reshape(D, D)
            dhidden = dhidden + dot_nn(weights, dproj_s[w, part])
        total = total + dot_nn(dhidden.astype(BF16), normed[w])
    total = total.astype(BF16)
    for b in range(PARTS):
        packed[slot_of(b ^ me), rows : rows + ROWS, :] = total[b * ROWS : (b + 1) * ROWS, :]
    for copy in copies[-2:]:
        copy.wait()
    send_packed(packed, kept, leaving, sems)


def last_pass(me, joint, dprojs, dattn, kept, came, near, far, after=()):
    windows, local, _ = kept.shape
    slots = 2 * local
    height = near.shape[1] + ROWS
    return pl.pallas_call(
        ignoring(last_kernel, 9, len(after)),
        in_specs=[pl.BlockSpec(memory_space=pltpu.SMEM)]
        + [IN_HBM] * 8
        + [ANYWHERE] * len(after),
        out_specs=[IN_HBM, IN_HBM],
        out_shape=[
            jax.ShapeDtypeStruct((PARTS // 2, height, LANES), BF16),
            jax.ShapeDtypeStruct((PARTS // 2, height, LANES), BF16),
        ],
        scratch_shapes=[
            pltpu.VMEM((PARTS, ROWS, 3 * D), BF16),
            pltpu.VMEM((windows, 3, D, slots), BF16),
            pltpu.VMEM((windows, D, slots), BF16),
            pltpu.VMEM((windows, slots, LANES), BF16),
            pltpu.VMEM((PARTS, height, LANES), BF16),
            pltpu.SemaphoreType.DMA((3 + 5 * windows,)),
        ],
        compiler_params=params(22),
        cost_estimate=cost(10e9, 10 * MIB),
        name="last",
    )(me, joint, *dprojs, dattn, kept, came, near, far, *after)


def adamw(weight, mean, square, grad, count_step):
    mean_next = 0.9 * mean + 0.1 * grad
    square_next = 0.999 * square + 0.001 * grad * grad
    mean_hat = mean_next / (1.0 - 0.9**count_step)
    square_hat = square_next / (1.0 - 0.999**count_step)
    weight_next = weight - 0.1 * (mean_hat / (jnp.sqrt(square_hat) + 1e-08) + 0.1 * weight)
    return (weight_next, mean_next, square_next)


def step_second_kernel(mine_a, other_a, mine_b, other_b, counted, *refs):
    held, results = refs[:15], refs[15:]
    grad = mine_a[...].astype(F32) + other_a[...].astype(F32)
    rest = mine_b[...].astype(F32) + other_b[...].astype(F32)

    def grad_rows(at, height):
        return grad[at : at + height] if at < CUT else rest[at - CUT : at - CUT + height]

    def update(which, at, value):
        states = [held[which * 3 + j] for j in range(3)]
        news = adamw(*[state[at] for state in states], value, float(STEP_NUMBER))
        for j in range(3):
            results[which * 3 + j][at] = news[j]

    def block(c):
        return slice(c * LANES, (c + 1) * LANES)

    for c in range(4):
        base = OUT_AT + c * ROWS
        update(0, (0, slice(None), block(c)), grad[base : base + ROWS])
    for c in range(16):
        base = UP_AT + c * ROWS
        update(1, (0, slice(None), block(c)), grad[base : base + ROWS])
    for c in range(4):
        update(2, (0, slice(None), block(c)), grad_rows(DOWN_AT + c * LANES, LANES))
    horizon = held[9].shape[-1]
    head = grad_rows(HEAD_AT, ROWS)
    update(3, (slice(None), slice(None)), head[:, 0:horizon])
    norm = jnp.concatenate([head] * (LANES // ROWS), axis=0).T[96:100, 0:ROWS]
    update(4, (0, slice(None), slice(None)), norm)
    results[15][0] = norm
    losses = jnp.sum(grad_rows(LOSS_AT, 1), 1, keepdims=True)
    results[16][...] = losses / counted[0:1, 0:1]


def step_second(pair_a, pair_b, counted, states):
    shapes = [jax.ShapeDtypeStruct(a.shape, F32) for a in states]
    return pl.pallas_call(
        step_second_kernel,
        out_shape=shapes
        + [jax.ShapeDtypeStruct(states[12].shape, F32), jax.ShapeDtypeStruct((1, 1), F32)],
        compiler_params=params(20),
        cost_estimate=cost(0, 5 * MIB),
        name="step_second",
    )(*pair_a, *pair_b, counted, *states)


def step_first_kernel(mine_a, other_a, mine_b, other_b, *refs):
    held, results = refs[:6], refs[6:]
    halves = [
        mine_a[...].astype(F32) + other_a[...].astype(F32),
        mine_b[...].astype(F32) + other_b[...].astype(F32),
    ]

    def update(which, at, value):
        states = [held[which * 3 + j] for j in range(3)]
        news = adamw(*[state[at] for state in states], value, float(STEP_NUMBER))
        for j in range(3):
            results[which * 3 + j][at] = news[j]

    for part in range(3):
        for side in range(2):
            for c in range(2):
                at = (part * 2 + c) * ROWS
                start = part * D + side * (D // 2) + c * LANES
                update(0, (0, slice(None), slice(start, start + LANES)), halves[side][at : at + ROWS])
    look = held[3].shape[-1]
    update(1, (slice(None), slice(None)), halves[1][6 * ROWS : 7 * ROWS, 0:look])


def step_first(pair_a, pair_b, states):
    shapes = [jax.ShapeDtypeStruct(a.shape, F32) for a in states]
    return pl.pallas_call(
        step_first_kernel,
        out_shape=shapes,
        compiler_params=params(12),
        cost_estimate=cost(0, 2 * MIB),
        name="step_first",
    )(*pair_a, *pair_b, *states)


def whole_windows_body(
    series,
    target,
    valid_slots,
    observed,
    embed_weight,
    joint_proj,
    out_proj,
    up_proj,
    down_proj,
    head_weight,
    norm_params,
    embed_mean,
    joint_mean,
    out_mean,
    up_mean,
    down_mean,
    head_mean,
    norm_mean,
    embed_square,
    joint_square,
    out_square,
    up_square,
    down_square,
    head_square,
    norm_square,
):
    me = lax.axis_index("var").astype(jnp.int32).reshape(1)
    pos = lax.axis_index("win").astype(jnp.int32).reshape(1)
    ff = up_proj.shape[-1]
    packed = pack_first(joint_proj, embed_weight.T)
    row = sent_along_z([packed] * 3)
    turned = [array.transpose(0, 2, 1) for array in (series, target, observed)]
    prepared = prep(pos, *turned, valid_slots.reshape(1, -1), [packed])
    own = prepared[4]
    kept, came = prepared[0:4:2], [swapped(sent, "win", 1) for sent in prepared[1:4:2]]
    (plane,) = stacked([[packed, *row]], [prepared[0]])
    bundles = pack_second(
        own, came[0], out_proj, up_proj, down_proj, head_weight, norm_params, [plane]
    )
    (held,) = stacked([[plane, swapped(plane, "var", 2)]], [bundles[0]])
    qkv, hid, joint, embed = project(me, (held, swapped(held, "var", 1)), kept[0], came[0])
    count = HEADS // 2
    plane_a, bundle_b = stacked(
        [[bundles[0], *sent_along_z([bundles[0]] * 3)], [bundles[1]]], [qkv]
    )
    bundle_b = bundle_b[0]
    sides = [attend(0, count, kept[0], came[0], qkv, [plane_a, came[1]])]
    held_a, plane_b = stacked(
        [
            [plane_a, swapped(plane_a, "var", 2)],
            [bundle_b, *sent_along_z([bundle_b] * 3)],
        ],
        [sides[0][1]],
    )
    sides.append(attend(count, count, kept[0], came[0], qkv, [plane_b]))
    (held_b,) = stacked([[plane_b, swapped(plane_b, "var", 2)]], [sides[1][1]])
    dmixed, dattn, counted, kept_a, leaving_a, kept_b, leaving_b = middle_pass(
        me,
        [held_a, swapped(held_a, "var", 1), held_b, swapped(held_b, "var", 1)],
        embed,
        kept,
        came,
        [side[1] for side in sides],
        ff,
    )

    def back(side, after):
        weights, mixed, scale = sides[side]
        return unattend(me, side * count, count, weights, scale, mixed, dmixed, qkv, hid, after)

    core_a = summed([core_terms(kept_a, leaving_a)])
    dproj_a, *joint_a = back(0, core_a[:1])
    sums = summed([y_terms(*core_a), core_terms(kept_b, leaving_b)], [dproj_a])
    y_a, core_b = sums[:4], sums[4:]
    dproj_b, *joint_b = back(1, core_b[:1])
    sums = summed([z_terms(*y_a), y_terms(*core_b), core_terms(*joint_a)], [dproj_b])
    mine_a, y_b, joint_a = sums[0], sums[1:5], sums[5:]
    leaving = last_pass(me, joint, [dproj_a, dproj_b], dattn, kept[0], came[0], *joint_b, [mine_a])
    pair_a = with_other(mine_a)
    sums = summed([z_terms(*y_b), y_terms(*joint_a), ([leaving[1]], 1)])
    mine_b, joint_a = sums[0], sums[1:5]
    pair_b = with_other(mine_b)
    rest = summed([core_terms(leaving[0], sums[5])])
    states = []
    for group in (
        (out_proj, out_mean, out_square),
        (up_proj, up_mean, up_square),
        (down_proj, down_mean, down_square),
        (head_weight, head_mean, head_square),
        (norm_params, norm_mean, norm_square),
    ):
        states.extend(group)
    new = step_second(pair_a, pair_b, counted, states)
    sums = summed([z_terms(*joint_a), y_terms(*rest)], [new[16]])
    first_a = with_other(sums[0])
    first_b = with_other(summed([z_terms(*sums[1:5])])[0])
    fresh = step_first(
        first_a,
        first_b,
        [joint_proj, joint_mean, joint_square, embed_weight.T, embed_mean.T, embed_square.T],
    )
    outs, ups, downs, heads, norms = [new[3 * i : 3 * i + 3] for i in range(5)]
    embeds = [e.T for e in fresh[3:6]]
    return (
        new[16].reshape(1),
        embeds[0],
        fresh[0],
        outs[0],
        ups[0],
        downs[0],
        heads[0],
        new[15],
        embeds[1],
        fresh[1],
        outs[1],
        ups[1],
        downs[1],
        heads[1],
        norms[1],
        embeds[2],
        fresh[2],
        outs[2],
        ups[2],
        downs[2],
        heads[2],
        norms[2],
    )


def passed_along(block, axis, distance):
    devices = range(lax.axis_size(axis))
    route = [((i - distance) % len(devices), i) for i in devices]
    return lax.ppermute(block, axis, route)


def layer_norm(resid, gain, shift):
    centre = jnp.mean(resid, -1, keepdims=True)
    offset = resid - centre
    spread = jnp.mean(offset * offset, -1, keepdims=True)
    return offset * lax.rsqrt(spread + 1e-05) * gain + shift


def to_items(matrix, windows, local, parts):
    shaped = matrix.reshape(windows, local, parts, HEADS, HEAD_SIZE).transpose(0, 3, 1, 2, 4)
    return shaped.reshape(windows * HEADS, local, parts * HEAD_SIZE)


def from_items(items, windows, local, parts):
    shaped = items.reshape(windows, HEADS, local, parts, HEAD_SIZE).transpose(0, 2, 3, 1, 4)
    return shaped.reshape(windows * local, parts * HEADS * HEAD_SIZE)


def masked_scores(query_rows, key_portion, markers, query_pos, key_pos):
    score_matrix = (
        jnp.einsum("acn,azn->acz", query_rows, key_portion, preferred_element_type=jnp.float32)
        * 0.125
    )
    allowed = (markers[None, :] > 0.5) | (query_pos[:, None] == key_pos[None, :])
    return jnp.where(allowed[None], score_matrix, -1e30)


def absorb(state, query_rows, paired_keys, markers, query_pos, key_pos):
    peak, totals, accum = state
    score_matrix = masked_scores(
        query_rows, paired_keys[..., :HEAD_SIZE], markers, query_pos, key_pos
    )
    top_new = jnp.maximum(peak, jnp.max(score_matrix, -1))
    rescale = jnp.exp(peak - top_new)
    weights = jnp.exp(score_matrix - top_new[..., None])
    totals = totals * rescale + jnp.sum(weights, -1)
    reduced_weights = weights.astype(jnp.bfloat16)
    accum = accum * rescale[..., None] + jnp.einsum(
        "zsx,zxj->zsj",
        reduced_weights,
        paired_keys[..., HEAD_SIZE:],
        preferred_element_type=jnp.float32,
    )
    return (top_new, totals, accum)


def release(
    dquery, query_rows, paired_keys, markers, query_pos, key_pos, log_total, mixed_gradient, deltas
):
    key_portion = paired_keys[..., :HEAD_SIZE]
    value_rows = paired_keys[..., HEAD_SIZE:]
    score_matrix = masked_scores(query_rows, key_portion, markers, query_pos, key_pos)
    weights = jnp.exp(score_matrix - log_total[..., None])
    weight_gradient = jnp.einsum(
        "acn,azn->acz", mixed_gradient, value_rows, preferred_element_type=jnp.float32
    )
    score_gradient = (weights * (weight_gradient - deltas[..., None])).astype(jnp.bfloat16)
    reduced_weights = weights.astype(jnp.bfloat16)
    dquery = (
        dquery
        + jnp.einsum(
            "zsx,zxj->zsj", score_gradient, key_portion, preferred_element_type=jnp.float32
        )
        * 0.125
    )
    key_gradient = (
        jnp.einsum("fov,foc->fvc", score_gradient, query_rows, preferred_element_type=jnp.float32)
        * 0.125
    )
    value_gradient = jnp.einsum(
        "fov,foc->fvc", reduced_weights, mixed_gradient, preferred_element_type=jnp.float32
    )
    return (dquery, key_gradient, value_gradient)


def empty_state(blocks, length):
    return (
        jnp.full((blocks, length), -1e30, jnp.float32),
        jnp.zeros((blocks, length), jnp.float32),
        jnp.zeros((blocks, length, HEAD_SIZE), jnp.float32),
    )


def attend_forward(items, markers, position, group, local):
    blocks = items.shape[0]
    query_rows = items[..., :HEAD_SIZE]
    paired_keys = items[..., HEAD_SIZE:]
    query_pos = position * local + jnp.arange(local, dtype=jnp.int32)
    state = absorb(
        empty_state(blocks, local), query_rows, paired_keys, markers, query_pos, query_pos
    )

    def turn(counter, carry):
        moving, moving_marks, state = carry
        moving, moving_marks = passed_along((moving, moving_marks), "win", 1)
        key_pos = (position - counter) % group * local + jnp.arange(local, dtype=jnp.int32)
        return (
            moving,
            moving_marks,
            absorb(state, query_rows, moving, moving_marks, query_pos, key_pos),
        )

    _, _, state = lax.fori_loop(1, group, turn, (paired_keys, markers, state))
    peak, totals, accum = state
    mixed_full = accum / totals[..., None]
    return (mixed_full.astype(jnp.bfloat16), (mixed_full, peak + jnp.log(totals)))


def attend_backward(items, markers, mixed_gradient, kept, position, group, local):
    blocks = items.shape[0]
    mixed_full, log_total = kept
    query_rows = items[..., :HEAD_SIZE]
    deltas = jnp.sum(mixed_gradient.astype(jnp.float32) * mixed_full, -1)
    query_pos = position * local + jnp.arange(local, dtype=jnp.int32)

    def turn(counter, carry):
        moving, moving_marks, dquery, dpairs = carry
        key_pos = (position - counter) % group * local + jnp.arange(local, dtype=jnp.int32)
        dquery, key_gradient, value_gradient = release(
            dquery,
            query_rows,
            moving,
            moving_marks,
            query_pos,
            key_pos,
            log_total,
            mixed_gradient,
            deltas,
        )
        dpairs = passed_along(
            (dpairs + jnp.concatenate([key_gradient, value_gradient], -1)).astype(jnp.bfloat16),
            "win",
            1,
        ).astype(jnp.float32)
        moving, moving_marks = passed_along((moving, moving_marks), "win", 1)
        return (moving, moving_marks, dquery, dpairs)

    start = (
        items[..., HEAD_SIZE:],
        markers,
        jnp.zeros((blocks, local, HEAD_SIZE), jnp.float32),
        jnp.zeros((blocks, local, 2 * HEAD_SIZE), jnp.float32),
    )
    _, _, dquery, dpairs = lax.fori_loop(0, group, turn, start)
    return jnp.concatenate([dquery, dpairs], -1).astype(jnp.bfloat16)


def layer_forward(hidden, layer_weights, markers, position, group, windows, local):
    joint, out_mat, up_mat, down_mat, norms = layer_weights
    hidden_low = hidden.astype(jnp.bfloat16)
    items = to_items(
        jnp.dot(hidden_low, joint, preferred_element_type=jnp.float32).astype(jnp.bfloat16),
        windows,
        local,
        3,
    )
    mixed_items, kept_attn = attend_forward(items, markers, position, group, local)
    mixed_low = from_items(mixed_items, windows, local, 1)
    resid_one = hidden + jnp.dot(mixed_low, out_mat, preferred_element_type=jnp.float32)
    middle = layer_norm(resid_one, norms[0], norms[1])
    middle_low = middle.astype(jnp.bfloat16)
    pre_gelu = jnp.dot(middle_low, up_mat, preferred_element_type=jnp.float32)
    activated = jax.nn.gelu(pre_gelu, approximate=False).astype(jnp.bfloat16)
    resid_two = middle + jnp.dot(activated, down_mat, preferred_element_type=jnp.float32)
    result = layer_norm(resid_two, norms[2], norms[3])
    return (
        result,
        (
            hidden_low,
            items,
            kept_attn,
            mixed_low,
            resid_one,
            middle_low,
            pre_gelu,
            activated,
            resid_two,
        ),
    )


def layer_backward(dresult, layer_weights, kept, markers, position, group, windows, local):
    joint, out_mat, up_mat, down_mat, norms = layer_weights
    (
        hidden_low,
        items,
        kept_attn,
        mixed_low,
        resid_one,
        middle_low,
        pre_gelu,
        activated,
        resid_two,
    ) = kept
    _, pull_two = jax.vjp(layer_norm, resid_two, norms[2], norms[3])
    dresid_two, dgain_two, dshift_two = pull_two(dresult)
    dbranch = dresid_two.astype(jnp.bfloat16)
    grad_down = jnp.dot(activated.T, dbranch, preferred_element_type=jnp.float32)
    dactive = jnp.dot(dbranch, down_mat.T, preferred_element_type=jnp.float32)
    _, pull_gelu = jax.vjp(partial(jax.nn.gelu, approximate=False), pre_gelu)
    dpre = pull_gelu(dactive)[0].astype(jnp.bfloat16)
    grad_up = jnp.dot(middle_low.T, dpre, preferred_element_type=jnp.float32)
    dmiddle = dresid_two + jnp.dot(dpre, up_mat.T, preferred_element_type=jnp.float32)
    _, pull_one = jax.vjp(layer_norm, resid_one, norms[0], norms[1])
    dresid_one, dgain_one, dshift_one = pull_one(dmiddle)
    dattn = dresid_one.astype(jnp.bfloat16)
    grad_out = jnp.dot(mixed_low.T, dattn, preferred_element_type=jnp.float32)
    mixed_gradient = jnp.dot(dattn, out_mat.T, preferred_element_type=jnp.float32).astype(
        jnp.bfloat16
    )
    ditems = attend_backward(
        items,
        markers,
        to_items(mixed_gradient, windows, local, 1),
        kept_attn,
        position,
        group,
        local,
    )
    dproj = from_items(ditems, windows, local, 3)
    grad_joint = jnp.dot(hidden_low.T, dproj, preferred_element_type=jnp.float32)
    dhidden = dresid_one + jnp.dot(dproj, joint.T, preferred_element_type=jnp.float32)
    grad_norm = jnp.stack([dgain_one, dshift_one, dgain_two, dshift_two])
    return (dhidden, (grad_joint, grad_out, grad_up, grad_down, grad_norm))


def sliced_windows_body(
    series,
    target,
    valid_slots,
    observed,
    embed_weight,
    joint_proj,
    out_proj,
    up_proj,
    down_proj,
    head_weight,
    norm_params,
    embed_mean,
    joint_mean,
    out_mean,
    up_mean,
    down_mean,
    head_mean,
    norm_mean,
    embed_square,
    joint_square,
    out_square,
    up_square,
    down_square,
    head_square,
    norm_square,
):
    windows = series.shape[0]
    local = series.shape[1]
    row_count = windows * local
    group = lax.axis_size("win")
    position = lax.axis_index("win")
    embed, joint, out_mat, up_mat, down_mat, head_mat, norms_low = (
        lax.all_gather(embed_weight.astype(jnp.bfloat16), "var", axis=1, tiled=True),
        lax.all_gather(joint_proj.astype(jnp.bfloat16), "var", axis=1, tiled=True),
        lax.all_gather(out_proj.astype(jnp.bfloat16), "var", axis=1, tiled=True),
        lax.all_gather(up_proj.astype(jnp.bfloat16), "var", axis=1, tiled=True),
        lax.all_gather(down_proj.astype(jnp.bfloat16), "var", axis=1, tiled=True),
        lax.all_gather(head_weight.astype(jnp.bfloat16), "var", axis=0, tiled=True),
        lax.all_gather(norm_params.astype(jnp.bfloat16), "var", axis=2, tiled=True),
    )
    norms = norms_low.astype(jnp.float32)
    weight_mask = observed.astype(jnp.float32) * valid_slots.astype(jnp.float32)[None, :, None]
    count = jnp.maximum(lax.psum(jnp.sum(weight_mask), ("var", "win")), 1.0)
    markers = valid_slots.astype(jnp.bfloat16)
    centre = jnp.mean(series, -1, keepdims=True)
    offset = series - centre
    spread = jnp.sqrt(jnp.mean(offset * offset, -1, keepdims=True) + 1e-05)
    normed = (offset / spread).astype(jnp.bfloat16).reshape(row_count, -1)
    hidden = jnp.dot(normed, embed, preferred_element_type=jnp.float32)
    layer = 0
    layer_weights = (joint[layer], out_mat[layer], up_mat[layer], down_mat[layer], norms[layer])
    hidden, kept = layer_forward(hidden, layer_weights, markers, position, group, windows, local)
    kept_layers = [kept]
    final_low = hidden.astype(jnp.bfloat16)
    guess = (
        jnp.dot(final_low, head_mat, preferred_element_type=jnp.float32).reshape(windows, local, -1)
        * spread
        + centre
    )
    error = guess - target
    loss_part = jnp.sum(weight_mask * error * error)
    dguess = (
        (2.0 * weight_mask * error / count * spread).reshape(row_count, -1).astype(jnp.bfloat16)
    )
    grad_head = jnp.dot(final_low.T, dguess, preferred_element_type=jnp.float32)
    dhidden = jnp.dot(dguess, head_mat.T, preferred_element_type=jnp.float32)
    layer_grads = [None] * LAYERS
    for layer in reversed(range(LAYERS)):
        layer_weights = (joint[layer], out_mat[layer], up_mat[layer], down_mat[layer], norms[layer])
        dhidden, layer_grads[layer] = layer_backward(
            dhidden, layer_weights, kept_layers[layer], markers, position, group, windows, local
        )
    grad_embed = jnp.dot(normed.T, dhidden.astype(jnp.bfloat16), preferred_element_type=jnp.float32)
    stacked = [jnp.stack([grads[i] for grads in layer_grads]) for i in range(5)]
    summed = (
        lax.psum_scatter(
            grad_embed.astype(jnp.bfloat16), "var", scatter_dimension=1, tiled=True
        ).astype(jnp.float32),
        lax.psum_scatter(
            stacked[0].astype(jnp.bfloat16), "var", scatter_dimension=1, tiled=True
        ).astype(jnp.float32),
        lax.psum_scatter(
            stacked[1].astype(jnp.bfloat16), "var", scatter_dimension=1, tiled=True
        ).astype(jnp.float32),
        lax.psum_scatter(
            stacked[2].astype(jnp.bfloat16), "var", scatter_dimension=1, tiled=True
        ).astype(jnp.float32),
        lax.psum_scatter(
            stacked[3].astype(jnp.bfloat16), "var", scatter_dimension=1, tiled=True
        ).astype(jnp.float32),
        lax.psum_scatter(
            grad_head.astype(jnp.bfloat16), "var", scatter_dimension=0, tiled=True
        ).astype(jnp.float32),
        lax.psum_scatter(
            stacked[4].astype(jnp.bfloat16), "var", scatter_dimension=2, tiled=True
        ).astype(jnp.float32),
    )
    totals = (
        lax.psum(summed[0].astype(jnp.bfloat16), "win").astype(jnp.float32),
        lax.psum(summed[1].astype(jnp.bfloat16), "win").astype(jnp.float32),
        lax.psum(summed[2].astype(jnp.bfloat16), "win").astype(jnp.float32),
        lax.psum(summed[3].astype(jnp.bfloat16), "win").astype(jnp.float32),
        lax.psum(summed[4].astype(jnp.bfloat16), "win").astype(jnp.float32),
        lax.psum(summed[5].astype(jnp.bfloat16), "win").astype(jnp.float32),
        lax.psum(summed[6].astype(jnp.bfloat16), "win").astype(jnp.float32),
    )
    loss = lax.psum(loss_part, ("var", "win")) / count
    count_step = float(STEP_NUMBER)
    weights = (embed_weight, joint_proj, out_proj, up_proj, down_proj, head_weight, norm_params)
    means = (embed_mean, joint_mean, out_mean, up_mean, down_mean, head_mean, norm_mean)
    squares = (
        embed_square,
        joint_square,
        out_square,
        up_square,
        down_square,
        head_square,
        norm_square,
    )
    results = [adamw(weights[i], means[i], squares[i], totals[i], count_step) for i in range(7)]
    return (
        loss.reshape(1),
        results[0][0],
        results[1][0],
        results[2][0],
        results[3][0],
        results[4][0],
        results[5][0],
        totals[6],
        results[0][1],
        results[1][1],
        results[2][1],
        results[3][1],
        results[4][1],
        results[5][1],
        results[6][1],
        results[0][2],
        results[1][2],
        results[2][2],
        results[3][2],
        results[4][2],
        results[5][2],
        results[6][2],
    )


def solution(mesh):
    swaps = mesh.shape["var"] == PARTS and mesh.shape["win"] == 2
    body = whole_windows_body if swaps else sliced_windows_body
    placed = (
        P("var", "win", None),
        P("var", "win", None),
        P("win"),
        P("var", "win", None),
        P(None, "var"),
        P(None, "var", None),
        P(None, "var", None),
        P(None, "var", None),
        P(None, "var", None),
        P("var", None),
        P(None, None, "var"),
        P(None, "var"),
        P(None, "var", None),
        P(None, "var", None),
        P(None, "var", None),
        P(None, "var", None),
        P("var", None),
        P(None, None, "var"),
        P(None, "var"),
        P(None, "var", None),
        P(None, "var", None),
        P(None, "var", None),
        P(None, "var", None),
        P("var", None),
        P(None, None, "var"),
    )
    return jax.shard_map(
        body,
        mesh=mesh,
        in_specs=placed,
        out_specs=(
            P(),
            P(None, "var"),
            P(None, "var", None),
            P(None, "var", None),
            P(None, "var", None),
            P(None, "var", None),
            P("var", None),
            P(None, None, "var"),
            P(None, "var"),
            P(None, "var", None),
            P(None, "var", None),
            P(None, "var", None),
            P(None, "var", None),
            P("var", None),
            P(None, None, "var"),
            P(None, "var"),
            P(None, "var", None),
            P(None, "var", None),
            P(None, "var", None),
            P(None, "var", None),
            P("var", None),
            P(None, None, "var"),
        ),
        check_vma=False,
    )
```

```python
from functools import partial

import jax
import jax.numpy as jnp
from jax import lax
from jax.experimental import pallas as pl
from jax.experimental.pallas import tpu as pltpu
from jax.sharding import PartitionSpec as P

HEADS = 8
HEAD_SIZE = 64
LAYERS = 1
STEP_NUMBER = 10

F32 = jnp.float32
BF16 = jnp.bfloat16
LANES = 128
D = HEADS * HEAD_SIZE
PARTS = 16
ROWS = D // PARTS
MIB = 1 << 20

OUT_AT, UP_AT, DOWN_AT, HEAD_AT, LOSS_AT, BUNDLE = 0, 128, 640, 1152, 1184, 1200
CUT = 896
EMBED_AT, FIRST = 384, 416


def dot_nn(a, b):
    return lax.dot_general(a, b, (((1,), (0,)), ((), ())), preferred_element_type=F32)


def dot_nt(a, b):
    return lax.dot_general(a, b, (((1,), (1,)), ((), ())), preferred_element_type=F32)


def dot_tn(a, b):
    return lax.dot_general(a, b, (((0,), (0,)), ((), ())), preferred_element_type=F32)


def offset_of(slot):
    return (slot % 4) * 4 + (slot // 4 % 2) * 2 + slot // 8


def slot_of(offset):
    return (offset & 1) * 8 + ((offset >> 1) & 1) * 4 + (offset >> 2)


def lane_index(shape):
    return lax.broadcasted_iota(jnp.int32, shape, len(shape) - 1)


IN_HBM = pl.BlockSpec(memory_space=pltpu.HBM)
ANYWHERE = pl.BlockSpec(memory_space=pl.ANY)


def ignoring(kernel, reads, ignored):
    def run(*refs):
        kernel(*refs[:reads], *refs[reads + ignored :])

    return run


def params(limit=63, **more):
    return pltpu.CompilerParams(vmem_limit_bytes=limit * MIB, **more)


def cost(flops, moved):
    return pl.CostEstimate(flops=int(flops), bytes_accessed=int(moved), transcendentals=0)


def swapped(block, axis, distance):
    count = lax.axis_size(axis)
    return lax.ppermute(block, axis, [(i, i ^ distance) for i in range(count)])


def sent_along_z(blocks):
    return [swapped(block, "var", 4 * i) for i, block in zip((1, 2, 3), blocks)]


def stacked_kernel(counts, *refs):
    ins, outs, sems = sum(counts), len(counts), refs[-1]
    blocks, results = refs[:ins], refs[ins : ins + outs]
    copies, at = [], 0
    for count, result in zip(counts, results):
        row = 0
        for block in blocks[at : at + count]:
            if len(block.shape) == 2:
                target, height = result.at[row], 1
            else:
                height = block.shape[0]
                target = result.at[pl.ds(row, height)]
            copies.append(pltpu.make_async_copy(block, target, sems.at[len(copies)]))
            row += height
        at += count
    for copy in copies:
        copy.start()
    for copy in copies:
        copy.wait()


def stacked(groups, after=()):
    counts = tuple(len(group) for group in groups)
    blocks = [block for group in groups for block in group]
    shapes = []
    for group in groups:
        rows = sum(1 if block.ndim == 2 else block.shape[0] for block in group)
        shapes.append(jax.ShapeDtypeStruct((rows, *group[0].shape[-2:]), BF16))
    vmem = pl.BlockSpec(memory_space=pltpu.VMEM)
    return pl.pallas_call(
        ignoring(partial(stacked_kernel, counts), len(blocks), len(after)),
        in_specs=[ANYWHERE] * (len(blocks) + len(after)),
        out_specs=[vmem] * len(shapes),
        out_shape=shapes,
        scratch_shapes=[pltpu.SemaphoreType.DMA((len(blocks),))],
        compiler_params=params(6),
        cost_estimate=cost(0, MIB),
        name="stacked",
    )(*blocks, *after)


def summed_kernel(groups, *refs):
    at, to = 0, sum(sum(counts) for counts, _ in groups)
    for counts, parts in groups:
        results = refs[to : to + parts]
        row = 0
        for count in counts:
            total = refs[at][...].astype(F32)
            for ref in refs[at + 1 : at + count]:
                total = total + ref[...].astype(F32)
            total = total.astype(BF16)
            rows = slice(row, row + total.shape[-2])
            for i, ref in enumerate(results):
                if total.ndim == 2:
                    ref[rows, :] = total
                elif len(ref.shape) == 2:
                    ref[rows, :] = total[i]
                else:
                    each = ref.shape[0]
                    ref[:, rows, :] = total[i * each : (i + 1) * each]
            row += total.shape[-2]
            at += count
        to += parts


def summed(groups, after=()):
    counts, shapes = [], []
    for columns, parts in groups:
        counts.append((tuple(len(terms) for terms in columns), parts))
        shape = columns[0][0].shape
        rows = sum(terms[0].shape[-2] for terms in columns)
        lead = () if len(shape) == 2 or shape[0] == parts else (shape[0] // parts,)
        shapes += [jax.ShapeDtypeStruct((*lead, rows, LANES), BF16)] * parts
    arrays = [term for columns, _ in groups for terms in columns for term in terms]
    vmem = pl.BlockSpec(memory_space=pltpu.VMEM)
    return pl.pallas_call(
        ignoring(partial(summed_kernel, tuple(counts)), len(arrays), len(after)),
        in_specs=[vmem] * len(arrays) + [ANYWHERE] * len(after),
        out_specs=[vmem] * len(shapes),
        out_shape=shapes,
        compiler_params=params(12),
        cost_estimate=cost(0, sum(array.size for array in arrays) * 3),
        name="summed",
    )(*arrays, *after)


def core_terms(kept, leaving):
    return [kept, swapped(leaving, "var", 1)]


def y_terms(near, far):
    return ([[near, swapped(far, "var", 2)]], 4)


def z_terms(mine, *others):
    return ([[mine, *sent_along_z(others)]], 1)


def with_other(mine):
    return (mine, swapped(mine, "win", 1))


def three_pieces(value):
    high = value.astype(BF16).astype(F32)
    middle = (value - high).astype(BF16).astype(F32)
    return (high, middle, value - high - middle)


def prep_kernel(
    pos_ref, series, target, observed, valid, kept_n, sent_n, kept_t, sent_t, count, total
):
    step = pl.program_id(0)
    half = pl.num_programs(0) // 2
    rows = series[0]
    look, local = rows.shape
    centre = jnp.mean(rows, 0, keepdims=True)
    offset = rows - centre
    spread = jnp.sqrt(jnp.mean(offset * offset, 0, keepdims=True) + 1e-05)
    normed = offset / spread
    mark = valid[...].astype(F32)
    weight = observed[0].astype(F32) * mark

    @pl.when(step == 0)
    def _():
        total[...] = jnp.zeros_like(total)

    total[...] += jnp.sum(jnp.sum(weight, 0, keepdims=True), 1, keepdims=True)
    spare = LANES - look
    row = lax.broadcasted_iota(jnp.int32, (spare, local), 0)
    extra = jnp.where(row == 0, mark, 0.0)
    for i, piece in enumerate(three_pieces(total[0:1, 0:1])):
        extra = jnp.where(row == 1 + i, piece, extra)
    normed = jnp.concatenate([normed, extra], axis=0).T.astype(BF16)
    extra = jnp.where(row == 0, centre, jnp.where(row == 1, spread, 0.0))
    future = jnp.concatenate([target[0], extra], axis=0).T
    weight = jnp.concatenate([weight, jnp.zeros((spare, local), F32)], axis=0).T

    @pl.when(step < half)
    def _():
        kept_n[0] = normed
        kept_t[0, :, 0:LANES] = future
        kept_t[0, :, LANES:] = weight

    @pl.when(step >= half)
    def _():
        sent_n[0] = normed
        sent_t[0, :, 0:LANES] = future
        sent_t[0, :, LANES:] = weight

    count[...] = total[...]


def prep(pos, series, target, observed, valid, after):
    windows, look, local = series.shape
    half = windows // 2

    def source(i, pos_ref):
        return (lax.rem(pos_ref[0] * half + i, windows), 0, 0)

    def kept(i, pos_ref):
        return (jnp.minimum(i, half - 1), 0, 0)

    def sent(i, pos_ref):
        return (jnp.maximum(i - half, 0), 0, 0)

    block = pl.BlockSpec((1, look, local), source)
    out_shape, out_specs = [], []
    for dtype, width in ((BF16, LANES), (F32, 2 * LANES)):
        for index in (kept, sent):
            out_shape.append(jax.ShapeDtypeStruct((half, local, width), dtype))
            out_specs.append(pl.BlockSpec((1, local, width), index))
    return pl.pallas_call(
        ignoring(prep_kernel, 5, len(after)),
        grid_spec=pltpu.PrefetchScalarGridSpec(
            num_scalar_prefetch=1,
            grid=(windows,),
            in_specs=[block, block, block, pl.BlockSpec((1, local), lambda i, p: (0, 0))]
            + [ANYWHERE] * len(after),
            out_specs=out_specs + [pl.BlockSpec((8, LANES), lambda i, p: (0, 0))],
            scratch_shapes=[pltpu.VMEM((8, LANES), F32)],
        ),
        out_shape=out_shape + [jax.ShapeDtypeStruct((8, LANES), F32)],
        compiler_params=params(8),
        cost_estimate=cost(0, 8 * MIB),
        name="prep",
    )(pos, series, target, observed, valid, *after)


def pack_first_kernel(joint, embed, out):
    for c in range(12):
        out[c * ROWS : (c + 1) * ROWS, :] = joint[0, :, c * LANES : (c + 1) * LANES].astype(BF16)
    look = embed.shape[-1]
    out[EMBED_AT:FIRST, 0:look] = embed[...].astype(BF16)
    out[EMBED_AT:FIRST, look:] = jnp.zeros((ROWS, LANES - look), BF16)


def pack_first(joint, embed):
    return pl.pallas_call(
        pack_first_kernel,
        out_shape=jax.ShapeDtypeStruct((FIRST, LANES), BF16),
        compiler_params=params(4),
        cost_estimate=cost(0, MIB // 2),
        name="pack_first",
    )(joint, embed)


def pack_second_kernel(own, came, out_w, up, down, head, norm, one, two):
    for c in range(4):
        one[OUT_AT + c * ROWS : OUT_AT + (c + 1) * ROWS, :] = out_w[
            0, :, c * LANES : (c + 1) * LANES
        ].astype(BF16)
    for c in range(16):
        one[UP_AT + c * ROWS : UP_AT + (c + 1) * ROWS, :] = up[
            0, :, c * LANES : (c + 1) * LANES
        ].astype(BF16)
    for c in range(4):
        two[c * LANES : (c + 1) * LANES, :] = down[0, :, c * LANES : (c + 1) * LANES].astype(BF16)
    horizon = head.shape[-1]
    spare = (ROWS, LANES - horizon)
    lane = lane_index(spare)
    count = own[0:1, 0:1] + jnp.sum(came[0, 0:1, 97:100].astype(F32), 1, keepdims=True)
    square = jnp.concatenate([norm[0], jnp.zeros((LANES - 4, ROWS), F32)], axis=0)
    square = jnp.concatenate([square] * (LANES // ROWS), axis=1).T
    extra = square[0:ROWS, 0 : LANES - horizon]
    for i, piece in enumerate(three_pieces(count)):
        extra = jnp.where(lane == 4 + i, piece, extra)
    two[HEAD_AT - DOWN_AT : LOSS_AT - DOWN_AT, 0:horizon] = head[...].astype(BF16)
    two[HEAD_AT - DOWN_AT : LOSS_AT - DOWN_AT, horizon:] = extra.astype(BF16)
    two[LOSS_AT - DOWN_AT :, :] = jnp.zeros((BUNDLE - LOSS_AT, LANES), BF16)


def pack_second(own, came, out_w, up, down, head, norm, after):
    half = came.shape[0]
    arrays = (own, came, out_w, up, down, head, norm)
    specs = [pl.BlockSpec(a.shape, lambda i, n=a.ndim: (0,) * n) for a in arrays]
    specs[1] = pl.BlockSpec((1, 16, LANES), lambda i: (half - 1, 0, 0))
    shapes = [(DOWN_AT, LANES), (BUNDLE - DOWN_AT, LANES)]
    return pl.pallas_call(
        ignoring(pack_second_kernel, len(arrays), len(after)),
        grid=(1,),
        in_specs=specs + [ANYWHERE] * len(after),
        out_specs=[pl.BlockSpec(shape, lambda i: (0, 0)) for shape in shapes],
        out_shape=[jax.ShapeDtypeStruct(shape, BF16) for shape in shapes],
        compiler_params=params(8),
        cost_estimate=cost(0, 2 * MIB),
        name="pack_second",
    )(*arrays, *after)


def project_kernel(me_ref, g0, g1, kept, came, qkv, hid, joint, embed):
    @pl.when(pl.program_id(0) == 0)
    def _():
        me = me_ref[0]
        for slot in range(PARTS):
            block = (g0, g1)[slot // 8]
            owner = me ^ offset_of(slot)
            for c in range(12):
                joint[owner, :, c * LANES : (c + 1) * LANES] = block[
                    slot % 8, c * ROWS : (c + 1) * ROWS, :
                ]
            embed[owner] = block[slot % 8, EMBED_AT:FIRST, :]

    normed = jnp.concatenate([kept[0], came[0]], axis=0)
    low = dot_nt(embed[...].reshape(D, LANES), normed).astype(BF16)
    hid[...] = low
    for part in range(3):
        weights = joint[:, :, part * D : (part + 1) * D].reshape(D, D)
        rows = dot_tn(weights, low)
        if part == 0:
            rows = rows * 0.18033688011112042
        qkv[part * D : (part + 1) * D, :] = rows.astype(BF16)


def project(me, bundle, kept, came):
    half, local, _ = kept.shape
    slots = 2 * local
    whole = pl.BlockSpec((8, FIRST, LANES), lambda w, m: (0, 0, 0))
    mine = pl.BlockSpec((1, local, LANES), lambda w, m: (w, 0, 0))
    return pl.pallas_call(
        project_kernel,
        grid_spec=pltpu.PrefetchScalarGridSpec(
            num_scalar_prefetch=1,
            grid=(half,),
            in_specs=[whole] * 2 + [mine] * 2,
            out_specs=[
                pl.BlockSpec((3 * D, slots), lambda w, m: (0, w)),
                pl.BlockSpec((D, slots), lambda w, m: (0, w)),
                pl.BlockSpec((PARTS, ROWS, 3 * D), lambda w, m: (0, 0, 0)),
                pl.BlockSpec((PARTS, ROWS, LANES), lambda w, m: (0, 0, 0)),
            ],
        ),
        out_shape=[
            jax.ShapeDtypeStruct((3 * D, half * slots), BF16),
            jax.ShapeDtypeStruct((D, half * slots), BF16),
            jax.ShapeDtypeStruct((PARTS, ROWS, 3 * D), BF16),
            jax.ShapeDtypeStruct((PARTS, ROWS, LANES), BF16),
        ],
        compiler_params=params(18),
        cost_estimate=cost(3e9, 12 * MIB),
        name="project",
    )(me, *bundle, kept, came)


def tiles_of(length, size):
    return [(at, min(size, length - at)) for at in range(0, length, size)]


PAIR = 2


def head_rows(i):
    return slice(i * HEAD_SIZE, (i + 1) * HEAD_SIZE)


def attend_kernel(kept, came, q, k, v, weights, mixed, scale, bias):
    slots = q.shape[1]
    local = slots // 2

    @pl.when((pl.program_id(0) == 0) & (pl.program_id(1) == 0))
    def _():
        for part, marks in enumerate((kept, came)):
            rows = slice(part * local, (part + 1) * local)
            mark = marks[0, :, 96:97].astype(F32)
            key = part * local + lax.broadcasted_iota(jnp.int32, (local, slots), 0)
            query = lane_index((local, slots))
            bias[rows, :] = jnp.where((mark > 0.5) | (key == query), 0.0, -1e30)

    def score_of(i):
        return dot_tn(k[head_rows(i), :], q[head_rows(i), :]) + bias[...]

    def weigh(i, score):
        weight = jnp.exp2(score - jnp.max(score, 0, keepdims=True))
        low = weight.astype(BF16)
        weights[i] = low
        return (low, jnp.sum(weight, 0, keepdims=True))

    def mix(i, low, total):
        inverse = 1.0 / total
        scale[i] = inverse
        mixed[head_rows(i), :] = (dot_nn(v[head_rows(i), :], low) * inverse).astype(BF16)

    score = score_of(0)
    pending = None
    for i in range(PAIR):
        coming = score_of(i + 1) if i + 1 < PAIR else None
        weighed = weigh(i, score)
        if pending is not None:
            mix(*pending)
        pending = (i, *weighed)
        score = coming
    mix(*pending)


def attend(first, count, kept, came, qkv, after=(), held=()):
    half, local, _ = kept.shape
    slots = 2 * local
    marks = pl.BlockSpec((1, local, LANES), lambda h, w: (0, 0, 0))

    def heads(part):
        return pl.BlockSpec(
            (PAIR * HEAD_SIZE, slots), lambda h, w: ((part * HEADS + first) // PAIR + h, w)
        )

    return pl.pallas_call(
        ignoring(attend_kernel, 5, len(held) + len(after)),
        grid=(count // PAIR, half),
        in_specs=[marks, marks, heads(0), heads(1), heads(2)] + [ANYWHERE] * (len(held) + len(after)),
        out_specs=[
            pl.BlockSpec(
                (PAIR, slots, slots), lambda h, w: ((first // PAIR + h) * half + w, 0, 0)
            ),
            pl.BlockSpec((PAIR * HEAD_SIZE, slots), lambda h, w: (h, w)),
            pl.BlockSpec((PAIR, 1, slots), lambda h, w: (h * half + w, 0, 0)),
        ],
        out_shape=[
            jax.ShapeDtypeStruct((HEADS * half, slots, slots), BF16),
            jax.ShapeDtypeStruct((count * HEAD_SIZE, half * slots), BF16),
            jax.ShapeDtypeStruct((count * half, 1, slots), F32),
        ],
        scratch_shapes=[pltpu.VMEM((slots, slots), F32)],
        compiler_params=params(39),
        cost_estimate=cost(count * half * 2e9, count * half * 2 * MIB),
        name="attend",
        input_output_aliases={5 + i: i for i in range(len(held))},
    )(kept, came, qkv, qkv, qkv, *held, *after)


def unattend_kernel(
    me_ref, weights, scale, mixed, dmixed, q, k, v, hid, dproj, kept, leaving, rows, packed, sems
):
    head, window = pl.program_id(0), pl.program_id(1)
    slots = q.shape[1]

    def prepared(i):
        low = (dmixed[head_rows(i), :].astype(F32) * scale[i]).astype(BF16)
        share = low.astype(F32) * mixed[head_rows(i), :].astype(F32)
        return (low, jnp.sum(share, 0, keepdims=True))

    def dweight_of(i, low, delta):
        return dot_tn(v[head_rows(i), :], low) - delta

    ready = [prepared(i) for i in range(PAIR)]
    dweight = dweight_of(0, *ready[0])
    for i in range(PAIR):
        coming = dweight_of(i + 1, *ready[i + 1]) if i + 1 < PAIR else None
        dscore = (weights[i].astype(F32) * dweight).astype(BF16)
        dquery = dot_nn(k[head_rows(i), :], dscore) * 0.125
        dkey = dot_nt(q[head_rows(i), :], dscore) * 0.6931471805599453
        dvalue = dot_nt(ready[i][0], weights[i])
        for part, grad in enumerate((dquery, dkey, dvalue)):
            dproj[part, head_rows(i), :] = grad.astype(BF16)
        dweight = coming
    start = pl.multiple_of(window * slots, LANES)
    for part in range(3):
        rows[part, head, :, pl.ds(start, slots)] = dproj[part]

    count = pl.num_programs(0)

    @pl.when((head == count - 1) & (window == pl.num_programs(1) - 1))
    def _():
        me = me_ref[0]
        width = rows.shape[1] * rows.shape[2]
        for part in range(3):
            grad = dot_nt(hid[...], rows[part].reshape(width, rows.shape[-1])).astype(BF16)
            for b in range(PARTS):
                slot = slot_of(b ^ me)
                for c in range(width // LANES):
                    at = (part * (width // LANES) + c) * ROWS
                    packed[slot, at : at + ROWS, :] = grad[
                        b * ROWS : (b + 1) * ROWS, c * LANES : (c + 1) * LANES
                    ]
        send_packed(packed, kept, leaving, sems)


def send_packed(packed, kept, leaving, sems, rows=None):
    half = PARTS // 2
    start, height = rows or (0, packed.shape[1])
    copies = [
        pltpu.make_async_copy(
            packed.at[pl.ds(i * half, half), pl.ds(start, height)], target, sems.at[i]
        )
        for i, target in enumerate((kept, leaving))
    ]
    for copy in copies:
        copy.start()
    for copy in copies:
        copy.wait()


def unattend(me, first, count, weights, scale, mixed, dmixed, qkv, hid, after=()):
    slots = weights.shape[-1]
    tokens = qkv.shape[1]
    half = tokens // slots
    height = 3 * count * HEAD_SIZE // LANES * ROWS
    lead = first // PAIR

    def heads(part):
        return pl.BlockSpec(
            (PAIR * HEAD_SIZE, slots), lambda h, w, m: (part * HEADS // PAIR + lead + h, w)
        )

    return pl.pallas_call(
        ignoring(unattend_kernel, 9, len(after)),
        grid_spec=pltpu.PrefetchScalarGridSpec(
            num_scalar_prefetch=1,
            grid=(count // PAIR, half),
            in_specs=[
                pl.BlockSpec(
                    (PAIR, slots, slots), lambda h, w, m: ((lead + h) * half + w, 0, 0)
                ),
                pl.BlockSpec((PAIR, 1, slots), lambda h, w, m: (h * half + w, 0, 0)),
                pl.BlockSpec((PAIR * HEAD_SIZE, slots), lambda h, w, m: (h, w)),
                pl.BlockSpec((PAIR * HEAD_SIZE, slots), lambda h, w, m: (lead + h, w)),
                heads(0),
                heads(1),
                heads(2),
                pl.BlockSpec((D, tokens), lambda h, w, m: (0, 0)),
            ]
            + [ANYWHERE] * len(after),
            out_specs=[
                pl.BlockSpec((3, PAIR * HEAD_SIZE, slots), lambda h, w, m: (0, h, w)),
                ANYWHERE,
                ANYWHERE,
            ],
            scratch_shapes=[
                pltpu.VMEM((3, count // PAIR, PAIR * HEAD_SIZE, tokens), BF16),
                pltpu.VMEM((PARTS, height, LANES), BF16),
                pltpu.SemaphoreType.DMA((2,)),
            ],
        ),
        out_shape=[
            jax.ShapeDtypeStruct((3, count * HEAD_SIZE, tokens), BF16),
            jax.ShapeDtypeStruct((PARTS // 2, height, LANES), BF16),
            jax.ShapeDtypeStruct((PARTS // 2, height, LANES), BF16),
        ],
        compiler_params=params(39),
        cost_estimate=cost(count * half * 2.8e9, count * half * 2 * MIB),
        name="unattend",
    )(me, weights, scale, mixed, dmixed, qkv, qkv, qkv, hid, *after)


def gelu_parts(pre):
    phi = 0.5 + 0.5 * lax.erf(pre * 0.7071067811865476)
    bell = jnp.exp2(pre * pre * -0.7213475204444817)
    return (pre * phi, phi + pre * (bell * 0.3989422804014327))


def norm_forward(resid, gain, shift):
    centre = jnp.mean(resid, 0, keepdims=True)
    offset = resid - centre
    inverse = lax.rsqrt(jnp.mean(offset * offset, 0, keepdims=True) + 1e-05)
    unit = offset * inverse
    return (unit * gain + shift, unit, inverse)


def norm_backward(grad, unit, inverse, gain):
    scaled = grad * gain
    first = jnp.mean(scaled, 0, keepdims=True)
    second = jnp.mean(scaled * unit, 0, keepdims=True)
    return (scaled - first - unit * second) * inverse


def wide(block, size):
    return jnp.concatenate([block] * (size // LANES), axis=1)


def folded(block):
    total = block[:, 0:LANES]
    for at in range(LANES, block.shape[1], LANES):
        total = total + block[:, at : at + LANES]
    return total


def middle_kernel(
    me_ref,
    a0,
    a1,
    b0,
    b1,
    *refs,
):
    fetched, (dmixed_out, dattn_out), refs = refs[:7], refs[7:9], refs[9:]
    spaces, (dmixed, dattn), refs = refs[-8:-3], refs[-3:-1], (*refs[:-8], refs[-1])
    embed, normed, future, mixed_a, mixed_b = spaces
    windows, local, _ = fetched[1].shape
    moves = [(fetched[0], embed), (fetched[5], mixed_a), (fetched[6], mixed_b)]
    for window in range(windows):
        for side in range(2):
            rows = pl.ds((2 * window + side) * local, local)
            moves.append((fetched[1 + side].at[window], normed.at[rows]))
            moves.append((fetched[3 + side].at[window], future.at[rows]))
    arrivals = [
        pltpu.make_async_copy(array, space, refs[-1].at[i])
        for i, (array, space) in enumerate(moves)
    ]
    for arrival in arrivals:
        arrival.start()
    results = [
        pltpu.make_async_copy(space, array, refs[-1].at[len(arrivals) + i])
        for i, (space, array) in enumerate(((dmixed, dmixed_out), (dattn, dattn_out)))
    ]
    middle_body(me_ref, a0, a1, b0, b1, *spaces, dmixed, dattn, *refs[:-1], arrivals, results)


def middle_body(
    me_ref,
    a0,
    a1,
    b0,
    b1,
    embed,
    normed,
    future,
    mixed_a,
    mixed_b,
    dmixed,
    dattn,
    counted,
    kept_a,
    leaving_a,
    kept_b,
    leaving_b,
    w_out,
    w_up,
    w_down,
    w_head,
    t_out,
    t_up,
    t_down,
    norms,
    middle_s,
    active_s,
    dbranch_s,
    dpre_s,
    final_s,
    dguess_s,
    norm_sums,
    loss_sum,
    packed,
    sems,
    arrivals,
    results,
):
    ff = active_s.shape[0]
    chunks = ff // D
    me = me_ref[0]
    tokens = normed.shape[0]

    def set_up():
        copies = [
            pltpu.make_async_copy(
                block, packed.at[pl.ds(i % 2 * 8, 8), pl.ds(at, block.shape[1])], sems.at[i]
            )
            for i, (at, block) in enumerate(((0, a0), (0, a1), (DOWN_AT, b0), (DOWN_AT, b1)))
        ]
        for copy in copies:
            copy.start()
        for copy in copies:
            copy.wait()
        total = jnp.zeros((1, 1), F32)
        for slot in range(PARTS):
            owner = me ^ offset_of(slot)
            for c in range(4):
                cols = slice(c * LANES, (c + 1) * LANES)
                at = OUT_AT + c * ROWS
                w_out[owner, :, cols] = packed[slot, at : at + ROWS, :]
                at = DOWN_AT + c * LANES
                w_down[owner, :, cols] = packed[slot, at : at + LANES, :]
            for c in range(16):
                at = UP_AT + c * ROWS
                w_up[owner, :, c * LANES : (c + 1) * LANES] = packed[slot, at : at + ROWS, :]
            head = packed[slot, HEAD_AT:LOSS_AT, :]
            w_head[owner] = head
            pieces = head[0:1, 100:103].astype(F32)
            total = total + jnp.sum(pieces, 1, keepdims=True)
        counted[...] = jnp.broadcast_to(jnp.maximum(total, 1.0), counted.shape)
        t_out[...] = w_out[...].reshape(D, D).T
        for c in range(chunks):
            rows = slice(c * D, (c + 1) * D)
            t_up[rows, :] = w_up[:, :, rows].reshape(D, D).T
            t_down[:, rows] = w_down[c * 4 : (c + 1) * 4].reshape(D, D).T
        extra = w_head[...].reshape(D, LANES)
        for i in range(4):
            column = extra[:, 96 + i : 97 + i].astype(F32)
            norms[i] = jnp.broadcast_to(column, (D, LANES))
        norm_sums[...] = jnp.zeros_like(norm_sums)
        loss_sum[...] = jnp.zeros_like(loss_sum)

    set_up()
    for arrival in arrivals:
        arrival.wait()
    tiles = [
        middle_tile(
            at,
            min(MIDDLE_SIZE, tokens - at),
            *(normed, future, embed, mixed_a, mixed_b, dmixed, dattn, counted),
            *(w_out, w_up, w_down, w_head, t_out, t_up, t_down, norms),
            *(middle_s, active_s, dbranch_s, dpre_s, final_s, dguess_s, norm_sums, loss_sum),
        )
        for at in range(0, tokens, MIDDLE_SIZE)
    ]
    in_turn(tiles, LAG)
    for result in results:
        result.start()

    def place(grad, first_row, blocks, base):
        height = grad.shape[0] // blocks
        for b in range(blocks):
            slot = slot_of((first_row + b) ^ me)
            for c in range(grad.shape[1] // LANES):
                at = base + c * height
                packed[slot, at : at + height, :] = grad[
                    b * height : (b + 1) * height, c * LANES : (c + 1) * LANES
                ]

    for c in range(chunks):
        rows = slice(c * D, (c + 1) * D)
        place(dot_nt(active_s[rows, :], dbranch_s[...]).astype(BF16), c * 4, 4, DOWN_AT)
        place(
            dot_nt(middle_s[...], dpre_s[rows, :]).astype(BF16),
            0,
            PARTS,
            UP_AT + c * (D // LANES) * ROWS,
        )
    for i, side in enumerate((mixed_a, mixed_b)):
        grad = dot_nt(side[...], dattn[...]).astype(BF16)
        place(grad, i * (PARTS // 2), PARTS // 2, OUT_AT)
    head = dot_nn(final_s[...], dguess_s[...])
    lane = lane_index(head.shape)
    for i in range(4):
        head = jnp.where(lane == 96 + i, jnp.sum(norm_sums[i], 1, keepdims=True), head)
    place(head.astype(BF16), 0, PARTS, HEAD_AT)
    row = lax.broadcasted_iota(jnp.int32, (BUNDLE - LOSS_AT, LANES), 0)
    losses = jnp.where(row == 0, loss_sum[...], 0.0).astype(BF16)
    for slot in range(PARTS):
        packed[slot, LOSS_AT:BUNDLE, :] = losses
    send_packed(packed, kept_a, leaving_a, sems, (0, CUT))
    send_packed(packed, kept_b, leaving_b, sems, (CUT, BUNDLE - CUT))
    for result in results:
        result.wait()


def in_turn(streams, lag):
    waiting = [lag * i for i in range(len(streams))]
    live = [True] * len(streams)
    while any(live):
        for i, stream in enumerate(streams):
            if waiting[i] > 0:
                waiting[i] -= 1
            elif live[i]:
                live[i] = next(stream, stream) is not stream


def middle_tile(
    at,
    size,
    normed,
    future,
    embed,
    mixed_a,
    mixed_b,
    dmixed,
    dattn,
    counted,
    w_out,
    w_up,
    w_down,
    w_head,
    t_out,
    t_up,
    t_down,
    norms,
    middle_s,
    active_s,
    dbranch_s,
    dpre_s,
    final_s,
    dguess_s,
    norm_sums,
    loss_sum,
):
    ff = active_s.shape[0]
    height = FF_ROWS
    cols = slice(at, at + size)
    mixed = jnp.concatenate([mixed_a[:, cols], mixed_b[:, cols]], axis=0)
    resid = dot_nt(embed[...].reshape(D, LANES), normed[cols, :]) + dot_nn(t_out[...], mixed)
    yield
    gain_one, gain_two = wide(norms[0], size), wide(norms[2], size)
    middle, unit_one, inverse_one = norm_forward(resid, gain_one, wide(norms[1], size))
    middle_low = middle.astype(BF16)
    middle_s[:, cols] = middle_low
    yield
    for row in range(0, ff, height):
        rows = slice(row, row + height)
        active, gradient = gelu_parts(dot_nn(t_up[rows, :], middle_low))
        active_s[rows, cols] = active.astype(BF16)
        dpre_s[rows, cols] = gradient.astype(BF16)
        yield
    yield
    resid = middle + dot_nn(t_down[...], active_s[:, cols])
    yield
    final, unit_two, inverse_two = norm_forward(resid, gain_two, wide(norms[3], size))
    final_low = final.astype(BF16)
    final_s[:, cols] = final_low
    w_h = w_head[...].reshape(D, LANES)
    yield
    guess = dot_tn(final_low, w_h)
    yield
    ahead = future[cols, 0:LANES]
    weighting = future[cols, LANES:]
    centre = future[cols, 96:97]
    spread = future[cols, 97:98]
    error = guess * spread + centre - ahead
    loss_sum[...] += jnp.sum(weighting * error * error, 0, keepdims=True)
    dguess = (2.0 * weighting * error / counted[0:1, 0:1] * spread).astype(BF16)
    dguess_s[cols, :] = dguess
    yield
    dfinal = dot_nt(w_h, dguess)
    yield
    norm_sums[2] += folded(dfinal * unit_two)
    norm_sums[3] += folded(dfinal)
    dresid = norm_backward(dfinal, unit_two, inverse_two, gain_two)
    dbranch = dresid.astype(BF16)
    dbranch_s[:, cols] = dbranch
    yield
    w_d = w_down[...].reshape(ff, D)
    for row in range(0, ff, height):
        rows = slice(row, row + height)
        dpre = (dot_nn(w_d[rows], dbranch) * dpre_s[rows, cols].astype(F32)).astype(BF16)
        dpre_s[rows, cols] = dpre
        yield
    yield
    dresid = dresid + dot_nn(w_up[...].reshape(D, ff), dpre_s[:, cols])
    yield
    norm_sums[0] += folded(dresid * unit_one)
    norm_sums[1] += folded(dresid)
    dfirst = norm_backward(dresid, unit_one, inverse_one, gain_one).astype(BF16)
    dattn[:, cols] = dfirst
    yield
    dmixed[:, cols] = dot_nn(w_out[...].reshape(D, D), dfirst).astype(BF16)


LAG = 2
MIDDLE_SIZE = 896
FF_ROWS = 512


def middle_pass(me, bundle, embed, kept, came, mixed, ff):
    tokens = mixed[0].shape[1]
    fetched = (embed, kept[0], came[0], kept[1], came[1], *mixed)
    vmem = pl.BlockSpec(memory_space=pltpu.VMEM)
    return pl.pallas_call(
        middle_kernel,
        in_specs=[pl.BlockSpec(memory_space=pltpu.SMEM)] + [ANYWHERE] * 4 + [IN_HBM] * 7,
        out_specs=[IN_HBM, IN_HBM, vmem] + [IN_HBM] * 4,
        scratch_shapes=[
            pltpu.VMEM((PARTS, ROWS, D), BF16),
            pltpu.VMEM((PARTS, ROWS, ff), BF16),
            pltpu.VMEM((PARTS, ff // PARTS, D), BF16),
            pltpu.VMEM((PARTS, ROWS, LANES), BF16),
            pltpu.VMEM((D, D), BF16),
            pltpu.VMEM((ff, D), BF16),
            pltpu.VMEM((D, ff), BF16),
            pltpu.VMEM((4, D, LANES), F32),
            pltpu.VMEM((D, tokens), BF16),
            pltpu.VMEM((ff, tokens), BF16),
            pltpu.VMEM((D, tokens), BF16),
            pltpu.VMEM((ff, tokens), BF16),
            pltpu.VMEM((D, tokens), BF16),
            pltpu.VMEM((tokens, LANES), BF16),
            pltpu.VMEM((4, D, LANES), F32),
            pltpu.VMEM((1, LANES), F32),
            pltpu.VMEM((PARTS, BUNDLE, LANES), BF16),
            pltpu.SemaphoreType.DMA((4,)),
        ]
        + [
            pltpu.VMEM(embed.shape, BF16),
            pltpu.VMEM((tokens, LANES), BF16),
            pltpu.VMEM((tokens, 2 * LANES), F32),
        ]
        + [pltpu.VMEM((D // 2, tokens), BF16)] * 2
        + [pltpu.VMEM((D, tokens), BF16)] * 2
        + [pltpu.SemaphoreType.DMA((5 + 4 * kept[0].shape[0],))],
        out_shape=[
            jax.ShapeDtypeStruct((D, tokens), BF16),
            jax.ShapeDtypeStruct((D, tokens), BF16),
            jax.ShapeDtypeStruct((8, LANES), F32),
            jax.ShapeDtypeStruct((PARTS // 2, CUT, LANES), BF16),
            jax.ShapeDtypeStruct((PARTS // 2, CUT, LANES), BF16),
            jax.ShapeDtypeStruct((PARTS // 2, BUNDLE - CUT, LANES), BF16),
            jax.ShapeDtypeStruct((PARTS // 2, BUNDLE - CUT, LANES), BF16),
        ],
        compiler_params=params(57),
        cost_estimate=cost(35e9, 20 * MIB),
        name="middle",
    )(me, *bundle, *fetched)


def last_kernel(
    me_ref, joint, dproj_a, dproj_b, dattn, kept_n, came_n, near, far, kept, leaving, *scratch
):
    joint_s, dproj_s, dattn_s, normed, packed, sems = scratch
    me = me_ref[0]
    windows, local, _ = kept_n.shape
    slots = 2 * local
    rows = near.shape[1]
    half = PARTS // 2
    copies = [pltpu.make_async_copy(joint, joint_s, sems.at[0])]
    for w in range(windows):
        cols = pl.ds(w * slots, slots)
        for source, target in (
            (dproj_a.at[:, :, cols], dproj_s.at[w, :, pl.ds(0, D // 2)]),
            (dproj_b.at[:, :, cols], dproj_s.at[w, :, pl.ds(D // 2, D // 2)]),
            (dattn.at[:, cols], dattn_s.at[w]),
            (kept_n.at[w], normed.at[w, pl.ds(0, local)]),
            (came_n.at[w], normed.at[w, pl.ds(local, local)]),
        ):
            copies.append(pltpu.make_async_copy(source, target, sems.at[len(copies)]))
    per_window = (len(copies) - 1) // windows
    for i, side in enumerate((near, far)):
        target = packed.at[pl.ds(i * half, half), pl.ds(0, rows)]
        copies.append(pltpu.make_async_copy(side, target, sems.at[len(copies)]))
    for copy in copies:
        copy.start()
    copies[0].wait()
    total = jnp.zeros((D, LANES), F32)
    for w in range(windows):
        for copy in copies[1 + w * per_window : 1 + (w + 1) * per_window]:
            copy.wait()
        dhidden = dattn_s[w].astype(F32)
        for part in range(3):
            weights = joint_s[:, :, part * D : (part + 1) * D].reshape(D, D)
            dhidden = dhidden + dot_nn(weights, dproj_s[w, part])
        total = total + dot_nn(dhidden.astype(BF16), normed[w])
    total = total.astype(BF16)
    for b in range(PARTS):
        packed[slot_of(b ^ me), rows : rows + ROWS, :] = total[b * ROWS : (b + 1) * ROWS, :]
    for copy in copies[-2:]:
        copy.wait()
    send_packed(packed, kept, leaving, sems)


def last_pass(me, joint, dprojs, dattn, kept, came, near, far, after=()):
    windows, local, _ = kept.shape
    slots = 2 * local
    height = near.shape[1] + ROWS
    return pl.pallas_call(
        ignoring(last_kernel, 9, len(after)),
        in_specs=[pl.BlockSpec(memory_space=pltpu.SMEM)]
        + [IN_HBM] * 8
        + [ANYWHERE] * len(after),
        out_specs=[IN_HBM, IN_HBM],
        out_shape=[
            jax.ShapeDtypeStruct((PARTS // 2, height, LANES), BF16),
            jax.ShapeDtypeStruct((PARTS // 2, height, LANES), BF16),
        ],
        scratch_shapes=[
            pltpu.VMEM((PARTS, ROWS, 3 * D), BF16),
            pltpu.VMEM((windows, 3, D, slots), BF16),
            pltpu.VMEM((windows, D, slots), BF16),
            pltpu.VMEM((windows, slots, LANES), BF16),
            pltpu.VMEM((PARTS, height, LANES), BF16),
            pltpu.SemaphoreType.DMA((3 + 5 * windows,)),
        ],
        compiler_params=params(22),
        cost_estimate=cost(10e9, 10 * MIB),
        name="last",
    )(me, joint, *dprojs, dattn, kept, came, near, far, *after)


def adamw(weight, mean, square, grad, count_step):
    mean_next = 0.9 * mean + 0.1 * grad
    square_next = 0.999 * square + 0.001 * grad * grad
    mean_hat = mean_next / (1.0 - 0.9**count_step)
    square_hat = square_next / (1.0 - 0.999**count_step)
    weight_next = weight - 0.1 * (mean_hat / (jnp.sqrt(square_hat) + 1e-08) + 0.1 * weight)
    return (weight_next, mean_next, square_next)


def step_second_kernel(mine_a, other_a, mine_b, other_b, counted, *refs):
    held, results = refs[:15], refs[15:]
    grad = mine_a[...].astype(F32) + other_a[...].astype(F32)
    rest = mine_b[...].astype(F32) + other_b[...].astype(F32)

    def grad_rows(at, height):
        return grad[at : at + height] if at < CUT else rest[at - CUT : at - CUT + height]

    def update(which, at, value):
        states = [held[which * 3 + j] for j in range(3)]
        news = adamw(*[state[at] for state in states], value, float(STEP_NUMBER))
        for j in range(3):
            results[which * 3 + j][at] = news[j]

    def block(c):
        return slice(c * LANES, (c + 1) * LANES)

    for c in range(4):
        base = OUT_AT + c * ROWS
        update(0, (0, slice(None), block(c)), grad[base : base + ROWS])
    for c in range(16):
        base = UP_AT + c * ROWS
        update(1, (0, slice(None), block(c)), grad[base : base + ROWS])
    for c in range(4):
        update(2, (0, slice(None), block(c)), grad_rows(DOWN_AT + c * LANES, LANES))
    horizon = held[9].shape[-1]
    head = grad_rows(HEAD_AT, ROWS)
    update(3, (slice(None), slice(None)), head[:, 0:horizon])
    norm = jnp.concatenate([head] * (LANES // ROWS), axis=0).T[96:100, 0:ROWS]
    update(4, (0, slice(None), slice(None)), norm)
    results[15][0] = norm
    losses = jnp.sum(grad_rows(LOSS_AT, 1), 1, keepdims=True)
    results[16][...] = losses / counted[0:1, 0:1]


def step_second(pair_a, pair_b, counted, states):
    shapes = [jax.ShapeDtypeStruct(a.shape, F32) for a in states]
    return pl.pallas_call(
        step_second_kernel,
        out_shape=shapes
        + [jax.ShapeDtypeStruct(states[12].shape, F32), jax.ShapeDtypeStruct((1, 1), F32)],
        compiler_params=params(20),
        cost_estimate=cost(0, 5 * MIB),
        name="step_second",
    )(*pair_a, *pair_b, counted, *states)


def step_first_kernel(mine_a, other_a, mine_b, other_b, *refs):
    held, results = refs[:6], refs[6:]
    halves = [
        mine_a[BUNDLE - CUT :, :].astype(F32) + other_a[BUNDLE - CUT :, :].astype(F32),
        mine_b[...].astype(F32) + other_b[...].astype(F32),
    ]

    def update(which, at, value):
        states = [held[which * 3 + j] for j in range(3)]
        news = adamw(*[state[at] for state in states], value, float(STEP_NUMBER))
        for j in range(3):
            results[which * 3 + j][at] = news[j]

    for part in range(3):
        for side in range(2):
            for c in range(2):
                at = (part * 2 + c) * ROWS
                start = part * D + side * (D // 2) + c * LANES
                update(0, (0, slice(None), slice(start, start + LANES)), halves[side][at : at + ROWS])
    look = held[3].shape[-1]
    update(1, (slice(None), slice(None)), halves[1][6 * ROWS : 7 * ROWS, 0:look])


def step_first(pair_a, pair_b, states):
    shapes = [jax.ShapeDtypeStruct(a.shape, F32) for a in states]
    return pl.pallas_call(
        step_first_kernel,
        out_shape=shapes,
        compiler_params=params(12),
        cost_estimate=cost(0, 2 * MIB),
        name="step_first",
    )(*pair_a, *pair_b, *states)


def whole_windows_body(
    series,
    target,
    valid_slots,
    observed,
    embed_weight,
    joint_proj,
    out_proj,
    up_proj,
    down_proj,
    head_weight,
    norm_params,
    embed_mean,
    joint_mean,
    out_mean,
    up_mean,
    down_mean,
    head_mean,
    norm_mean,
    embed_square,
    joint_square,
    out_square,
    up_square,
    down_square,
    head_square,
    norm_square,
):
    me = lax.axis_index("var").astype(jnp.int32).reshape(1)
    pos = lax.axis_index("win").astype(jnp.int32).reshape(1)
    ff = up_proj.shape[-1]
    packed = pack_first(joint_proj, embed_weight.T)
    row = sent_along_z([packed] * 3)
    turned = [array.transpose(0, 2, 1) for array in (series, target, observed)]
    prepared = prep(pos, *turned, valid_slots.reshape(1, -1), [packed])
    own = prepared[4]
    kept, came = prepared[0:4:2], [swapped(sent, "win", 1) for sent in prepared[1:4:2]]
    (plane,) = stacked([[packed, *row]], [prepared[0]])
    bundles = pack_second(
        own, came[0], out_proj, up_proj, down_proj, head_weight, norm_params, [plane]
    )
    (held,) = stacked([[plane, swapped(plane, "var", 2)]], [bundles[0]])
    qkv, hid, joint, embed = project(me, (held, swapped(held, "var", 1)), kept[0], came[0])
    count = HEADS // 2
    plane_a, bundle_b = stacked(
        [[bundles[0], *sent_along_z([bundles[0]] * 3)], [bundles[1]]], [qkv]
    )
    bundle_b = bundle_b[0]
    sides = [attend(0, count, kept[0], came[0], qkv, [plane_a, came[1]])]
    held_a, plane_b = stacked(
        [
            [plane_a, swapped(plane_a, "var", 2)],
            [bundle_b, *sent_along_z([bundle_b] * 3)],
        ],
        [sides[0][1]],
    )
    sides.append(attend(count, count, kept[0], came[0], qkv, [plane_b], [sides[0][0]]))
    (held_b,) = stacked([[plane_b, swapped(plane_b, "var", 2)]], [sides[1][1]])
    dmixed, dattn, counted, kept_a, leaving_a, kept_b, leaving_b = middle_pass(
        me,
        [held_a, swapped(held_a, "var", 1), held_b, swapped(held_b, "var", 1)],
        embed,
        kept,
        came,
        [side[1] for side in sides],
        ff,
    )

    def back(side, after):
        _, mixed, scale = sides[side]
        weights = sides[1][0]
        return unattend(me, side * count, count, weights, scale, mixed, dmixed, qkv, hid, after)

    core_a = summed([([core_terms(kept_a, leaving_a)], 2)])
    dproj_a, *joint_a = back(0, core_a[:1])
    sums = summed(
        [y_terms(*core_a), ([core_terms(kept_b, leaving_b), core_terms(*joint_a)], 2)], [dproj_a]
    )
    y_a, core_b = sums[:4], sums[4:]
    dproj_b, *joint_b = back(1, core_b[:1])
    sums = summed([z_terms(*y_a), y_terms(*core_b)], [dproj_b])
    mine_a, y_b = sums[0], sums[1:]
    leaving = last_pass(me, joint, [dproj_a, dproj_b], dattn, kept[0], came[0], *joint_b, [mine_a])
    pair_a = with_other(mine_a)
    mine_b, onward = summed([z_terms(*y_b), ([[leaving[1]]], 1)], [pair_a[1]])
    pair_b = with_other(mine_b)
    rest = summed([([core_terms(leaving[0], onward)], 2)])
    states = []
    for group in (
        (out_proj, out_mean, out_square),
        (up_proj, up_mean, up_square),
        (down_proj, down_mean, down_square),
        (head_weight, head_mean, head_square),
        (norm_params, norm_mean, norm_square),
    ):
        states.extend(group)
    new = step_second(pair_a, pair_b, counted, states)
    first_b = with_other(summed([z_terms(*summed([y_terms(*rest)]))], [new[16]])[0])
    fresh = step_first(
        pair_b,
        first_b,
        [joint_proj, joint_mean, joint_square, embed_weight.T, embed_mean.T, embed_square.T],
    )
    outs, ups, downs, heads, norms = [new[3 * i : 3 * i + 3] for i in range(5)]
    embeds = [e.T for e in fresh[3:6]]
    return (
        new[16].reshape(1),
        embeds[0],
        fresh[0],
        outs[0],
        ups[0],
        downs[0],
        heads[0],
        new[15],
        embeds[1],
        fresh[1],
        outs[1],
        ups[1],
        downs[1],
        heads[1],
        norms[1],
        embeds[2],
        fresh[2],
        outs[2],
        ups[2],
        downs[2],
        heads[2],
        norms[2],
    )


def passed_along(block, axis, distance):
    devices = range(lax.axis_size(axis))
    route = [((i - distance) % len(devices), i) for i in devices]
    return lax.ppermute(block, axis, route)


def layer_norm(resid, gain, shift):
    centre = jnp.mean(resid, -1, keepdims=True)
    offset = resid - centre
    spread = jnp.mean(offset * offset, -1, keepdims=True)
    return offset * lax.rsqrt(spread + 1e-05) * gain + shift


def to_items(matrix, windows, local, parts):
    shaped = matrix.reshape(windows, local, parts, HEADS, HEAD_SIZE).transpose(0, 3, 1, 2, 4)
    return shaped.reshape(windows * HEADS, local, parts * HEAD_SIZE)


def from_items(items, windows, local, parts):
    shaped = items.reshape(windows, HEADS, local, parts, HEAD_SIZE).transpose(0, 2, 3, 1, 4)
    return shaped.reshape(windows * local, parts * HEADS * HEAD_SIZE)


def masked_scores(query_rows, key_portion, markers, query_pos, key_pos):
    score_matrix = (
        jnp.einsum("acn,azn->acz", query_rows, key_portion, preferred_element_type=jnp.float32)
        * 0.125
    )
    allowed = (markers[None, :] > 0.5) | (query_pos[:, None] == key_pos[None, :])
    return jnp.where(allowed[None], score_matrix, -1e30)


def absorb(state, query_rows, paired_keys, markers, query_pos, key_pos):
    peak, totals, accum = state
    score_matrix = masked_scores(
        query_rows, paired_keys[..., :HEAD_SIZE], markers, query_pos, key_pos
    )
    top_new = jnp.maximum(peak, jnp.max(score_matrix, -1))
    rescale = jnp.exp(peak - top_new)
    weights = jnp.exp(score_matrix - top_new[..., None])
    totals = totals * rescale + jnp.sum(weights, -1)
    reduced_weights = weights.astype(jnp.bfloat16)
    accum = accum * rescale[..., None] + jnp.einsum(
        "zsx,zxj->zsj",
        reduced_weights,
        paired_keys[..., HEAD_SIZE:],
        preferred_element_type=jnp.float32,
    )
    return (top_new, totals, accum)


def release(
    dquery, query_rows, paired_keys, markers, query_pos, key_pos, log_total, mixed_gradient, deltas
):
    key_portion = paired_keys[..., :HEAD_SIZE]
    value_rows = paired_keys[..., HEAD_SIZE:]
    score_matrix = masked_scores(query_rows, key_portion, markers, query_pos, key_pos)
    weights = jnp.exp(score_matrix - log_total[..., None])
    weight_gradient = jnp.einsum(
        "acn,azn->acz", mixed_gradient, value_rows, preferred_element_type=jnp.float32
    )
    score_gradient = (weights * (weight_gradient - deltas[..., None])).astype(jnp.bfloat16)
    reduced_weights = weights.astype(jnp.bfloat16)
    dquery = (
        dquery
        + jnp.einsum(
            "zsx,zxj->zsj", score_gradient, key_portion, preferred_element_type=jnp.float32
        )
        * 0.125
    )
    key_gradient = (
        jnp.einsum("fov,foc->fvc", score_gradient, query_rows, preferred_element_type=jnp.float32)
        * 0.125
    )
    value_gradient = jnp.einsum(
        "fov,foc->fvc", reduced_weights, mixed_gradient, preferred_element_type=jnp.float32
    )
    return (dquery, key_gradient, value_gradient)


def empty_state(blocks, length):
    return (
        jnp.full((blocks, length), -1e30, jnp.float32),
        jnp.zeros((blocks, length), jnp.float32),
        jnp.zeros((blocks, length, HEAD_SIZE), jnp.float32),
    )


def attend_forward(items, markers, position, group, local):
    blocks = items.shape[0]
    query_rows = items[..., :HEAD_SIZE]
    paired_keys = items[..., HEAD_SIZE:]
    query_pos = position * local + jnp.arange(local, dtype=jnp.int32)
    state = absorb(
        empty_state(blocks, local), query_rows, paired_keys, markers, query_pos, query_pos
    )

    def turn(counter, carry):
        moving, moving_marks, state = carry
        moving, moving_marks = passed_along((moving, moving_marks), "win", 1)
        key_pos = (position - counter) % group * local + jnp.arange(local, dtype=jnp.int32)
        return (
            moving,
            moving_marks,
            absorb(state, query_rows, moving, moving_marks, query_pos, key_pos),
        )

    _, _, state = lax.fori_loop(1, group, turn, (paired_keys, markers, state))
    peak, totals, accum = state
    mixed_full = accum / totals[..., None]
    return (mixed_full.astype(jnp.bfloat16), (mixed_full, peak + jnp.log(totals)))


def attend_backward(items, markers, mixed_gradient, kept, position, group, local):
    blocks = items.shape[0]
    mixed_full, log_total = kept
    query_rows = items[..., :HEAD_SIZE]
    deltas = jnp.sum(mixed_gradient.astype(jnp.float32) * mixed_full, -1)
    query_pos = position * local + jnp.arange(local, dtype=jnp.int32)

    def turn(counter, carry):
        moving, moving_marks, dquery, dpairs = carry
        key_pos = (position - counter) % group * local + jnp.arange(local, dtype=jnp.int32)
        dquery, key_gradient, value_gradient = release(
            dquery,
            query_rows,
            moving,
            moving_marks,
            query_pos,
            key_pos,
            log_total,
            mixed_gradient,
            deltas,
        )
        dpairs = passed_along(
            (dpairs + jnp.concatenate([key_gradient, value_gradient], -1)).astype(jnp.bfloat16),
            "win",
            1,
        ).astype(jnp.float32)
        moving, moving_marks = passed_along((moving, moving_marks), "win", 1)
        return (moving, moving_marks, dquery, dpairs)

    start = (
        items[..., HEAD_SIZE:],
        markers,
        jnp.zeros((blocks, local, HEAD_SIZE), jnp.float32),
        jnp.zeros((blocks, local, 2 * HEAD_SIZE), jnp.float32),
    )
    _, _, dquery, dpairs = lax.fori_loop(0, group, turn, start)
    return jnp.concatenate([dquery, dpairs], -1).astype(jnp.bfloat16)


def layer_forward(hidden, layer_weights, markers, position, group, windows, local):
    joint, out_mat, up_mat, down_mat, norms = layer_weights
    hidden_low = hidden.astype(jnp.bfloat16)
    items = to_items(
        jnp.dot(hidden_low, joint, preferred_element_type=jnp.float32).astype(jnp.bfloat16),
        windows,
        local,
        3,
    )
    mixed_items, kept_attn = attend_forward(items, markers, position, group, local)
    mixed_low = from_items(mixed_items, windows, local, 1)
    resid_one = hidden + jnp.dot(mixed_low, out_mat, preferred_element_type=jnp.float32)
    middle = layer_norm(resid_one, norms[0], norms[1])
    middle_low = middle.astype(jnp.bfloat16)
    pre_gelu = jnp.dot(middle_low, up_mat, preferred_element_type=jnp.float32)
    activated = jax.nn.gelu(pre_gelu, approximate=False).astype(jnp.bfloat16)
    resid_two = middle + jnp.dot(activated, down_mat, preferred_element_type=jnp.float32)
    result = layer_norm(resid_two, norms[2], norms[3])
    return (
        result,
        (
            hidden_low,
            items,
            kept_attn,
            mixed_low,
            resid_one,
            middle_low,
            pre_gelu,
            activated,
            resid_two,
        ),
    )


def layer_backward(dresult, layer_weights, kept, markers, position, group, windows, local):
    joint, out_mat, up_mat, down_mat, norms = layer_weights
    (
        hidden_low,
        items,
        kept_attn,
        mixed_low,
        resid_one,
        middle_low,
        pre_gelu,
        activated,
        resid_two,
    ) = kept
    _, pull_two = jax.vjp(layer_norm, resid_two, norms[2], norms[3])
    dresid_two, dgain_two, dshift_two = pull_two(dresult)
    dbranch = dresid_two.astype(jnp.bfloat16)
    grad_down = jnp.dot(activated.T, dbranch, preferred_element_type=jnp.float32)
    dactive = jnp.dot(dbranch, down_mat.T, preferred_element_type=jnp.float32)
    _, pull_gelu = jax.vjp(partial(jax.nn.gelu, approximate=False), pre_gelu)
    dpre = pull_gelu(dactive)[0].astype(jnp.bfloat16)
    grad_up = jnp.dot(middle_low.T, dpre, preferred_element_type=jnp.float32)
    dmiddle = dresid_two + jnp.dot(dpre, up_mat.T, preferred_element_type=jnp.float32)
    _, pull_one = jax.vjp(layer_norm, resid_one, norms[0], norms[1])
    dresid_one, dgain_one, dshift_one = pull_one(dmiddle)
    dattn = dresid_one.astype(jnp.bfloat16)
    grad_out = jnp.dot(mixed_low.T, dattn, preferred_element_type=jnp.float32)
    mixed_gradient = jnp.dot(dattn, out_mat.T, preferred_element_type=jnp.float32).astype(
        jnp.bfloat16
    )
    ditems = attend_backward(
        items,
        markers,
        to_items(mixed_gradient, windows, local, 1),
        kept_attn,
        position,
        group,
        local,
    )
    dproj = from_items(ditems, windows, local, 3)
    grad_joint = jnp.dot(hidden_low.T, dproj, preferred_element_type=jnp.float32)
    dhidden = dresid_one + jnp.dot(dproj, joint.T, preferred_element_type=jnp.float32)
    grad_norm = jnp.stack([dgain_one, dshift_one, dgain_two, dshift_two])
    return (dhidden, (grad_joint, grad_out, grad_up, grad_down, grad_norm))


def sliced_windows_body(
    series,
    target,
    valid_slots,
    observed,
    embed_weight,
    joint_proj,
    out_proj,
    up_proj,
    down_proj,
    head_weight,
    norm_params,
    embed_mean,
    joint_mean,
    out_mean,
    up_mean,
    down_mean,
    head_mean,
    norm_mean,
    embed_square,
    joint_square,
    out_square,
    up_square,
    down_square,
    head_square,
    norm_square,
):
    windows = series.shape[0]
    local = series.shape[1]
    row_count = windows * local
    group = lax.axis_size("win")
    position = lax.axis_index("win")
    embed, joint, out_mat, up_mat, down_mat, head_mat, norms_low = (
        lax.all_gather(embed_weight.astype(jnp.bfloat16), "var", axis=1, tiled=True),
        lax.all_gather(joint_proj.astype(jnp.bfloat16), "var", axis=1, tiled=True),
        lax.all_gather(out_proj.astype(jnp.bfloat16), "var", axis=1, tiled=True),
        lax.all_gather(up_proj.astype(jnp.bfloat16), "var", axis=1, tiled=True),
        lax.all_gather(down_proj.astype(jnp.bfloat16), "var", axis=1, tiled=True),
        lax.all_gather(head_weight.astype(jnp.bfloat16), "var", axis=0, tiled=True),
        lax.all_gather(norm_params.astype(jnp.bfloat16), "var", axis=2, tiled=True),
    )
    norms = norms_low.astype(jnp.float32)
    weight_mask = observed.astype(jnp.float32) * valid_slots.astype(jnp.float32)[None, :, None]
    count = jnp.maximum(lax.psum(jnp.sum(weight_mask), ("var", "win")), 1.0)
    markers = valid_slots.astype(jnp.bfloat16)
    centre = jnp.mean(series, -1, keepdims=True)
    offset = series - centre
    spread = jnp.sqrt(jnp.mean(offset * offset, -1, keepdims=True) + 1e-05)
    normed = (offset / spread).astype(jnp.bfloat16).reshape(row_count, -1)
    hidden = jnp.dot(normed, embed, preferred_element_type=jnp.float32)
    layer = 0
    layer_weights = (joint[layer], out_mat[layer], up_mat[layer], down_mat[layer], norms[layer])
    hidden, kept = layer_forward(hidden, layer_weights, markers, position, group, windows, local)
    kept_layers = [kept]
    final_low = hidden.astype(jnp.bfloat16)
    guess = (
        jnp.dot(final_low, head_mat, preferred_element_type=jnp.float32).reshape(windows, local, -1)
        * spread
        + centre
    )
    error = guess - target
    loss_part = jnp.sum(weight_mask * error * error)
    dguess = (
        (2.0 * weight_mask * error / count * spread).reshape(row_count, -1).astype(jnp.bfloat16)
    )
    grad_head = jnp.dot(final_low.T, dguess, preferred_element_type=jnp.float32)
    dhidden = jnp.dot(dguess, head_mat.T, preferred_element_type=jnp.float32)
    layer_grads = [None] * LAYERS
    for layer in reversed(range(LAYERS)):
        layer_weights = (joint[layer], out_mat[layer], up_mat[layer], down_mat[layer], norms[layer])
        dhidden, layer_grads[layer] = layer_backward(
            dhidden, layer_weights, kept_layers[layer], markers, position, group, windows, local
        )
    grad_embed = jnp.dot(normed.T, dhidden.astype(jnp.bfloat16), preferred_element_type=jnp.float32)
    stacked = [jnp.stack([grads[i] for grads in layer_grads]) for i in range(5)]
    summed = (
        lax.psum_scatter(
            grad_embed.astype(jnp.bfloat16), "var", scatter_dimension=1, tiled=True
        ).astype(jnp.float32),
        lax.psum_scatter(
            stacked[0].astype(jnp.bfloat16), "var", scatter_dimension=1, tiled=True
        ).astype(jnp.float32),
        lax.psum_scatter(
            stacked[1].astype(jnp.bfloat16), "var", scatter_dimension=1, tiled=True
        ).astype(jnp.float32),
        lax.psum_scatter(
            stacked[2].astype(jnp.bfloat16), "var", scatter_dimension=1, tiled=True
        ).astype(jnp.float32),
        lax.psum_scatter(
            stacked[3].astype(jnp.bfloat16), "var", scatter_dimension=1, tiled=True
        ).astype(jnp.float32),
        lax.psum_scatter(
            grad_head.astype(jnp.bfloat16), "var", scatter_dimension=0, tiled=True
        ).astype(jnp.float32),
        lax.psum_scatter(
            stacked[4].astype(jnp.bfloat16), "var", scatter_dimension=2, tiled=True
        ).astype(jnp.float32),
    )
    totals = (
        lax.psum(summed[0].astype(jnp.bfloat16), "win").astype(jnp.float32),
        lax.psum(summed[1].astype(jnp.bfloat16), "win").astype(jnp.float32),
        lax.psum(summed[2].astype(jnp.bfloat16), "win").astype(jnp.float32),
        lax.psum(summed[3].astype(jnp.bfloat16), "win").astype(jnp.float32),
        lax.psum(summed[4].astype(jnp.bfloat16), "win").astype(jnp.float32),
        lax.psum(summed[5].astype(jnp.bfloat16), "win").astype(jnp.float32),
        lax.psum(summed[6].astype(jnp.bfloat16), "win").astype(jnp.float32),
    )
    loss = lax.psum(loss_part, ("var", "win")) / count
    count_step = float(STEP_NUMBER)
    weights = (embed_weight, joint_proj, out_proj, up_proj, down_proj, head_weight, norm_params)
    means = (embed_mean, joint_mean, out_mean, up_mean, down_mean, head_mean, norm_mean)
    squares = (
        embed_square,
        joint_square,
        out_square,
        up_square,
        down_square,
        head_square,
        norm_square,
    )
    results = [adamw(weights[i], means[i], squares[i], totals[i], count_step) for i in range(7)]
    return (
        loss.reshape(1),
        results[0][0],
        results[1][0],
        results[2][0],
        results[3][0],
        results[4][0],
        results[5][0],
        totals[6],
        results[0][1],
        results[1][1],
        results[2][1],
        results[3][1],
        results[4][1],
        results[5][1],
        results[6][1],
        results[0][2],
        results[1][2],
        results[2][2],
        results[3][2],
        results[4][2],
        results[5][2],
        results[6][2],
    )


def solution(mesh):
    swaps = mesh.shape["var"] == PARTS and mesh.shape["win"] == 2
    body = whole_windows_body if swaps else sliced_windows_body
    placed = (
        P("var", "win", None),
        P("var", "win", None),
        P("win"),
        P("var", "win", None),
        P(None, "var"),
        P(None, "var", None),
        P(None, "var", None),
        P(None, "var", None),
        P(None, "var", None),
        P("var", None),
        P(None, None, "var"),
        P(None, "var"),
        P(None, "var", None),
        P(None, "var", None),
        P(None, "var", None),
        P(None, "var", None),
        P("var", None),
        P(None, None, "var"),
        P(None, "var"),
        P(None, "var", None),
        P(None, "var", None),
        P(None, "var", None),
        P(None, "var", None),
        P("var", None),
        P(None, None, "var"),
    )
    return jax.shard_map(
        body,
        mesh=mesh,
        in_specs=placed,
        out_specs=(
            P(),
            P(None, "var"),
            P(None, "var", None),
            P(None, "var", None),
            P(None, "var", None),
            P(None, "var", None),
            P("var", None),
            P(None, None, "var"),
            P(None, "var"),
            P(None, "var", None),
            P(None, "var", None),
            P(None, "var", None),
            P(None, "var", None),
            P("var", None),
            P(None, None, "var"),
            P(None, "var"),
            P(None, "var", None),
            P(None, "var", None),
            P(None, "var", None),
            P(None, "var", None),
            P("var", None),
            P(None, None, "var"),
        ),
        check_vma=False,
    )
```

```python
from functools import partial

import jax
import jax.numpy as jnp
from jax import lax
from jax.experimental import pallas as pl
from jax.experimental.pallas import tpu as pltpu
from jax.sharding import PartitionSpec as P

HEADS = 8
HEAD_SIZE = 64
LAYERS = 1
STEP_NUMBER = 10

F32 = jnp.float32
BF16 = jnp.bfloat16
LANES = 128
D = HEADS * HEAD_SIZE
PARTS = 16
ROWS = D // PARTS
QUARTER = PARTS // 4
MIB = 1 << 20

OUT_AT, UP_AT, DOWN_AT, HEAD_AT, LOSS_AT, BUNDLE = 0, 128, 640, 1152, 1184, 1200
CUT = 896
EMBED_AT, FIRST = 384, 416


def dot_nn(a, b):
    return lax.dot_general(a, b, (((1,), (0,)), ((), ())), preferred_element_type=F32)


def dot_nt(a, b):
    return lax.dot_general(a, b, (((1,), (1,)), ((), ())), preferred_element_type=F32)


def dot_tn(a, b):
    return lax.dot_general(a, b, (((0,), (0,)), ((), ())), preferred_element_type=F32)


def offset_of(slot):
    return (slot % 4) * 4 + (slot // 4 % 2) * 2 + slot // 8


def slot_of(offset):
    return (offset & 1) * 8 + ((offset >> 1) & 1) * 4 + (offset >> 2)


def lane_index(shape):
    return lax.broadcasted_iota(jnp.int32, shape, len(shape) - 1)


IN_HBM = pl.BlockSpec(memory_space=pltpu.HBM)
ANYWHERE = pl.BlockSpec(memory_space=pl.ANY)


def ignoring(kernel, reads, ignored):
    def run(*refs):
        kernel(*refs[:reads], *refs[reads + ignored :])

    return run


def params(limit=63, **more):
    return pltpu.CompilerParams(vmem_limit_bytes=limit * MIB, **more)


def cost(flops, moved):
    return pl.CostEstimate(flops=int(flops), bytes_accessed=int(moved), transcendentals=0)


def swapped(block, axis, distance):
    count = lax.axis_size(axis)
    return lax.ppermute(block, axis, [(i, i ^ distance) for i in range(count)])


def sent_along_z(blocks):
    return [swapped(block, "var", 4 * i) for i, block in zip((1, 2, 3), blocks)]


def stacked_kernel(counts, *refs):
    ins, outs, sems = sum(counts), len(counts), refs[-1]
    blocks, results = refs[:ins], refs[ins : ins + outs]
    copies, at = [], 0
    for count, result in zip(counts, results):
        row = 0
        for block in blocks[at : at + count]:
            if len(block.shape) == 2:
                target, height = result.at[row], 1
            else:
                height = block.shape[0]
                target = result.at[pl.ds(row, height)]
            copies.append(pltpu.make_async_copy(block, target, sems.at[len(copies)]))
            row += height
        at += count
    for copy in copies:
        copy.start()
    for copy in copies:
        copy.wait()


def stacked(groups, after=()):
    counts = tuple(len(group) for group in groups)
    blocks = [block for group in groups for block in group]
    shapes = []
    for group in groups:
        rows = sum(1 if block.ndim == 2 else block.shape[0] for block in group)
        shapes.append(jax.ShapeDtypeStruct((rows, *group[0].shape[-2:]), BF16))
    vmem = pl.BlockSpec(memory_space=pltpu.VMEM)
    return pl.pallas_call(
        ignoring(partial(stacked_kernel, counts), len(blocks), len(after)),
        in_specs=[ANYWHERE] * (len(blocks) + len(after)),
        out_specs=[vmem] * len(shapes),
        out_shape=shapes,
        scratch_shapes=[pltpu.SemaphoreType.DMA((len(blocks),))],
        compiler_params=params(6),
        cost_estimate=cost(0, MIB),
        name="stacked",
    )(*blocks, *after)


def summed_kernel(groups, *refs):
    at, to = 0, sum(len(count) for counts, _ in groups for count in counts)
    for counts, parts in groups:
        results = refs[to : to + parts]
        row = 0
        for count in counts:
            height = min(ref.shape[-2] for ref in refs[at : at + len(count)])
            total = None
            for ref, start in zip(refs[at : at + len(count)], count):
                term = ref[..., start : start + height, :].astype(F32)
                total = term if total is None else total + term
            total = total.astype(BF16)
            rows = slice(row, row + total.shape[-2])
            for i, ref in enumerate(results):
                if total.ndim == 2:
                    ref[rows, :] = total
                elif len(ref.shape) == 2:
                    ref[rows, :] = total[i]
                else:
                    each = ref.shape[0]
                    ref[:, rows, :] = total[i * each : (i + 1) * each]
            row += total.shape[-2]
            at += len(count)
        to += parts


def summed(groups, after=()):
    groups = [
        ([[t if isinstance(t, tuple) else (t, 0) for t in terms] for terms in columns], parts)
        for columns, parts in groups
    ]
    counts, shapes = [], []
    for columns, parts in groups:
        counts.append((tuple(tuple(start for _, start in terms) for terms in columns), parts))
        shape = columns[0][0][0].shape
        rows = sum(min(array.shape[-2] for array, _ in terms) for terms in columns)
        lead = () if len(shape) == 2 or shape[0] == parts else (shape[0] // parts,)
        shapes += [jax.ShapeDtypeStruct((*lead, rows, LANES), BF16)] * parts
    arrays = [array for columns, _ in groups for terms in columns for array, _ in terms]
    vmem = pl.BlockSpec(memory_space=pltpu.VMEM)
    return pl.pallas_call(
        ignoring(partial(summed_kernel, tuple(counts)), len(arrays), len(after)),
        in_specs=[vmem] * len(arrays) + [ANYWHERE] * len(after),
        out_specs=[vmem] * len(shapes),
        out_shape=shapes,
        compiler_params=params(12),
        cost_estimate=cost(0, sum(array.size for array in arrays) * 3),
        name="summed",
    )(*arrays, *after)


def far_terms(kept_near, kept_far, near, far):
    return [kept_far, swapped(far, "var", 1)]


def near_terms(quarter, across, start=0):
    kept_near, _, near, _ = quarter
    return [kept_near, swapped(near, "var", 1), (across, start)]


def z_terms(mine, *others):
    return ([[mine, *sent_along_z(others)]], 1)


def with_other(mine):
    return (mine, swapped(mine, "win", 1))


def three_pieces(value):
    high = value.astype(BF16).astype(F32)
    middle = (value - high).astype(BF16).astype(F32)
    return (high, middle, value - high - middle)


def prep_kernel(
    pos_ref, series, target, observed, valid, kept_n, sent_n, kept_t, sent_t, count, total
):
    step = pl.program_id(0)
    half = pl.num_programs(0) // 2
    rows = series[0]
    look, local = rows.shape
    centre = jnp.mean(rows, 0, keepdims=True)
    offset = rows - centre
    spread = jnp.sqrt(jnp.mean(offset * offset, 0, keepdims=True) + 1e-05)
    normed = offset / spread
    mark = valid[...].astype(F32)
    weight = observed[0].astype(F32) * mark

    @pl.when(step == 0)
    def _():
        total[...] = jnp.zeros_like(total)

    total[...] += jnp.sum(jnp.sum(weight, 0, keepdims=True), 1, keepdims=True)
    spare = LANES - look
    row = lax.broadcasted_iota(jnp.int32, (spare, local), 0)
    extra = jnp.where(row == 0, mark, 0.0)
    for i, piece in enumerate(three_pieces(total[0:1, 0:1])):
        extra = jnp.where(row == 1 + i, piece, extra)
    normed = jnp.concatenate([normed, extra], axis=0).T.astype(BF16)
    extra = jnp.where(row == 0, centre, jnp.where(row == 1, spread, 0.0))
    future = jnp.concatenate([target[0], extra], axis=0).T
    weight = jnp.concatenate([weight, jnp.zeros((spare, local), F32)], axis=0).T

    @pl.when(step < half)
    def _():
        kept_n[0] = normed
        kept_t[0, :, 0:LANES] = future
        kept_t[0, :, LANES:] = weight

    @pl.when(step >= half)
    def _():
        sent_n[0] = normed
        sent_t[0, :, 0:LANES] = future
        sent_t[0, :, LANES:] = weight

    count[...] = total[...]


def prep(pos, series, target, observed, valid, after):
    windows, look, local = series.shape
    half = windows // 2

    def source(i, pos_ref):
        return (lax.rem(pos_ref[0] * half + i, windows), 0, 0)

    def kept(i, pos_ref):
        return (jnp.minimum(i, half - 1), 0, 0)

    def sent(i, pos_ref):
        return (jnp.maximum(i - half, 0), 0, 0)

    block = pl.BlockSpec((1, look, local), source)
    out_shape, out_specs = [], []
    for dtype, width in ((BF16, LANES), (F32, 2 * LANES)):
        for index in (kept, sent):
            out_shape.append(jax.ShapeDtypeStruct((half, local, width), dtype))
            out_specs.append(pl.BlockSpec((1, local, width), index))
    return pl.pallas_call(
        ignoring(prep_kernel, 5, len(after)),
        grid_spec=pltpu.PrefetchScalarGridSpec(
            num_scalar_prefetch=1,
            grid=(windows,),
            in_specs=[block, block, block, pl.BlockSpec((1, local), lambda i, p: (0, 0))]
            + [ANYWHERE] * len(after),
            out_specs=out_specs + [pl.BlockSpec((8, LANES), lambda i, p: (0, 0))],
            scratch_shapes=[pltpu.VMEM((8, LANES), F32)],
        ),
        out_shape=out_shape + [jax.ShapeDtypeStruct((8, LANES), F32)],
        compiler_params=params(8),
        cost_estimate=cost(0, 8 * MIB),
        name="prep",
    )(pos, series, target, observed, valid, *after)


def pack_first_kernel(joint, embed, out):
    for c in range(12):
        out[c * ROWS : (c + 1) * ROWS, :] = joint[0, :, c * LANES : (c + 1) * LANES].astype(BF16)
    look = embed.shape[-1]
    out[EMBED_AT:FIRST, 0:look] = embed[...].astype(BF16)
    out[EMBED_AT:FIRST, look:] = jnp.zeros((ROWS, LANES - look), BF16)


def pack_first(joint, embed):
    return pl.pallas_call(
        pack_first_kernel,
        out_shape=jax.ShapeDtypeStruct((FIRST, LANES), BF16),
        compiler_params=params(4),
        cost_estimate=cost(0, MIB // 2),
        name="pack_first",
    )(joint, embed)


def pack_second_kernel(own, came, out_w, up, down, head, norm, one, two):
    for c in range(4):
        one[OUT_AT + c * ROWS : OUT_AT + (c + 1) * ROWS, :] = out_w[
            0, :, c * LANES : (c + 1) * LANES
        ].astype(BF16)
    for c in range(16):
        one[UP_AT + c * ROWS : UP_AT + (c + 1) * ROWS, :] = up[
            0, :, c * LANES : (c + 1) * LANES
        ].astype(BF16)
    for c in range(4):
        two[c * LANES : (c + 1) * LANES, :] = down[0, :, c * LANES : (c + 1) * LANES].astype(BF16)
    horizon = head.shape[-1]
    spare = (ROWS, LANES - horizon)
    lane = lane_index(spare)
    count = own[0:1, 0:1] + jnp.sum(came[0, 0:1, 97:100].astype(F32), 1, keepdims=True)
    square = jnp.concatenate([norm[0], jnp.zeros((LANES - 4, ROWS), F32)], axis=0)
    square = jnp.concatenate([square] * (LANES // ROWS), axis=1).T
    extra = square[0:ROWS, 0 : LANES - horizon]
    for i, piece in enumerate(three_pieces(count)):
        extra = jnp.where(lane == 4 + i, piece, extra)
    two[HEAD_AT - DOWN_AT : LOSS_AT - DOWN_AT, 0:horizon] = head[...].astype(BF16)
    two[HEAD_AT - DOWN_AT : LOSS_AT - DOWN_AT, horizon:] = extra.astype(BF16)
    two[LOSS_AT - DOWN_AT :, :] = jnp.zeros((BUNDLE - LOSS_AT, LANES), BF16)


def pack_second(own, came, out_w, up, down, head, norm, after):
    half = came.shape[0]
    arrays = (own, came, out_w, up, down, head, norm)
    specs = [pl.BlockSpec(a.shape, lambda i, n=a.ndim: (0,) * n) for a in arrays]
    specs[1] = pl.BlockSpec((1, 16, LANES), lambda i: (half - 1, 0, 0))
    shapes = [(DOWN_AT, LANES), (BUNDLE - DOWN_AT, LANES)]
    return pl.pallas_call(
        ignoring(pack_second_kernel, len(arrays), len(after)),
        grid=(1,),
        in_specs=specs + [ANYWHERE] * len(after),
        out_specs=[pl.BlockSpec(shape, lambda i: (0, 0)) for shape in shapes],
        out_shape=[jax.ShapeDtypeStruct(shape, BF16) for shape in shapes],
        compiler_params=params(8),
        cost_estimate=cost(0, 2 * MIB),
        name="pack_second",
    )(*arrays, *after)


def project_kernel(me_ref, g0, g1, kept, came, qkv, hid, joint, embed):
    @pl.when(pl.program_id(0) == 0)
    def _():
        me = me_ref[0]
        for slot in range(PARTS):
            block = (g0, g1)[slot // 8]
            owner = me ^ offset_of(slot)
            for c in range(12):
                joint[owner, :, c * LANES : (c + 1) * LANES] = block[
                    slot % 8, c * ROWS : (c + 1) * ROWS, :
                ]
            embed[owner] = block[slot % 8, EMBED_AT:FIRST, :]

    normed = jnp.concatenate([kept[0], came[0]], axis=0)
    low = dot_nt(embed[...].reshape(D, LANES), normed).astype(BF16)
    hid[...] = low
    for part in range(3):
        weights = joint[:, :, part * D : (part + 1) * D].reshape(D, D)
        rows = dot_tn(weights, low)
        if part == 0:
            rows = rows * 0.18033688011112042
        qkv[part * D : (part + 1) * D, :] = rows.astype(BF16)


def project(me, bundle, kept, came):
    half, local, _ = kept.shape
    slots = 2 * local
    whole = pl.BlockSpec((8, FIRST, LANES), lambda w, m: (0, 0, 0))
    mine = pl.BlockSpec((1, local, LANES), lambda w, m: (w, 0, 0))
    return pl.pallas_call(
        project_kernel,
        grid_spec=pltpu.PrefetchScalarGridSpec(
            num_scalar_prefetch=1,
            grid=(half,),
            in_specs=[whole] * 2 + [mine] * 2,
            out_specs=[
                pl.BlockSpec((3 * D, slots), lambda w, m: (0, w)),
                pl.BlockSpec((D, slots), lambda w, m: (0, w)),
                pl.BlockSpec((PARTS, ROWS, 3 * D), lambda w, m: (0, 0, 0)),
                pl.BlockSpec((PARTS, ROWS, LANES), lambda w, m: (0, 0, 0)),
            ],
        ),
        out_shape=[
            jax.ShapeDtypeStruct((3 * D, half * slots), BF16),
            jax.ShapeDtypeStruct((D, half * slots), BF16),
            jax.ShapeDtypeStruct((PARTS, ROWS, 3 * D), BF16),
            jax.ShapeDtypeStruct((PARTS, ROWS, LANES), BF16),
        ],
        compiler_params=params(18),
        cost_estimate=cost(1e6, 1000),
        name="project",
    )(me, *bundle, kept, came)


def tiles_of(length, size):
    return [(at, min(size, length - at)) for at in range(0, length, size)]


PAIR = 2


def head_rows(i):
    return slice(i * HEAD_SIZE, (i + 1) * HEAD_SIZE)


def attend_kernel(kept, came, q, k, v, weights, mixed, scale, bias):
    slots = q.shape[1]
    local = slots // 2

    @pl.when((pl.program_id(0) == 0) & (pl.program_id(1) == 0))
    def _():
        for part, marks in enumerate((kept, came)):
            rows = slice(part * local, (part + 1) * local)
            mark = marks[0, :, 96:97].astype(F32)
            key = part * local + lax.broadcasted_iota(jnp.int32, (local, slots), 0)
            query = lane_index((local, slots))
            bias[rows, :] = jnp.where((mark > 0.5) | (key == query), 0.0, -1e30)

    def score_of(i):
        return dot_tn(k[head_rows(i), :], q[head_rows(i), :]) + bias[...]

    def weigh(i, score):
        weight = jnp.exp2(score - jnp.max(score, 0, keepdims=True))
        low = weight.astype(BF16)
        weights[i] = low
        return (low, jnp.sum(weight, 0, keepdims=True))

    def mix(i, low, total):
        inverse = 1.0 / total
        scale[i] = inverse
        mixed[head_rows(i), :] = (dot_nn(v[head_rows(i), :], low) * inverse).astype(BF16)

    score = score_of(0)
    pending = None
    for i in range(PAIR):
        coming = score_of(i + 1) if i + 1 < PAIR else None
        weighed = weigh(i, score)
        if pending is not None:
            mix(*pending)
        pending = (i, *weighed)
        score = coming
    mix(*pending)


def attend(first, count, kept, came, qkv, after=(), held=()):
    half, local, _ = kept.shape
    slots = 2 * local
    marks = pl.BlockSpec((1, local, LANES), lambda h, w: (0, 0, 0))

    def heads(part):
        return pl.BlockSpec(
            (PAIR * HEAD_SIZE, slots), lambda h, w: ((part * HEADS + first) // PAIR + h, w)
        )

    return pl.pallas_call(
        ignoring(attend_kernel, 5, len(held) + len(after)),
        grid=(count // PAIR, half),
        in_specs=[marks, marks, heads(0), heads(1), heads(2)] + [ANYWHERE] * (len(held) + len(after)),
        out_specs=[
            pl.BlockSpec(
                (PAIR, slots, slots), lambda h, w: ((first // PAIR + h) * half + w, 0, 0)
            ),
            pl.BlockSpec((PAIR * HEAD_SIZE, slots), lambda h, w: (h, w)),
            pl.BlockSpec((PAIR, 1, slots), lambda h, w: (h * half + w, 0, 0)),
        ],
        out_shape=[
            jax.ShapeDtypeStruct((HEADS * half, slots, slots), BF16),
            jax.ShapeDtypeStruct((count * HEAD_SIZE, half * slots), BF16),
            jax.ShapeDtypeStruct((count * half, 1, slots), F32),
        ],
        scratch_shapes=[pltpu.VMEM((slots, slots), F32)],
        compiler_params=params(39),
        cost_estimate=cost(count * half * 2e9, count * half * 2 * MIB),
        name="attend",
        input_output_aliases={5 + i: i for i in range(len(held))},
    )(kept, came, qkv, qkv, qkv, *held, *after)


def unattend_kernel(
    me_ref, weights, scale, mixed, dmixed, q, k, v, hid, dproj, *refs
):
    targets, (rows, packed, sems) = refs[:4], refs[4:]
    head, window = pl.program_id(0), pl.program_id(1)
    slots = q.shape[1]

    def prepared(i):
        low = (dmixed[head_rows(i), :].astype(F32) * scale[i]).astype(BF16)
        share = low.astype(F32) * mixed[head_rows(i), :].astype(F32)
        return (low, jnp.sum(share, 0, keepdims=True))

    def dweight_of(i, low, delta):
        return dot_tn(v[head_rows(i), :], low) - delta

    ready = [prepared(i) for i in range(PAIR)]
    dweight = dweight_of(0, *ready[0])
    for i in range(PAIR):
        coming = dweight_of(i + 1, *ready[i + 1]) if i + 1 < PAIR else None
        dscore = (weights[i].astype(F32) * dweight).astype(BF16)
        dquery = dot_nn(k[head_rows(i), :], dscore) * 0.125
        dkey = dot_nt(q[head_rows(i), :], dscore) * 0.6931471805599453
        dvalue = dot_nt(ready[i][0], weights[i])
        for part, grad in enumerate((dquery, dkey, dvalue)):
            dproj[part, head_rows(i), :] = grad.astype(BF16)
        dweight = coming
    start = pl.multiple_of(window * slots, LANES)
    for part in range(3):
        rows[part, head, :, pl.ds(start, slots)] = dproj[part]

    count = pl.num_programs(0)

    @pl.when((head == count - 1) & (window == pl.num_programs(1) - 1))
    def _():
        me = me_ref[0]
        width = rows.shape[1] * rows.shape[2]
        for part in range(3):
            grad = dot_nt(hid[...], rows[part].reshape(width, rows.shape[-1])).astype(BF16)
            for b in range(PARTS):
                slot = slot_of(b ^ me)
                for c in range(width // LANES):
                    at = (part * (width // LANES) + c) * ROWS
                    packed[slot, at : at + ROWS, :] = grad[
                        b * ROWS : (b + 1) * ROWS, c * LANES : (c + 1) * LANES
                    ]
        send_packed(packed, targets, sems)


def send_packed(packed, targets, sems, rows=None):
    start, height = rows or (0, packed.shape[1])
    copies = [
        pltpu.make_async_copy(
            packed.at[pl.ds(i * QUARTER, QUARTER), pl.ds(start, height)], target, sems.at[i]
        )
        for i, target in enumerate(targets)
    ]
    for copy in copies:
        copy.start()
    for copy in copies:
        copy.wait()


def quarters(height):
    return [jax.ShapeDtypeStruct((QUARTER, height, LANES), BF16)] * 4


def unattend(me, first, count, weights, scale, mixed, dmixed, qkv, hid, after=()):
    slots = weights.shape[-1]
    tokens = qkv.shape[1]
    half = tokens // slots
    height = 3 * count * HEAD_SIZE // LANES * ROWS
    lead = first // PAIR

    def heads(part):
        return pl.BlockSpec(
            (PAIR * HEAD_SIZE, slots), lambda h, w, m: (part * HEADS // PAIR + lead + h, w)
        )

    return pl.pallas_call(
        ignoring(unattend_kernel, 9, len(after)),
        grid_spec=pltpu.PrefetchScalarGridSpec(
            num_scalar_prefetch=1,
            grid=(count // PAIR, half),
            in_specs=[
                pl.BlockSpec(
                    (PAIR, slots, slots), lambda h, w, m: ((lead + h) * half + w, 0, 0)
                ),
                pl.BlockSpec((PAIR, 1, slots), lambda h, w, m: (h * half + w, 0, 0)),
                pl.BlockSpec((PAIR * HEAD_SIZE, slots), lambda h, w, m: (h, w)),
                pl.BlockSpec((PAIR * HEAD_SIZE, slots), lambda h, w, m: (lead + h, w)),
                heads(0),
                heads(1),
                heads(2),
                pl.BlockSpec((D, tokens), lambda h, w, m: (0, 0)),
            ]
            + [ANYWHERE] * len(after),
            out_specs=[
                pl.BlockSpec((3, PAIR * HEAD_SIZE, slots), lambda h, w, m: (0, h, w)),
                *[ANYWHERE] * 4,
            ],
            scratch_shapes=[
                pltpu.VMEM((3, count // PAIR, PAIR * HEAD_SIZE, tokens), BF16),
                pltpu.VMEM((PARTS, height, LANES), BF16),
                pltpu.SemaphoreType.DMA((4,)),
            ],
        ),
        out_shape=[
            jax.ShapeDtypeStruct((3, count * HEAD_SIZE, tokens), BF16),
            *quarters(height),
        ],
        compiler_params=params(39),
        cost_estimate=cost(count * half * 2.8e9, count * half * 2 * MIB),
        name="unattend",
    )(me, weights, scale, mixed, dmixed, qkv, qkv, qkv, hid, *after)


def gelu_parts(pre):
    phi = 0.5 + 0.5 * lax.erf(pre * 0.7071067811865476)
    bell = jnp.exp2(pre * pre * -0.7213475204444817)
    return (pre * phi, phi + pre * (bell * 0.3989422804014327))


def norm_forward(resid, gain, shift):
    centre = jnp.mean(resid, 0, keepdims=True)
    offset = resid - centre
    inverse = lax.rsqrt(jnp.mean(offset * offset, 0, keepdims=True) + 1e-05)
    unit = offset * inverse
    return (unit * gain + shift, unit, inverse)


def norm_backward(grad, unit, inverse, gain):
    scaled = grad * gain
    first = jnp.mean(scaled, 0, keepdims=True)
    second = jnp.mean(scaled * unit, 0, keepdims=True)
    return (scaled - first - unit * second) * inverse


def wide(block, size):
    return jnp.concatenate([block] * (size // LANES), axis=1)


def folded(block):
    total = block[:, 0:LANES]
    for at in range(LANES, block.shape[1], LANES):
        total = total + block[:, at : at + LANES]
    return total


def middle_kernel(
    me_ref,
    a0,
    a1,
    b0,
    b1,
    *refs,
):
    fetched, (dmixed_out, dattn_out), refs = refs[:7], refs[7:9], refs[9:]
    spaces, (dmixed, dattn), refs = refs[-8:-3], refs[-3:-1], (*refs[:-8], refs[-1])
    embed, normed, future, mixed_a, mixed_b = spaces
    windows, local, _ = fetched[1].shape
    moves = [(fetched[0], embed), (fetched[5], mixed_a), (fetched[6], mixed_b)]
    for window in range(windows):
        for side in range(2):
            rows = pl.ds((2 * window + side) * local, local)
            moves.append((fetched[1 + side].at[window], normed.at[rows]))
            moves.append((fetched[3 + side].at[window], future.at[rows]))
    arrivals = [
        pltpu.make_async_copy(array, space, refs[-1].at[i])
        for i, (array, space) in enumerate(moves)
    ]
    for arrival in arrivals:
        arrival.start()
    results = [
        pltpu.make_async_copy(space, array, refs[-1].at[len(arrivals) + i])
        for i, (space, array) in enumerate(((dmixed, dmixed_out), (dattn, dattn_out)))
    ]
    middle_body(me_ref, a0, a1, b0, b1, *spaces, dmixed, dattn, *refs[:-1], arrivals, results)


def middle_body(
    me_ref,
    a0,
    a1,
    b0,
    b1,
    embed,
    normed,
    future,
    mixed_a,
    mixed_b,
    dmixed,
    dattn,
    counted,
    kept_near_a,
    kept_far_a,
    near_a,
    far_a,
    kept_near_b,
    kept_far_b,
    near_b,
    far_b,
    w_out,
    w_up,
    w_down,
    w_head,
    t_out,
    t_up,
    t_down,
    norms,
    middle_s,
    active_s,
    dbranch_s,
    dpre_s,
    final_s,
    dguess_s,
    norm_sums,
    loss_sum,
    packed,
    sems,
    arrivals,
    results,
):
    ff = active_s.shape[0]
    chunks = ff // D
    me = me_ref[0]
    tokens = normed.shape[0]

    def set_up():
        copies = [
            pltpu.make_async_copy(
                block, packed.at[pl.ds(i % 2 * 8, 8), pl.ds(at, block.shape[1])], sems.at[i]
            )
            for i, (at, block) in enumerate(((0, a0), (0, a1), (DOWN_AT, b0), (DOWN_AT, b1)))
        ]
        for copy in copies:
            copy.start()
        for copy in copies:
            copy.wait()
        total = jnp.zeros((1, 1), F32)
        for slot in range(PARTS):
            owner = me ^ offset_of(slot)
            for c in range(4):
                cols = slice(c * LANES, (c + 1) * LANES)
                at = OUT_AT + c * ROWS
                w_out[owner, :, cols] = packed[slot, at : at + ROWS, :]
                at = DOWN_AT + c * LANES
                w_down[owner, :, cols] = packed[slot, at : at + LANES, :]
            for c in range(16):
                at = UP_AT + c * ROWS
                w_up[owner, :, c * LANES : (c + 1) * LANES] = packed[slot, at : at + ROWS, :]
            head = packed[slot, HEAD_AT:LOSS_AT, :]
            w_head[owner] = head
            pieces = head[0:1, 100:103].astype(F32)
            total = total + jnp.sum(pieces, 1, keepdims=True)
        counted[...] = jnp.broadcast_to(jnp.maximum(total, 1.0), counted.shape)
        t_out[...] = w_out[...].reshape(D, D).T
        for c in range(chunks):
            rows = slice(c * D, (c + 1) * D)
            t_up[rows, :] = w_up[:, :, rows].reshape(D, D).T
            t_down[:, rows] = w_down[c * 4 : (c + 1) * 4].reshape(D, D).T
        extra = w_head[...].reshape(D, LANES)
        for i in range(4):
            column = extra[:, 96 + i : 97 + i].astype(F32)
            norms[i] = jnp.broadcast_to(column, (D, LANES))
        norm_sums[...] = jnp.zeros_like(norm_sums)
        loss_sum[...] = jnp.zeros_like(loss_sum)

    set_up()
    for arrival in arrivals:
        arrival.wait()
    tiles = [
        middle_tile(
            at,
            min(MIDDLE_SIZE, tokens - at),
            *(normed, future, embed, mixed_a, mixed_b, dmixed, dattn, counted),
            *(w_out, w_up, w_down, w_head, t_out, t_up, t_down, norms),
            *(middle_s, active_s, dbranch_s, dpre_s, final_s, dguess_s, norm_sums, loss_sum),
        )
        for at in range(0, tokens, MIDDLE_SIZE)
    ]
    in_turn(tiles, LAG)
    for result in results:
        result.start()

    def place(grad, first_row, blocks, base):
        height = grad.shape[0] // blocks
        for b in range(blocks):
            slot = slot_of((first_row + b) ^ me)
            for c in range(grad.shape[1] // LANES):
                at = base + c * height
                packed[slot, at : at + height, :] = grad[
                    b * height : (b + 1) * height, c * LANES : (c + 1) * LANES
                ]

    for c in range(chunks):
        rows = slice(c * D, (c + 1) * D)
        place(dot_nt(active_s[rows, :], dbranch_s[...]).astype(BF16), c * 4, 4, DOWN_AT)
        place(
            dot_nt(middle_s[...], dpre_s[rows, :]).astype(BF16),
            0,
            PARTS,
            UP_AT + c * (D // LANES) * ROWS,
        )
    for i, side in enumerate((mixed_a, mixed_b)):
        grad = dot_nt(side[...], dattn[...]).astype(BF16)
        place(grad, i * (PARTS // 2), PARTS // 2, OUT_AT)
    head = dot_nn(final_s[...], dguess_s[...])
    lane = lane_index(head.shape)
    for i in range(4):
        head = jnp.where(lane == 96 + i, jnp.sum(norm_sums[i], 1, keepdims=True), head)
    place(head.astype(BF16), 0, PARTS, HEAD_AT)
    row = lax.broadcasted_iota(jnp.int32, (BUNDLE - LOSS_AT, LANES), 0)
    losses = jnp.where(row == 0, loss_sum[...], 0.0).astype(BF16)
    for slot in range(PARTS):
        packed[slot, LOSS_AT:BUNDLE, :] = losses
    send_packed(packed, (kept_near_a, kept_far_a, near_a, far_a), sems, (0, CUT))
    send_packed(packed, (kept_near_b, kept_far_b, near_b, far_b), sems, (CUT, BUNDLE - CUT))
    for result in results:
        result.wait()


def in_turn(streams, lag):
    waiting = [lag * i for i in range(len(streams))]
    live = [True] * len(streams)
    while any(live):
        for i, stream in enumerate(streams):
            if waiting[i] > 0:
                waiting[i] -= 1
            elif live[i]:
                live[i] = next(stream, stream) is not stream


def middle_tile(
    at,
    size,
    normed,
    future,
    embed,
    mixed_a,
    mixed_b,
    dmixed,
    dattn,
    counted,
    w_out,
    w_up,
    w_down,
    w_head,
    t_out,
    t_up,
    t_down,
    norms,
    middle_s,
    active_s,
    dbranch_s,
    dpre_s,
    final_s,
    dguess_s,
    norm_sums,
    loss_sum,
):
    ff = active_s.shape[0]
    height = FF_ROWS
    cols = slice(at, at + size)
    mixed = jnp.concatenate([mixed_a[:, cols], mixed_b[:, cols]], axis=0)
    resid = dot_nt(embed[...].reshape(D, LANES), normed[cols, :]) + dot_nn(t_out[...], mixed)
    yield
    gain_one, gain_two = wide(norms[0], size), wide(norms[2], size)
    middle, unit_one, inverse_one = norm_forward(resid, gain_one, wide(norms[1], size))
    middle_low = middle.astype(BF16)
    middle_s[:, cols] = middle_low
    yield
    for row in range(0, ff, height):
        rows = slice(row, row + height)
        active, gradient = gelu_parts(dot_nn(t_up[rows, :], middle_low))
        active_s[rows, cols] = active.astype(BF16)
        dpre_s[rows, cols] = gradient.astype(BF16)
        yield
    yield
    resid = middle + dot_nn(t_down[...], active_s[:, cols])
    yield
    final, unit_two, inverse_two = norm_forward(resid, gain_two, wide(norms[3], size))
    final_low = final.astype(BF16)
    final_s[:, cols] = final_low
    w_h = w_head[...].reshape(D, LANES)
    yield
    guess = dot_tn(final_low, w_h)
    yield
    ahead = future[cols, 0:LANES]
    weighting = future[cols, LANES:]
    centre = future[cols, 96:97]
    spread = future[cols, 97:98]
    error = guess * spread + centre - ahead
    loss_sum[...] += jnp.sum(weighting * error * error, 0, keepdims=True)
    dguess = (2.0 * weighting * error / counted[0:1, 0:1] * spread).astype(BF16)
    dguess_s[cols, :] = dguess
    yield
    dfinal = dot_nt(w_h, dguess)
    yield
    norm_sums[2] += folded(dfinal * unit_two)
    norm_sums[3] += folded(dfinal)
    dresid = norm_backward(dfinal, unit_two, inverse_two, gain_two)
    dbranch = dresid.astype(BF16)
    dbranch_s[:, cols] = dbranch
    yield
    w_d = w_down[...].reshape(ff, D)
    for row in range(0, ff, height):
        rows = slice(row, row + height)
        dpre = (dot_nn(w_d[rows], dbranch) * dpre_s[rows, cols].astype(F32)).astype(BF16)
        dpre_s[rows, cols] = dpre
        yield
    yield
    dresid = dresid + dot_nn(w_up[...].reshape(D, ff), dpre_s[:, cols])
    yield
    norm_sums[0] += folded(dresid * unit_one)
    norm_sums[1] += folded(dresid)
    dfirst = norm_backward(dresid, unit_one, inverse_one, gain_one).astype(BF16)
    dattn[:, cols] = dfirst
    yield
    dmixed[:, cols] = dot_nn(w_out[...].reshape(D, D), dfirst).astype(BF16)


LAG = 2
MIDDLE_SIZE = 896
FF_ROWS = 512


def middle_pass(me, bundle, embed, kept, came, mixed, ff):
    tokens = mixed[0].shape[1]
    fetched = (embed, kept[0], came[0], kept[1], came[1], *mixed)
    vmem = pl.BlockSpec(memory_space=pltpu.VMEM)
    return pl.pallas_call(
        middle_kernel,
        in_specs=[pl.BlockSpec(memory_space=pltpu.SMEM)] + [ANYWHERE] * 4 + [IN_HBM] * 7,
        out_specs=[IN_HBM, IN_HBM, vmem] + [IN_HBM] * 8,
        scratch_shapes=[
            pltpu.VMEM((PARTS, ROWS, D), BF16),
            pltpu.VMEM((PARTS, ROWS, ff), BF16),
            pltpu.VMEM((PARTS, ff // PARTS, D), BF16),
            pltpu.VMEM((PARTS, ROWS, LANES), BF16),
            pltpu.VMEM((D, D), BF16),
            pltpu.VMEM((ff, D), BF16),
            pltpu.VMEM((D, ff), BF16),
            pltpu.VMEM((4, D, LANES), F32),
            pltpu.VMEM((D, tokens), BF16),
            pltpu.VMEM((ff, tokens), BF16),
            pltpu.VMEM((D, tokens), BF16),
            pltpu.VMEM((ff, tokens), BF16),
            pltpu.VMEM((D, tokens), BF16),
            pltpu.VMEM((tokens, LANES), BF16),
            pltpu.VMEM((4, D, LANES), F32),
            pltpu.VMEM((1, LANES), F32),
            pltpu.VMEM((PARTS, BUNDLE, LANES), BF16),
            pltpu.SemaphoreType.DMA((4,)),
        ]
        + [
            pltpu.VMEM(embed.shape, BF16),
            pltpu.VMEM((tokens, LANES), BF16),
            pltpu.VMEM((tokens, 2 * LANES), F32),
        ]
        + [pltpu.VMEM((D // 2, tokens), BF16)] * 2
        + [pltpu.VMEM((D, tokens), BF16)] * 2
        + [pltpu.SemaphoreType.DMA((5 + 4 * kept[0].shape[0],))],
        out_shape=[
            jax.ShapeDtypeStruct((D, tokens), BF16),
            jax.ShapeDtypeStruct((D, tokens), BF16),
            jax.ShapeDtypeStruct((8, LANES), F32),
            *quarters(CUT),
            *quarters(BUNDLE - CUT),
        ],
        compiler_params=params(57),
        cost_estimate=cost(35e9, 20 * MIB),
        name="middle",
    )(me, *bundle, *fetched)


def last_kernel(
    me_ref, joint, dproj_a, dproj_b, dattn, kept_n, came_n, *refs
):
    riders, targets, scratch = refs[:4], refs[4:8], refs[8:]
    joint_s, dproj_s, dattn_s, normed, packed, sems = scratch
    me = me_ref[0]
    windows, local, _ = kept_n.shape
    slots = 2 * local
    rows = riders[0].shape[1]
    copies = [pltpu.make_async_copy(joint, joint_s, sems.at[0])]
    for w in range(windows):
        cols = pl.ds(w * slots, slots)
        for source, target in (
            (dproj_a.at[:, :, cols], dproj_s.at[w, :, pl.ds(0, D // 2)]),
            (dproj_b.at[:, :, cols], dproj_s.at[w, :, pl.ds(D // 2, D // 2)]),
            (dattn.at[:, cols], dattn_s.at[w]),
            (kept_n.at[w], normed.at[w, pl.ds(0, local)]),
            (came_n.at[w], normed.at[w, pl.ds(local, local)]),
        ):
            copies.append(pltpu.make_async_copy(source, target, sems.at[len(copies)]))
    per_window = (len(copies) - 1) // windows
    for i, side in enumerate(riders):
        target = packed.at[pl.ds(i * QUARTER, QUARTER), pl.ds(0, rows)]
        copies.append(pltpu.make_async_copy(side, target, sems.at[len(copies)]))
    for copy in copies:
        copy.start()
    copies[0].wait()
    total = jnp.zeros((D, LANES), F32)
    for w in range(windows):
        for copy in copies[1 + w * per_window : 1 + (w + 1) * per_window]:
            copy.wait()
        dhidden = dattn_s[w].astype(F32)
        for part in range(3):
            weights = joint_s[:, :, part * D : (part + 1) * D].reshape(D, D)
            dhidden = dhidden + dot_nn(weights, dproj_s[w, part])
        total = total + dot_nn(dhidden.astype(BF16), normed[w])
    total = total.astype(BF16)
    for b in range(PARTS):
        packed[slot_of(b ^ me), rows : rows + ROWS, :] = total[b * ROWS : (b + 1) * ROWS, :]
    for copy in copies[-4:]:
        copy.wait()
    send_packed(packed, targets, sems)


def last_pass(me, joint, dprojs, dattn, kept, came, riders, after=()):
    windows, local, _ = kept.shape
    slots = 2 * local
    height = riders[0].shape[1] + ROWS
    return pl.pallas_call(
        ignoring(last_kernel, 11, len(after)),
        in_specs=[pl.BlockSpec(memory_space=pltpu.SMEM)]
        + [IN_HBM] * 10
        + [ANYWHERE] * len(after),
        out_specs=[ANYWHERE] * 4,
        out_shape=quarters(height),
        scratch_shapes=[
            pltpu.VMEM((PARTS, ROWS, 3 * D), BF16),
            pltpu.VMEM((windows, 3, D, slots), BF16),
            pltpu.VMEM((windows, D, slots), BF16),
            pltpu.VMEM((windows, slots, LANES), BF16),
            pltpu.VMEM((PARTS, height, LANES), BF16),
            pltpu.SemaphoreType.DMA((5 + 5 * windows,)),
        ],
        compiler_params=params(22),
        cost_estimate=cost(10e9, 10 * MIB),
        name="last",
    )(me, joint, *dprojs, dattn, kept, came, *riders, *after)


def adamw(weight, mean, square, grad, count_step):
    mean_next = 0.9 * mean + 0.1 * grad
    square_next = 0.999 * square + 0.001 * grad * grad
    mean_hat = mean_next / (1.0 - 0.9**count_step)
    square_hat = square_next / (1.0 - 0.999**count_step)
    weight_next = weight - 0.1 * (mean_hat / (jnp.sqrt(square_hat) + 1e-08) + 0.1 * weight)
    return (weight_next, mean_next, square_next)


def step_second_kernel(mine_a, other_a, mine_b, other_b, counted, *refs):
    held, results = refs[:15], refs[15:]
    grad = mine_a[...].astype(F32) + other_a[...].astype(F32)
    rest = mine_b[...].astype(F32) + other_b[...].astype(F32)

    def grad_rows(at, height):
        return grad[at : at + height] if at < CUT else rest[at - CUT : at - CUT + height]

    def update(which, at, value):
        states = [held[which * 3 + j] for j in range(3)]
        news = adamw(*[state[at] for state in states], value, float(STEP_NUMBER))
        for j in range(3):
            results[which * 3 + j][at] = news[j]

    def block(c):
        return slice(c * LANES, (c + 1) * LANES)

    for c in range(4):
        base = OUT_AT + c * ROWS
        update(0, (0, slice(None), block(c)), grad[base : base + ROWS])
    for c in range(16):
        base = UP_AT + c * ROWS
        update(1, (0, slice(None), block(c)), grad[base : base + ROWS])
    for c in range(4):
        update(2, (0, slice(None), block(c)), grad_rows(DOWN_AT + c * LANES, LANES))
    horizon = held[9].shape[-1]
    head = grad_rows(HEAD_AT, ROWS)
    update(3, (slice(None), slice(None)), head[:, 0:horizon])
    norm = jnp.concatenate([head] * (LANES // ROWS), axis=0).T[96:100, 0:ROWS]
    update(4, (0, slice(None), slice(None)), norm)
    results[15][0] = norm
    losses = jnp.sum(grad_rows(LOSS_AT, 1), 1, keepdims=True)
    results[16][...] = losses / counted[0:1, 0:1]


def step_second(pair_a, pair_b, counted, states):
    shapes = [jax.ShapeDtypeStruct(a.shape, F32) for a in states]
    return pl.pallas_call(
        step_second_kernel,
        out_shape=shapes
        + [jax.ShapeDtypeStruct(states[12].shape, F32), jax.ShapeDtypeStruct((1, 1), F32)],
        compiler_params=params(20),
        cost_estimate=cost(0, 5 * MIB),
        name="step_second",
    )(*pair_a, *pair_b, counted, *states)


def step_first_kernel(mine_a, other_a, mine_b, other_b, *refs):
    held, results = refs[:6], refs[6:]
    halves = [
        mine_a[BUNDLE - CUT :, :].astype(F32) + other_a[BUNDLE - CUT :, :].astype(F32),
        mine_b[...].astype(F32) + other_b[...].astype(F32),
    ]

    def update(which, at, value):
        states = [held[which * 3 + j] for j in range(3)]
        news = adamw(*[state[at] for state in states], value, float(STEP_NUMBER))
        for j in range(3):
            results[which * 3 + j][at] = news[j]

    for part in range(3):
        for side in range(2):
            for c in range(2):
                at = (part * 2 + c) * ROWS
                start = part * D + side * (D // 2) + c * LANES
                update(0, (0, slice(None), slice(start, start + LANES)), halves[side][at : at + ROWS])
    look = held[3].shape[-1]
    update(1, (slice(None), slice(None)), halves[1][6 * ROWS : 7 * ROWS, 0:look])


def step_first(pair_a, pair_b, states):
    shapes = [jax.ShapeDtypeStruct(a.shape, F32) for a in states]
    return pl.pallas_call(
        step_first_kernel,
        out_shape=shapes,
        compiler_params=params(12),
        cost_estimate=cost(0, 2 * MIB),
        name="step_first",
    )(*pair_a, *pair_b, *states)


def whole_windows_body(
    series,
    target,
    valid_slots,
    observed,
    embed_weight,
    joint_proj,
    out_proj,
    up_proj,
    down_proj,
    head_weight,
    norm_params,
    embed_mean,
    joint_mean,
    out_mean,
    up_mean,
    down_mean,
    head_mean,
    norm_mean,
    embed_square,
    joint_square,
    out_square,
    up_square,
    down_square,
    head_square,
    norm_square,
):
    me = lax.axis_index("var").astype(jnp.int32).reshape(1)
    pos = lax.axis_index("win").astype(jnp.int32).reshape(1)
    ff = up_proj.shape[-1]
    packed = pack_first(joint_proj, embed_weight.T)
    row = sent_along_z([packed] * 3)
    turned = [array.transpose(0, 2, 1) for array in (series, target, observed)]
    prepared = prep(pos, *turned, valid_slots.reshape(1, -1), [packed])
    own = prepared[4]
    kept, came = prepared[0:4:2], [swapped(sent, "win", 1) for sent in prepared[1:4:2]]
    (plane,) = stacked([[packed, *row]], [prepared[0]])
    bundles = pack_second(
        own, came[0], out_proj, up_proj, down_proj, head_weight, norm_params, [plane]
    )
    (held,) = stacked([[plane, swapped(plane, "var", 2)]], [bundles[0]])
    qkv, hid, joint, embed = project(me, (held, swapped(held, "var", 1)), kept[0], came[0])
    count = HEADS // 2
    plane_a, bundle_b = stacked(
        [[bundles[0], *sent_along_z([bundles[0]] * 3)], [bundles[1]]], [qkv]
    )
    bundle_b = bundle_b[0]
    sides = [attend(0, count, kept[0], came[0], qkv, [plane_a, came[1]])]
    held_a, plane_b = stacked(
        [
            [plane_a, swapped(plane_a, "var", 2)],
            [bundle_b, *sent_along_z([bundle_b] * 3)],
        ],
        [sides[0][1]],
    )
    sides.append(attend(count, count, kept[0], came[0], qkv, [plane_b], [sides[0][0]]))
    (held_b,) = stacked([[plane_b, swapped(plane_b, "var", 2)]], [sides[1][1]])
    dmixed, dattn, counted, *grads = middle_pass(
        me,
        [held_a, swapped(held_a, "var", 1), held_b, swapped(held_b, "var", 1)],
        embed,
        kept,
        came,
        [side[1] for side in sides],
        ff,
    )

    def back(side, after):
        _, mixed, scale = sides[side]
        weights = sides[1][0]
        return unattend(me, side * count, count, weights, scale, mixed, dmixed, qkv, hid, after)

    part_a, part_b = grads[:4], grads[4:]
    far_a = summed([([far_terms(*part_a)], 1)])
    dproj_a, *joint_a = back(0, far_a)
    *y_a, far_b = summed(
        [
            ([near_terms(part_a, swapped(far_a[0], "var", 2))], QUARTER),
            ([far_terms(*part_b), far_terms(*joint_a)], 1),
        ],
        [dproj_a],
    )
    dproj_b, *joint_b = back(1, [far_b])
    across = swapped(far_b, "var", 2)
    both = [near_terms(part_b, across), near_terms(joint_a, across, BUNDLE - CUT)]
    mine_a, *y_b = summed([z_terms(*y_a), (both, QUARTER)], [dproj_b])
    rest = last_pass(me, joint, [dproj_a, dproj_b], dattn, kept[0], came[0], joint_b, [mine_a])
    pair_a = with_other(mine_a)
    mine_b, onward = summed([z_terms(*y_b), ([[rest[3]]], 1)], [pair_a[1]])
    pair_b = with_other(mine_b)
    (far,) = summed([([far_terms(*rest[:3], onward)], 1)])
    rest = summed([([near_terms(rest, swapped(far, "var", 2))], QUARTER)])
    states = []
    for group in (
        (out_proj, out_mean, out_square),
        (up_proj, up_mean, up_square),
        (down_proj, down_mean, down_square),
        (head_weight, head_mean, head_square),
        (norm_params, norm_mean, norm_square),
    ):
        states.extend(group)
    new = step_second(pair_a, pair_b, counted, states)
    first_b = with_other(summed([z_terms(*rest)], [new[16]])[0])
    fresh = step_first(
        pair_b,
        first_b,
        [joint_proj, joint_mean, joint_square, embed_weight.T, embed_mean.T, embed_square.T],
    )
    outs, ups, downs, heads, norms = [new[3 * i : 3 * i + 3] for i in range(5)]
    embeds = [e.T for e in fresh[3:6]]
    return (
        new[16].reshape(1),
        embeds[0],
        fresh[0],
        outs[0],
        ups[0],
        downs[0],
        heads[0],
        new[15],
        embeds[1],
        fresh[1],
        outs[1],
        ups[1],
        downs[1],
        heads[1],
        norms[1],
        embeds[2],
        fresh[2],
        outs[2],
        ups[2],
        downs[2],
        heads[2],
        norms[2],
    )


def passed_along(block, axis, distance):
    devices = range(lax.axis_size(axis))
    route = [((i - distance) % len(devices), i) for i in devices]
    return lax.ppermute(block, axis, route)


def layer_norm(resid, gain, shift):
    centre = jnp.mean(resid, -1, keepdims=True)
    offset = resid - centre
    spread = jnp.mean(offset * offset, -1, keepdims=True)
    return offset * lax.rsqrt(spread + 1e-05) * gain + shift


def to_items(matrix, windows, local, parts):
    shaped = matrix.reshape(windows, local, parts, HEADS, HEAD_SIZE).transpose(0, 3, 1, 2, 4)
    return shaped.reshape(windows * HEADS, local, parts * HEAD_SIZE)


def from_items(items, windows, local, parts):
    shaped = items.reshape(windows, HEADS, local, parts, HEAD_SIZE).transpose(0, 2, 3, 1, 4)
    return shaped.reshape(windows * local, parts * HEADS * HEAD_SIZE)


def masked_scores(query_rows, key_portion, markers, query_pos, key_pos):
    score_matrix = (
        jnp.einsum("acn,azn->acz", query_rows, key_portion, preferred_element_type=jnp.float32)
        * 0.125
    )
    allowed = (markers[None, :] > 0.5) | (query_pos[:, None] == key_pos[None, :])
    return jnp.where(allowed[None], score_matrix, -1e30)


def absorb(state, query_rows, paired_keys, markers, query_pos, key_pos):
    peak, totals, accum = state
    score_matrix = masked_scores(
        query_rows, paired_keys[..., :HEAD_SIZE], markers, query_pos, key_pos
    )
    top_new = jnp.maximum(peak, jnp.max(score_matrix, -1))
    rescale = jnp.exp(peak - top_new)
    weights = jnp.exp(score_matrix - top_new[..., None])
    totals = totals * rescale + jnp.sum(weights, -1)
    reduced_weights = weights.astype(jnp.bfloat16)
    accum = accum * rescale[..., None] + jnp.einsum(
        "zsx,zxj->zsj",
        reduced_weights,
        paired_keys[..., HEAD_SIZE:],
        preferred_element_type=jnp.float32,
    )
    return (top_new, totals, accum)


def release(
    dquery, query_rows, paired_keys, markers, query_pos, key_pos, log_total, mixed_gradient, deltas
):
    key_portion = paired_keys[..., :HEAD_SIZE]
    value_rows = paired_keys[..., HEAD_SIZE:]
    score_matrix = masked_scores(query_rows, key_portion, markers, query_pos, key_pos)
    weights = jnp.exp(score_matrix - log_total[..., None])
    weight_gradient = jnp.einsum(
        "acn,azn->acz", mixed_gradient, value_rows, preferred_element_type=jnp.float32
    )
    score_gradient = (weights * (weight_gradient - deltas[..., None])).astype(jnp.bfloat16)
    reduced_weights = weights.astype(jnp.bfloat16)
    dquery = (
        dquery
        + jnp.einsum(
            "zsx,zxj->zsj", score_gradient, key_portion, preferred_element_type=jnp.float32
        )
        * 0.125
    )
    key_gradient = (
        jnp.einsum("fov,foc->fvc", score_gradient, query_rows, preferred_element_type=jnp.float32)
        * 0.125
    )
    value_gradient = jnp.einsum(
        "fov,foc->fvc", reduced_weights, mixed_gradient, preferred_element_type=jnp.float32
    )
    return (dquery, key_gradient, value_gradient)


def empty_state(blocks, length):
    return (
        jnp.full((blocks, length), -1e30, jnp.float32),
        jnp.zeros((blocks, length), jnp.float32),
        jnp.zeros((blocks, length, HEAD_SIZE), jnp.float32),
    )


def attend_forward(items, markers, position, group, local):
    blocks = items.shape[0]
    query_rows = items[..., :HEAD_SIZE]
    paired_keys = items[..., HEAD_SIZE:]
    query_pos = position * local + jnp.arange(local, dtype=jnp.int32)
    state = absorb(
        empty_state(blocks, local), query_rows, paired_keys, markers, query_pos, query_pos
    )

    def turn(counter, carry):
        moving, moving_marks, state = carry
        moving, moving_marks = passed_along((moving, moving_marks), "win", 1)
        key_pos = (position - counter) % group * local + jnp.arange(local, dtype=jnp.int32)
        return (
            moving,
            moving_marks,
            absorb(state, query_rows, moving, moving_marks, query_pos, key_pos),
        )

    _, _, state = lax.fori_loop(1, group, turn, (paired_keys, markers, state))
    peak, totals, accum = state
    mixed_full = accum / totals[..., None]
    return (mixed_full.astype(jnp.bfloat16), (mixed_full, peak + jnp.log(totals)))


def attend_backward(items, markers, mixed_gradient, kept, position, group, local):
    blocks = items.shape[0]
    mixed_full, log_total = kept
    query_rows = items[..., :HEAD_SIZE]
    deltas = jnp.sum(mixed_gradient.astype(jnp.float32) * mixed_full, -1)
    query_pos = position * local + jnp.arange(local, dtype=jnp.int32)

    def turn(counter, carry):
        moving, moving_marks, dquery, dpairs = carry
        key_pos = (position - counter) % group * local + jnp.arange(local, dtype=jnp.int32)
        dquery, key_gradient, value_gradient = release(
            dquery,
            query_rows,
            moving,
            moving_marks,
            query_pos,
            key_pos,
            log_total,
            mixed_gradient,
            deltas,
        )
        dpairs = passed_along(
            (dpairs + jnp.concatenate([key_gradient, value_gradient], -1)).astype(jnp.bfloat16),
            "win",
            1,
        ).astype(jnp.float32)
        moving, moving_marks = passed_along((moving, moving_marks), "win", 1)
        return (moving, moving_marks, dquery, dpairs)

    start = (
        items[..., HEAD_SIZE:],
        markers,
        jnp.zeros((blocks, local, HEAD_SIZE), jnp.float32),
        jnp.zeros((blocks, local, 2 * HEAD_SIZE), jnp.float32),
    )
    _, _, dquery, dpairs = lax.fori_loop(0, group, turn, start)
    return jnp.concatenate([dquery, dpairs], -1).astype(jnp.bfloat16)


def layer_forward(hidden, layer_weights, markers, position, group, windows, local):
    joint, out_mat, up_mat, down_mat, norms = layer_weights
    hidden_low = hidden.astype(jnp.bfloat16)
    items = to_items(
        jnp.dot(hidden_low, joint, preferred_element_type=jnp.float32).astype(jnp.bfloat16),
        windows,
        local,
        3,
    )
    mixed_items, kept_attn = attend_forward(items, markers, position, group, local)
    mixed_low = from_items(mixed_items, windows, local, 1)
    resid_one = hidden + jnp.dot(mixed_low, out_mat, preferred_element_type=jnp.float32)
    middle = layer_norm(resid_one, norms[0], norms[1])
    middle_low = middle.astype(jnp.bfloat16)
    pre_gelu = jnp.dot(middle_low, up_mat, preferred_element_type=jnp.float32)
    activated = jax.nn.gelu(pre_gelu, approximate=False).astype(jnp.bfloat16)
    resid_two = middle + jnp.dot(activated, down_mat, preferred_element_type=jnp.float32)
    result = layer_norm(resid_two, norms[2], norms[3])
    return (
        result,
        (
            hidden_low,
            items,
            kept_attn,
            mixed_low,
            resid_one,
            middle_low,
            pre_gelu,
            activated,
            resid_two,
        ),
    )


def layer_backward(dresult, layer_weights, kept, markers, position, group, windows, local):
    joint, out_mat, up_mat, down_mat, norms = layer_weights
    (
        hidden_low,
        items,
        kept_attn,
        mixed_low,
        resid_one,
        middle_low,
        pre_gelu,
        activated,
        resid_two,
    ) = kept
    _, pull_two = jax.vjp(layer_norm, resid_two, norms[2], norms[3])
    dresid_two, dgain_two, dshift_two = pull_two(dresult)
    dbranch = dresid_two.astype(jnp.bfloat16)
    grad_down = jnp.dot(activated.T, dbranch, preferred_element_type=jnp.float32)
    dactive = jnp.dot(dbranch, down_mat.T, preferred_element_type=jnp.float32)
    _, pull_gelu = jax.vjp(partial(jax.nn.gelu, approximate=False), pre_gelu)
    dpre = pull_gelu(dactive)[0].astype(jnp.bfloat16)
    grad_up = jnp.dot(middle_low.T, dpre, preferred_element_type=jnp.float32)
    dmiddle = dresid_two + jnp.dot(dpre, up_mat.T, preferred_element_type=jnp.float32)
    _, pull_one = jax.vjp(layer_norm, resid_one, norms[0], norms[1])
    dresid_one, dgain_one, dshift_one = pull_one(dmiddle)
    dattn = dresid_one.astype(jnp.bfloat16)
    grad_out = jnp.dot(mixed_low.T, dattn, preferred_element_type=jnp.float32)
    mixed_gradient = jnp.dot(dattn, out_mat.T, preferred_element_type=jnp.float32).astype(
        jnp.bfloat16
    )
    ditems = attend_backward(
        items,
        markers,
        to_items(mixed_gradient, windows, local, 1),
        kept_attn,
        position,
        group,
        local,
    )
    dproj = from_items(ditems, windows, local, 3)
    grad_joint = jnp.dot(hidden_low.T, dproj, preferred_element_type=jnp.float32)
    dhidden = dresid_one + jnp.dot(dproj, joint.T, preferred_element_type=jnp.float32)
    grad_norm = jnp.stack([dgain_one, dshift_one, dgain_two, dshift_two])
    return (dhidden, (grad_joint, grad_out, grad_up, grad_down, grad_norm))


def sliced_windows_body(
    series,
    target,
    valid_slots,
    observed,
    embed_weight,
    joint_proj,
    out_proj,
    up_proj,
    down_proj,
    head_weight,
    norm_params,
    embed_mean,
    joint_mean,
    out_mean,
    up_mean,
    down_mean,
    head_mean,
    norm_mean,
    embed_square,
    joint_square,
    out_square,
    up_square,
    down_square,
    head_square,
    norm_square,
):
    windows = series.shape[0]
    local = series.shape[1]
    row_count = windows * local
    group = lax.axis_size("win")
    position = lax.axis_index("win")
    embed, joint, out_mat, up_mat, down_mat, head_mat, norms_low = (
        lax.all_gather(embed_weight.astype(jnp.bfloat16), "var", axis=1, tiled=True),
        lax.all_gather(joint_proj.astype(jnp.bfloat16), "var", axis=1, tiled=True),
        lax.all_gather(out_proj.astype(jnp.bfloat16), "var", axis=1, tiled=True),
        lax.all_gather(up_proj.astype(jnp.bfloat16), "var", axis=1, tiled=True),
        lax.all_gather(down_proj.astype(jnp.bfloat16), "var", axis=1, tiled=True),
        lax.all_gather(head_weight.astype(jnp.bfloat16), "var", axis=0, tiled=True),
        lax.all_gather(norm_params.astype(jnp.bfloat16), "var", axis=2, tiled=True),
    )
    norms = norms_low.astype(jnp.float32)
    weight_mask = observed.astype(jnp.float32) * valid_slots.astype(jnp.float32)[None, :, None]
    count = jnp.maximum(lax.psum(jnp.sum(weight_mask), ("var", "win")), 1.0)
    markers = valid_slots.astype(jnp.bfloat16)
    centre = jnp.mean(series, -1, keepdims=True)
    offset = series - centre
    spread = jnp.sqrt(jnp.mean(offset * offset, -1, keepdims=True) + 1e-05)
    normed = (offset / spread).astype(jnp.bfloat16).reshape(row_count, -1)
    hidden = jnp.dot(normed, embed, preferred_element_type=jnp.float32)
    layer = 0
    layer_weights = (joint[layer], out_mat[layer], up_mat[layer], down_mat[layer], norms[layer])
    hidden, kept = layer_forward(hidden, layer_weights, markers, position, group, windows, local)
    kept_layers = [kept]
    final_low = hidden.astype(jnp.bfloat16)
    guess = (
        jnp.dot(final_low, head_mat, preferred_element_type=jnp.float32).reshape(windows, local, -1)
        * spread
        + centre
    )
    error = guess - target
    loss_part = jnp.sum(weight_mask * error * error)
    dguess = (
        (2.0 * weight_mask * error / count * spread).reshape(row_count, -1).astype(jnp.bfloat16)
    )
    grad_head = jnp.dot(final_low.T, dguess, preferred_element_type=jnp.float32)
    dhidden = jnp.dot(dguess, head_mat.T, preferred_element_type=jnp.float32)
    layer_grads = [None] * LAYERS
    for layer in reversed(range(LAYERS)):
        layer_weights = (joint[layer], out_mat[layer], up_mat[layer], down_mat[layer], norms[layer])
        dhidden, layer_grads[layer] = layer_backward(
            dhidden, layer_weights, kept_layers[layer], markers, position, group, windows, local
        )
    grad_embed = jnp.dot(normed.T, dhidden.astype(jnp.bfloat16), preferred_element_type=jnp.float32)
    stacked = [jnp.stack([grads[i] for grads in layer_grads]) for i in range(5)]
    summed = (
        lax.psum_scatter(
            grad_embed.astype(jnp.bfloat16), "var", scatter_dimension=1, tiled=True
        ).astype(jnp.float32),
        lax.psum_scatter(
            stacked[0].astype(jnp.bfloat16), "var", scatter_dimension=1, tiled=True
        ).astype(jnp.float32),
        lax.psum_scatter(
            stacked[1].astype(jnp.bfloat16), "var", scatter_dimension=1, tiled=True
        ).astype(jnp.float32),
        lax.psum_scatter(
            stacked[2].astype(jnp.bfloat16), "var", scatter_dimension=1, tiled=True
        ).astype(jnp.float32),
        lax.psum_scatter(
            stacked[3].astype(jnp.bfloat16), "var", scatter_dimension=1, tiled=True
        ).astype(jnp.float32),
        lax.psum_scatter(
            grad_head.astype(jnp.bfloat16), "var", scatter_dimension=0, tiled=True
        ).astype(jnp.float32),
        lax.psum_scatter(
            stacked[4].astype(jnp.bfloat16), "var", scatter_dimension=2, tiled=True
        ).astype(jnp.float32),
    )
    totals = (
        lax.psum(summed[0].astype(jnp.bfloat16), "win").astype(jnp.float32),
        lax.psum(summed[1].astype(jnp.bfloat16), "win").astype(jnp.float32),
        lax.psum(summed[2].astype(jnp.bfloat16), "win").astype(jnp.float32),
        lax.psum(summed[3].astype(jnp.bfloat16), "win").astype(jnp.float32),
        lax.psum(summed[4].astype(jnp.bfloat16), "win").astype(jnp.float32),
        lax.psum(summed[5].astype(jnp.bfloat16), "win").astype(jnp.float32),
        lax.psum(summed[6].astype(jnp.bfloat16), "win").astype(jnp.float32),
    )
    loss = lax.psum(loss_part, ("var", "win")) / count
    count_step = float(STEP_NUMBER)
    weights = (embed_weight, joint_proj, out_proj, up_proj, down_proj, head_weight, norm_params)
    means = (embed_mean, joint_mean, out_mean, up_mean, down_mean, head_mean, norm_mean)
    squares = (
        embed_square,
        joint_square,
        out_square,
        up_square,
        down_square,
        head_square,
        norm_square,
    )
    results = [adamw(weights[i], means[i], squares[i], totals[i], count_step) for i in range(7)]
    return (
        loss.reshape(1),
        results[0][0],
        results[1][0],
        results[2][0],
        results[3][0],
        results[4][0],
        results[5][0],
        totals[6],
        results[0][1],
        results[1][1],
        results[2][1],
        results[3][1],
        results[4][1],
        results[5][1],
        results[6][1],
        results[0][2],
        results[1][2],
        results[2][2],
        results[3][2],
        results[4][2],
        results[5][2],
        results[6][2],
    )


def solution(mesh):
    swaps = mesh.shape["var"] == PARTS and mesh.shape["win"] == 2
    body = whole_windows_body if swaps else sliced_windows_body
    placed = (
        P("var", "win", None),
        P("var", "win", None),
        P("win"),
        P("var", "win", None),
        P(None, "var"),
        P(None, "var", None),
        P(None, "var", None),
        P(None, "var", None),
        P(None, "var", None),
        P("var", None),
        P(None, None, "var"),
        P(None, "var"),
        P(None, "var", None),
        P(None, "var", None),
        P(None, "var", None),
        P(None, "var", None),
        P("var", None),
        P(None, None, "var"),
        P(None, "var"),
        P(None, "var", None),
        P(None, "var", None),
        P(None, "var", None),
        P(None, "var", None),
        P("var", None),
        P(None, None, "var"),
    )
    return jax.shard_map(
        body,
        mesh=mesh,
        in_specs=placed,
        out_specs=(
            P(),
            P(None, "var"),
            P(None, "var", None),
            P(None, "var", None),
            P(None, "var", None),
            P(None, "var", None),
            P("var", None),
            P(None, None, "var"),
            P(None, "var"),
            P(None, "var", None),
            P(None, "var", None),
            P(None, "var", None),
            P(None, "var", None),
            P("var", None),
            P(None, None, "var"),
            P(None, "var"),
            P(None, "var", None),
            P(None, "var", None),
            P(None, "var", None),
            P(None, "var", None),
            P("var", None),
            P(None, None, "var"),
        ),
        check_vma=False,
    )
```

```python
from functools import partial

import jax
import jax.numpy as jnp
from jax import lax
from jax.experimental import pallas as pl
from jax.experimental.pallas import tpu as pltpu
from jax.sharding import PartitionSpec as P

HEADS = 8
HEAD_SIZE = 64
LAYERS = 1
STEP_NUMBER = 10

F32 = jnp.float32
BF16 = jnp.bfloat16
LANES = 128
D = HEADS * HEAD_SIZE
PARTS = 16
ROWS = D // PARTS
MIB = 1 << 20

OUT_AT, UP_AT, DOWN_AT, HEAD_AT, LOSS_AT, BUNDLE = 0, 128, 640, 1152, 1184, 1200
CUT = 896
EMBED_AT, FIRST = 384, 416


def dot_nn(a, b):
    return lax.dot_general(a, b, (((1,), (0,)), ((), ())), preferred_element_type=F32)


def dot_nt(a, b):
    return lax.dot_general(a, b, (((1,), (1,)), ((), ())), preferred_element_type=F32)


def dot_tn(a, b):
    return lax.dot_general(a, b, (((0,), (0,)), ((), ())), preferred_element_type=F32)


def offset_of(slot):
    return (slot % 4) * 4 + (slot // 4 % 2) * 2 + slot // 8


def slot_of(offset):
    return (offset & 1) * 8 + ((offset >> 1) & 1) * 4 + (offset >> 2)


def lane_index(shape):
    return lax.broadcasted_iota(jnp.int32, shape, len(shape) - 1)


IN_HBM = pl.BlockSpec(memory_space=pltpu.HBM)
ANYWHERE = pl.BlockSpec(memory_space=pl.ANY)


def ignoring(kernel, reads, ignored):
    def run(*refs):
        kernel(*refs[:reads], *refs[reads + ignored :])

    return run


def params(limit=63, **more):
    return pltpu.CompilerParams(vmem_limit_bytes=limit * MIB, **more)


def cost(flops, moved):
    return pl.CostEstimate(flops=int(flops), bytes_accessed=int(moved), transcendentals=0)


def swapped(block, axis, distance):
    count = lax.axis_size(axis)
    return lax.ppermute(block, axis, [(i, i ^ distance) for i in range(count)])


def sent_along_z(blocks):
    return [swapped(block, "var", 4 * i) for i, block in zip((1, 2, 3), blocks)]


def stacked_kernel(counts, *refs):
    ins, outs, sems = sum(counts), len(counts), refs[-1]
    blocks, results = refs[:ins], refs[ins : ins + outs]
    copies, at = [], 0
    for count, result in zip(counts, results):
        row = 0
        for block in blocks[at : at + count]:
            if len(block.shape) == 2:
                target, height = result.at[row], 1
            else:
                height = block.shape[0]
                target = result.at[pl.ds(row, height)]
            copies.append(pltpu.make_async_copy(block, target, sems.at[len(copies)]))
            row += height
        at += count
    for copy in copies:
        copy.start()
    for copy in copies:
        copy.wait()


def stacked(groups, after=()):
    counts = tuple(len(group) for group in groups)
    blocks = [block for group in groups for block in group]
    shapes = []
    for group in groups:
        rows = sum(1 if block.ndim == 2 else block.shape[0] for block in group)
        shapes.append(jax.ShapeDtypeStruct((rows, *group[0].shape[-2:]), BF16))
    vmem = pl.BlockSpec(memory_space=pltpu.VMEM)
    return pl.pallas_call(
        ignoring(partial(stacked_kernel, counts), len(blocks), len(after)),
        in_specs=[ANYWHERE] * (len(blocks) + len(after)),
        out_specs=[vmem] * len(shapes),
        out_shape=shapes,
        scratch_shapes=[pltpu.SemaphoreType.DMA((len(blocks),))],
        compiler_params=params(6),
        cost_estimate=cost(0, MIB),
        name="stacked",
    )(*blocks, *after)


def summed_kernel(groups, *refs):
    at, to = 0, sum(sum(counts) for counts, _ in groups)
    for counts, parts in groups:
        results = refs[to : to + parts]
        row = 0
        for count in counts:
            total = refs[at][...].astype(F32)
            for ref in refs[at + 1 : at + count]:
                total = total + ref[...].astype(F32)
            total = total.astype(BF16)
            rows = slice(row, row + total.shape[-2])
            for i, ref in enumerate(results):
                if total.ndim == 2:
                    ref[rows, :] = total
                elif len(ref.shape) == 2:
                    ref[rows, :] = total[i]
                else:
                    each = ref.shape[0]
                    ref[:, rows, :] = total[i * each : (i + 1) * each]
            row += total.shape[-2]
            at += count
        to += parts


def summed(groups, after=()):
    counts, shapes = [], []
    for columns, parts in groups:
        counts.append((tuple(len(terms) for terms in columns), parts))
        shape = columns[0][0].shape
        rows = sum(terms[0].shape[-2] for terms in columns)
        lead = () if len(shape) == 2 or shape[0] == parts else (shape[0] // parts,)
        shapes += [jax.ShapeDtypeStruct((*lead, rows, LANES), BF16)] * parts
    arrays = [term for columns, _ in groups for terms in columns for term in terms]
    vmem = pl.BlockSpec(memory_space=pltpu.VMEM)
    return pl.pallas_call(
        ignoring(partial(summed_kernel, tuple(counts)), len(arrays), len(after)),
        in_specs=[vmem] * len(arrays) + [ANYWHERE] * len(after),
        out_specs=[vmem] * len(shapes),
        out_shape=shapes,
        compiler_params=params(12),
        cost_estimate=cost(0, sum(array.size for array in arrays) * 3),
        name="summed",
    )(*arrays, *after)


def core_terms(kept, leaving):
    return [kept, swapped(leaving, "var", 1)]


def y_terms(near, far):
    return ([[near, swapped(far, "var", 2)]], 4)


def z_terms(mine, *others):
    return ([[mine, *sent_along_z(others)]], 1)


def with_other(mine):
    return (mine, swapped(mine, "win", 1))


def three_pieces(value):
    high = value.astype(BF16).astype(F32)
    middle = (value - high).astype(BF16).astype(F32)
    return (high, middle, value - high - middle)


def prep_kernel(
    pos_ref, series, target, observed, valid, kept_n, sent_n, kept_t, sent_t, count, total
):
    step = pl.program_id(0)
    half = pl.num_programs(0) // 2
    rows = series[0]
    look, local = rows.shape
    centre = jnp.mean(rows, 0, keepdims=True)
    offset = rows - centre
    spread = jnp.sqrt(jnp.mean(offset * offset, 0, keepdims=True) + 1e-05)
    normed = offset / spread
    mark = valid[...].astype(F32)
    weight = observed[0].astype(F32) * mark

    @pl.when(step == 0)
    def _():
        total[...] = jnp.zeros_like(total)

    total[...] += jnp.sum(jnp.sum(weight, 0, keepdims=True), 1, keepdims=True)
    spare = LANES - look
    row = lax.broadcasted_iota(jnp.int32, (spare, local), 0)
    extra = jnp.where(row == 0, mark, 0.0)
    for i, piece in enumerate(three_pieces(total[0:1, 0:1])):
        extra = jnp.where(row == 1 + i, piece, extra)
    normed = jnp.concatenate([normed, extra], axis=0).T.astype(BF16)
    extra = jnp.where(row == 0, centre, jnp.where(row == 1, spread, 0.0))
    future = jnp.concatenate([target[0], extra], axis=0).T
    weight = jnp.concatenate([weight, jnp.zeros((spare, local), F32)], axis=0).T

    @pl.when(step < half)
    def _():
        kept_n[0] = normed
        kept_t[0, :, 0:LANES] = future
        kept_t[0, :, LANES:] = weight

    @pl.when(step >= half)
    def _():
        sent_n[0] = normed
        sent_t[0, :, 0:LANES] = future
        sent_t[0, :, LANES:] = weight

    count[...] = total[...]


def prep(pos, series, target, observed, valid, after):
    windows, look, local = series.shape
    half = windows // 2

    def source(i, pos_ref):
        return (lax.rem(pos_ref[0] * half + i, windows), 0, 0)

    def kept(i, pos_ref):
        return (jnp.minimum(i, half - 1), 0, 0)

    def sent(i, pos_ref):
        return (jnp.maximum(i - half, 0), 0, 0)

    block = pl.BlockSpec((1, look, local), source)
    out_shape, out_specs = [], []
    for dtype, width in ((BF16, LANES), (F32, 2 * LANES)):
        for index in (kept, sent):
            out_shape.append(jax.ShapeDtypeStruct((half, local, width), dtype))
            out_specs.append(pl.BlockSpec((1, local, width), index))
    return pl.pallas_call(
        ignoring(prep_kernel, 5, len(after)),
        grid_spec=pltpu.PrefetchScalarGridSpec(
            num_scalar_prefetch=1,
            grid=(windows,),
            in_specs=[block, block, block, pl.BlockSpec((1, local), lambda i, p: (0, 0))]
            + [ANYWHERE] * len(after),
            out_specs=out_specs + [pl.BlockSpec((8, LANES), lambda i, p: (0, 0))],
            scratch_shapes=[pltpu.VMEM((8, LANES), F32)],
        ),
        out_shape=out_shape + [jax.ShapeDtypeStruct((8, LANES), F32)],
        compiler_params=params(8),
        cost_estimate=cost(0, 8 * MIB),
        name="prep",
    )(pos, series, target, observed, valid, *after)


def pack_first_kernel(joint, embed, out):
    for c in range(12):
        out[c * ROWS : (c + 1) * ROWS, :] = joint[0, :, c * LANES : (c + 1) * LANES].astype(BF16)
    look = embed.shape[-1]
    out[EMBED_AT:FIRST, 0:look] = embed[...].astype(BF16)
    out[EMBED_AT:FIRST, look:] = jnp.zeros((ROWS, LANES - look), BF16)


def pack_first(joint, embed):
    return pl.pallas_call(
        pack_first_kernel,
        out_shape=jax.ShapeDtypeStruct((FIRST, LANES), BF16),
        compiler_params=params(4),
        cost_estimate=cost(0, MIB // 2),
        name="pack_first",
    )(joint, embed)


def pack_second_kernel(own, came, out_w, up, down, head, norm, one, two):
    for c in range(4):
        one[OUT_AT + c * ROWS : OUT_AT + (c + 1) * ROWS, :] = out_w[
            0, :, c * LANES : (c + 1) * LANES
        ].astype(BF16)
    for c in range(16):
        one[UP_AT + c * ROWS : UP_AT + (c + 1) * ROWS, :] = up[
            0, :, c * LANES : (c + 1) * LANES
        ].astype(BF16)
    for c in range(4):
        two[c * LANES : (c + 1) * LANES, :] = down[0, :, c * LANES : (c + 1) * LANES].astype(BF16)
    horizon = head.shape[-1]
    spare = (ROWS, LANES - horizon)
    lane = lane_index(spare)
    count = own[0:1, 0:1] + jnp.sum(came[0, 0:1, 97:100].astype(F32), 1, keepdims=True)
    square = jnp.concatenate([norm[0], jnp.zeros((LANES - 4, ROWS), F32)], axis=0)
    square = jnp.concatenate([square] * (LANES // ROWS), axis=1).T
    extra = square[0:ROWS, 0 : LANES - horizon]
    for i, piece in enumerate(three_pieces(count)):
        extra = jnp.where(lane == 4 + i, piece, extra)
    two[HEAD_AT - DOWN_AT : LOSS_AT - DOWN_AT, 0:horizon] = head[...].astype(BF16)
    two[HEAD_AT - DOWN_AT : LOSS_AT - DOWN_AT, horizon:] = extra.astype(BF16)
    two[LOSS_AT - DOWN_AT :, :] = jnp.zeros((BUNDLE - LOSS_AT, LANES), BF16)


def pack_second(own, came, out_w, up, down, head, norm, after):
    half = came.shape[0]
    arrays = (own, came, out_w, up, down, head, norm)
    specs = [pl.BlockSpec(a.shape, lambda i, n=a.ndim: (0,) * n) for a in arrays]
    specs[1] = pl.BlockSpec((1, 16, LANES), lambda i: (half - 1, 0, 0))
    shapes = [(DOWN_AT, LANES), (BUNDLE - DOWN_AT, LANES)]
    return pl.pallas_call(
        ignoring(pack_second_kernel, len(arrays), len(after)),
        grid=(1,),
        in_specs=specs + [ANYWHERE] * len(after),
        out_specs=[pl.BlockSpec(shape, lambda i: (0, 0)) for shape in shapes],
        out_shape=[jax.ShapeDtypeStruct(shape, BF16) for shape in shapes],
        compiler_params=params(8),
        cost_estimate=cost(0, 2 * MIB),
        name="pack_second",
    )(*arrays, *after)


def project_kernel(me_ref, g0, g1, kept, came, qkv, hid, joint, embed):
    @pl.when(pl.program_id(0) == 0)
    def _():
        me = me_ref[0]
        for slot in range(PARTS):
            block = (g0, g1)[slot // 8]
            owner = me ^ offset_of(slot)
            for c in range(12):
                joint[owner, :, c * LANES : (c + 1) * LANES] = block[
                    slot % 8, c * ROWS : (c + 1) * ROWS, :
                ]
            embed[owner] = block[slot % 8, EMBED_AT:FIRST, :]

    normed = jnp.concatenate([kept[0], came[0]], axis=0)
    low = dot_nt(embed[...].reshape(D, LANES), normed).astype(BF16)
    hid[...] = low
    for part in range(3):
        weights = joint[:, :, part * D : (part + 1) * D].reshape(D, D)
        rows = dot_tn(weights, low)
        if part == 0:
            rows = rows * 0.18033688011112042
        qkv[part * D : (part + 1) * D, :] = rows.astype(BF16)


def project(me, bundle, kept, came):
    half, local, _ = kept.shape
    slots = 2 * local
    whole = pl.BlockSpec((8, FIRST, LANES), lambda w, m: (0, 0, 0))
    mine = pl.BlockSpec((1, local, LANES), lambda w, m: (w, 0, 0))
    return pl.pallas_call(
        project_kernel,
        grid_spec=pltpu.PrefetchScalarGridSpec(
            num_scalar_prefetch=1,
            grid=(half,),
            in_specs=[whole] * 2 + [mine] * 2,
            out_specs=[
                pl.BlockSpec((3 * D, slots), lambda w, m: (0, w)),
                pl.BlockSpec((D, slots), lambda w, m: (0, w)),
                pl.BlockSpec((PARTS, ROWS, 3 * D), lambda w, m: (0, 0, 0)),
                pl.BlockSpec((PARTS, ROWS, LANES), lambda w, m: (0, 0, 0)),
            ],
        ),
        out_shape=[
            jax.ShapeDtypeStruct((3 * D, half * slots), BF16),
            jax.ShapeDtypeStruct((D, half * slots), BF16),
            jax.ShapeDtypeStruct((PARTS, ROWS, 3 * D), BF16),
            jax.ShapeDtypeStruct((PARTS, ROWS, LANES), BF16),
        ],
        compiler_params=params(18),
        cost_estimate=cost(1e6, 1000),
        name="project",
    )(me, *bundle, kept, came)


def tiles_of(length, size):
    return [(at, min(size, length - at)) for at in range(0, length, size)]


PAIR = 2


def head_rows(i):
    return slice(i * HEAD_SIZE, (i + 1) * HEAD_SIZE)


def attend_kernel(kept, came, q, k, v, weights, mixed, scale, bias):
    slots = q.shape[1]
    local = slots // 2

    @pl.when((pl.program_id(0) == 0) & (pl.program_id(1) == 0))
    def _():
        for part, marks in enumerate((kept, came)):
            rows = slice(part * local, (part + 1) * local)
            mark = marks[0, :, 96:97].astype(F32)
            key = part * local + lax.broadcasted_iota(jnp.int32, (local, slots), 0)
            query = lane_index((local, slots))
            bias[rows, :] = jnp.where((mark > 0.5) | (key == query), 0.0, -1e30)

    def score_of(i):
        return dot_tn(k[head_rows(i), :], q[head_rows(i), :]) + bias[...]

    def weigh(i, score):
        weight = jnp.exp2(score - jnp.max(score, 0, keepdims=True))
        low = weight.astype(BF16)
        weights[i] = low
        return (low, jnp.sum(weight, 0, keepdims=True))

    def mix(i, low, total):
        inverse = 1.0 / total
        scale[i] = inverse
        mixed[head_rows(i), :] = (dot_nn(v[head_rows(i), :], low) * inverse).astype(BF16)

    score = score_of(0)
    pending = None
    for i in range(PAIR):
        coming = score_of(i + 1) if i + 1 < PAIR else None
        weighed = weigh(i, score)
        if pending is not None:
            mix(*pending)
        pending = (i, *weighed)
        score = coming
    mix(*pending)


def attend(first, count, kept, came, qkv, after=(), held=()):
    half, local, _ = kept.shape
    slots = 2 * local
    marks = pl.BlockSpec((1, local, LANES), lambda h, w: (0, 0, 0))

    def heads(part):
        return pl.BlockSpec(
            (PAIR * HEAD_SIZE, slots), lambda h, w: ((part * HEADS + first) // PAIR + h, w)
        )

    return pl.pallas_call(
        ignoring(attend_kernel, 5, len(held) + len(after)),
        grid=(count // PAIR, half),
        in_specs=[marks, marks, heads(0), heads(1), heads(2)] + [ANYWHERE] * (len(held) + len(after)),
        out_specs=[
            pl.BlockSpec(
                (PAIR, slots, slots), lambda h, w: ((first // PAIR + h) * half + w, 0, 0)
            ),
            pl.BlockSpec((PAIR * HEAD_SIZE, slots), lambda h, w: (h, w)),
            pl.BlockSpec((PAIR, 1, slots), lambda h, w: (h * half + w, 0, 0)),
        ],
        out_shape=[
            jax.ShapeDtypeStruct((HEADS * half, slots, slots), BF16),
            jax.ShapeDtypeStruct((count * HEAD_SIZE, half * slots), BF16),
            jax.ShapeDtypeStruct((count * half, 1, slots), F32),
        ],
        scratch_shapes=[pltpu.VMEM((slots, slots), F32)],
        compiler_params=params(39),
        cost_estimate=cost(count * half * 2e9, count * half * 2 * MIB),
        name="attend",
        input_output_aliases={5 + i: i for i in range(len(held))},
    )(kept, came, qkv, qkv, qkv, *held, *after)


def unattend_kernel(
    me_ref, weights, scale, mixed, dmixed, q, k, v, hid, dproj, kept, leaving, rows, packed, sems
):
    head, window = pl.program_id(0), pl.program_id(1)
    slots = q.shape[1]

    def prepared(i):
        low = (dmixed[head_rows(i), :].astype(F32) * scale[i]).astype(BF16)
        share = low.astype(F32) * mixed[head_rows(i), :].astype(F32)
        return (low, jnp.sum(share, 0, keepdims=True))

    def dweight_of(i, low, delta):
        return dot_tn(v[head_rows(i), :], low) - delta

    ready = [prepared(i) for i in range(PAIR)]
    dweight = dweight_of(0, *ready[0])
    for i in range(PAIR):
        coming = dweight_of(i + 1, *ready[i + 1]) if i + 1 < PAIR else None
        dscore = (weights[i].astype(F32) * dweight).astype(BF16)
        dquery = dot_nn(k[head_rows(i), :], dscore) * 0.125
        dkey = dot_nt(q[head_rows(i), :], dscore) * 0.6931471805599453
        dvalue = dot_nt(ready[i][0], weights[i])
        for part, grad in enumerate((dquery, dkey, dvalue)):
            dproj[part, head_rows(i), :] = grad.astype(BF16)
        dweight = coming
    start = pl.multiple_of(window * slots, LANES)
    for part in range(3):
        rows[part, head, :, pl.ds(start, slots)] = dproj[part]

    count = pl.num_programs(0)

    @pl.when((head == count - 1) & (window == pl.num_programs(1) - 1))
    def _():
        me = me_ref[0]
        width = rows.shape[1] * rows.shape[2]
        for part in range(3):
            grad = dot_nt(hid[...], rows[part].reshape(width, rows.shape[-1])).astype(BF16)
            for b in range(PARTS):
                slot = slot_of(b ^ me)
                for c in range(width // LANES):
                    at = (part * (width // LANES) + c) * ROWS
                    packed[slot, at : at + ROWS, :] = grad[
                        b * ROWS : (b + 1) * ROWS, c * LANES : (c + 1) * LANES
                    ]
        send_packed(packed, kept, leaving, sems)


def send_packed(packed, kept, leaving, sems, rows=None):
    half = PARTS // 2
    start, height = rows or (0, packed.shape[1])
    copies = [
        pltpu.make_async_copy(
            packed.at[pl.ds(i * half, half), pl.ds(start, height)], target, sems.at[i]
        )
        for i, target in enumerate((kept, leaving))
    ]
    for copy in copies:
        copy.start()
    for copy in copies:
        copy.wait()


def unattend(me, first, count, weights, scale, mixed, dmixed, qkv, hid, after=()):
    slots = weights.shape[-1]
    tokens = qkv.shape[1]
    half = tokens // slots
    height = 3 * count * HEAD_SIZE // LANES * ROWS
    lead = first // PAIR

    def heads(part):
        return pl.BlockSpec(
            (PAIR * HEAD_SIZE, slots), lambda h, w, m: (part * HEADS // PAIR + lead + h, w)
        )

    return pl.pallas_call(
        ignoring(unattend_kernel, 9, len(after)),
        grid_spec=pltpu.PrefetchScalarGridSpec(
            num_scalar_prefetch=1,
            grid=(count // PAIR, half),
            in_specs=[
                pl.BlockSpec(
                    (PAIR, slots, slots), lambda h, w, m: ((lead + h) * half + w, 0, 0)
                ),
                pl.BlockSpec((PAIR, 1, slots), lambda h, w, m: (h * half + w, 0, 0)),
                pl.BlockSpec((PAIR * HEAD_SIZE, slots), lambda h, w, m: (h, w)),
                pl.BlockSpec((PAIR * HEAD_SIZE, slots), lambda h, w, m: (lead + h, w)),
                heads(0),
                heads(1),
                heads(2),
                pl.BlockSpec((D, tokens), lambda h, w, m: (0, 0)),
            ]
            + [ANYWHERE] * len(after),
            out_specs=[
                pl.BlockSpec((3, PAIR * HEAD_SIZE, slots), lambda h, w, m: (0, h, w)),
                ANYWHERE,
                ANYWHERE,
            ],
            scratch_shapes=[
                pltpu.VMEM((3, count // PAIR, PAIR * HEAD_SIZE, tokens), BF16),
                pltpu.VMEM((PARTS, height, LANES), BF16),
                pltpu.SemaphoreType.DMA((2,)),
            ],
        ),
        out_shape=[
            jax.ShapeDtypeStruct((3, count * HEAD_SIZE, tokens), BF16),
            jax.ShapeDtypeStruct((PARTS // 2, height, LANES), BF16),
            jax.ShapeDtypeStruct((PARTS // 2, height, LANES), BF16),
        ],
        compiler_params=params(45),
        cost_estimate=cost(count * half * 2.8e9, count * half * 2 * MIB),
        name="unattend",
    )(me, weights, scale, mixed, dmixed, qkv, qkv, qkv, hid, *after)


def gelu_parts(pre):
    phi = 0.5 + 0.5 * lax.erf(pre * 0.7071067811865476)
    bell = jnp.exp2(pre * pre * -0.7213475204444817)
    return (pre * phi, phi + pre * (bell * 0.3989422804014327))


def norm_forward(resid, gain, shift):
    centre = jnp.mean(resid, 0, keepdims=True)
    offset = resid - centre
    inverse = lax.rsqrt(jnp.mean(offset * offset, 0, keepdims=True) + 1e-05)
    unit = offset * inverse
    return (unit * gain + shift, unit, inverse)


def norm_backward(grad, unit, inverse, gain):
    scaled = grad * gain
    first = jnp.mean(scaled, 0, keepdims=True)
    second = jnp.mean(scaled * unit, 0, keepdims=True)
    return (scaled - first - unit * second) * inverse


def wide(block, size):
    return jnp.concatenate([block] * (size // LANES), axis=1)


def folded(block):
    total = block[:, 0:LANES]
    for at in range(LANES, block.shape[1], LANES):
        total = total + block[:, at : at + LANES]
    return total


def middle_kernel(
    me_ref,
    a0,
    a1,
    b0,
    b1,
    *refs,
):
    fetched, (dmixed_out, dattn_out), refs = refs[:7], refs[7:9], refs[9:]
    spaces, (dmixed, dattn), refs = refs[-8:-3], refs[-3:-1], (*refs[:-8], refs[-1])
    embed, normed, future, mixed_a, mixed_b = spaces
    windows, local, _ = fetched[1].shape
    moves = [(fetched[0], embed), (fetched[5], mixed_a), (fetched[6], mixed_b)]
    for window in range(windows):
        for side in range(2):
            rows = pl.ds((2 * window + side) * local, local)
            moves.append((fetched[1 + side].at[window], normed.at[rows]))
            moves.append((fetched[3 + side].at[window], future.at[rows]))
    arrivals = [
        pltpu.make_async_copy(array, space, refs[-1].at[i])
        for i, (array, space) in enumerate(moves)
    ]
    for arrival in arrivals:
        arrival.start()
    results = [
        pltpu.make_async_copy(space, array, refs[-1].at[len(arrivals) + i])
        for i, (space, array) in enumerate(((dmixed, dmixed_out), (dattn, dattn_out)))
    ]
    middle_body(me_ref, a0, a1, b0, b1, *spaces, dmixed, dattn, *refs[:-1], arrivals, results)


def middle_body(
    me_ref,
    a0,
    a1,
    b0,
    b1,
    embed,
    normed,
    future,
    mixed_a,
    mixed_b,
    dmixed,
    dattn,
    counted,
    kept_a,
    leaving_a,
    kept_b,
    leaving_b,
    w_out,
    w_up,
    w_down,
    w_head,
    t_out,
    t_up,
    t_down,
    norms,
    middle_s,
    active_s,
    dbranch_s,
    dpre_s,
    final_s,
    dguess_s,
    norm_sums,
    loss_sum,
    packed,
    sems,
    arrivals,
    results,
):
    ff = active_s.shape[0]
    chunks = ff // D
    me = me_ref[0]
    tokens = normed.shape[0]

    def set_up():
        copies = [
            pltpu.make_async_copy(
                block, packed.at[pl.ds(i % 2 * 8, 8), pl.ds(at, block.shape[1])], sems.at[i]
            )
            for i, (at, block) in enumerate(((0, a0), (0, a1), (DOWN_AT, b0), (DOWN_AT, b1)))
        ]
        for copy in copies:
            copy.start()
        for copy in copies:
            copy.wait()
        total = jnp.zeros((1, 1), F32)
        for slot in range(PARTS):
            owner = me ^ offset_of(slot)
            for c in range(4):
                cols = slice(c * LANES, (c + 1) * LANES)
                at = OUT_AT + c * ROWS
                w_out[owner, :, cols] = packed[slot, at : at + ROWS, :]
                at = DOWN_AT + c * LANES
                w_down[owner, :, cols] = packed[slot, at : at + LANES, :]
            for c in range(16):
                at = UP_AT + c * ROWS
                w_up[owner, :, c * LANES : (c + 1) * LANES] = packed[slot, at : at + ROWS, :]
            head = packed[slot, HEAD_AT:LOSS_AT, :]
            w_head[owner] = head
            pieces = head[0:1, 100:103].astype(F32)
            total = total + jnp.sum(pieces, 1, keepdims=True)
        counted[...] = jnp.broadcast_to(jnp.maximum(total, 1.0), counted.shape)
        t_out[...] = w_out[...].reshape(D, D).T
        for c in range(chunks):
            rows = slice(c * D, (c + 1) * D)
            t_up[rows, :] = w_up[:, :, rows].reshape(D, D).T
            t_down[:, rows] = w_down[c * 4 : (c + 1) * 4].reshape(D, D).T
        extra = w_head[...].reshape(D, LANES)
        for i in range(4):
            column = extra[:, 96 + i : 97 + i].astype(F32)
            norms[i] = jnp.broadcast_to(column, (D, LANES))
        norm_sums[...] = jnp.zeros_like(norm_sums)
        loss_sum[...] = jnp.zeros_like(loss_sum)

    set_up()
    for arrival in arrivals:
        arrival.wait()
    tiles = [
        middle_tile(
            at,
            min(MIDDLE_SIZE, tokens - at),
            *(normed, future, embed, mixed_a, mixed_b, dmixed, dattn, counted),
            *(w_out, w_up, w_down, w_head, t_out, t_up, t_down, norms),
            *(middle_s, active_s, dbranch_s, dpre_s, final_s, dguess_s, norm_sums, loss_sum),
        )
        for at in range(0, tokens, MIDDLE_SIZE)
    ]
    in_turn(tiles, LAG)
    for result in results:
        result.start()

    def place(grad, first_row, blocks, base):
        height = grad.shape[0] // blocks
        for b in range(blocks):
            slot = slot_of((first_row + b) ^ me)
            for c in range(grad.shape[1] // LANES):
                at = base + c * height
                packed[slot, at : at + height, :] = grad[
                    b * height : (b + 1) * height, c * LANES : (c + 1) * LANES
                ]

    for c in range(chunks):
        rows = slice(c * D, (c + 1) * D)
        place(dot_nt(active_s[rows, :], dbranch_s[...]).astype(BF16), c * 4, 4, DOWN_AT)
        place(
            dot_nt(middle_s[...], dpre_s[rows, :]).astype(BF16),
            0,
            PARTS,
            UP_AT + c * (D // LANES) * ROWS,
        )
    for i, side in enumerate((mixed_a, mixed_b)):
        grad = dot_nt(side[...], dattn[...]).astype(BF16)
        place(grad, i * (PARTS // 2), PARTS // 2, OUT_AT)
    head = dot_nn(final_s[...], dguess_s[...])
    lane = lane_index(head.shape)
    for i in range(4):
        head = jnp.where(lane == 96 + i, jnp.sum(norm_sums[i], 1, keepdims=True), head)
    place(head.astype(BF16), 0, PARTS, HEAD_AT)
    row = lax.broadcasted_iota(jnp.int32, (BUNDLE - LOSS_AT, LANES), 0)
    losses = jnp.where(row == 0, loss_sum[...], 0.0).astype(BF16)
    for slot in range(PARTS):
        packed[slot, LOSS_AT:BUNDLE, :] = losses
    send_packed(packed, kept_a, leaving_a, sems, (0, CUT))
    send_packed(packed, kept_b, leaving_b, sems, (CUT, BUNDLE - CUT))
    for result in results:
        result.wait()


def in_turn(streams, lag):
    waiting = [lag * i for i in range(len(streams))]
    live = [True] * len(streams)
    while any(live):
        for i, stream in enumerate(streams):
            if waiting[i] > 0:
                waiting[i] -= 1
            elif live[i]:
                live[i] = next(stream, stream) is not stream


def middle_tile(
    at,
    size,
    normed,
    future,
    embed,
    mixed_a,
    mixed_b,
    dmixed,
    dattn,
    counted,
    w_out,
    w_up,
    w_down,
    w_head,
    t_out,
    t_up,
    t_down,
    norms,
    middle_s,
    active_s,
    dbranch_s,
    dpre_s,
    final_s,
    dguess_s,
    norm_sums,
    loss_sum,
):
    ff = active_s.shape[0]
    height = FF_ROWS
    cols = slice(at, at + size)
    mixed = jnp.concatenate([mixed_a[:, cols], mixed_b[:, cols]], axis=0)
    resid = dot_nt(embed[...].reshape(D, LANES), normed[cols, :]) + dot_nn(t_out[...], mixed)
    yield
    gain_one, gain_two = wide(norms[0], size), wide(norms[2], size)
    middle, unit_one, inverse_one = norm_forward(resid, gain_one, wide(norms[1], size))
    middle_low = middle.astype(BF16)
    middle_s[:, cols] = middle_low
    yield
    for row in range(0, ff, height):
        rows = slice(row, row + height)
        active, gradient = gelu_parts(dot_nn(t_up[rows, :], middle_low))
        active_s[rows, cols] = active.astype(BF16)
        dpre_s[rows, cols] = gradient.astype(BF16)
        yield
    yield
    resid = middle + dot_nn(t_down[...], active_s[:, cols])
    yield
    final, unit_two, inverse_two = norm_forward(resid, gain_two, wide(norms[3], size))
    final_low = final.astype(BF16)
    final_s[:, cols] = final_low
    w_h = w_head[...].reshape(D, LANES)
    yield
    guess = dot_tn(final_low, w_h)
    yield
    ahead = future[cols, 0:LANES]
    weighting = future[cols, LANES:]
    centre = future[cols, 96:97]
    spread = future[cols, 97:98]
    error = guess * spread + centre - ahead
    loss_sum[...] += jnp.sum(weighting * error * error, 0, keepdims=True)
    dguess = (2.0 * weighting * error / counted[0:1, 0:1] * spread).astype(BF16)
    dguess_s[cols, :] = dguess
    yield
    dfinal = dot_nt(w_h, dguess)
    yield
    norm_sums[2] += folded(dfinal * unit_two)
    norm_sums[3] += folded(dfinal)
    dresid = norm_backward(dfinal, unit_two, inverse_two, gain_two)
    dbranch = dresid.astype(BF16)
    dbranch_s[:, cols] = dbranch
    yield
    w_d = w_down[...].reshape(ff, D)
    for row in range(0, ff, height):
        rows = slice(row, row + height)
        dpre = (dot_nn(w_d[rows], dbranch) * dpre_s[rows, cols].astype(F32)).astype(BF16)
        dpre_s[rows, cols] = dpre
        yield
    yield
    dresid = dresid + dot_nn(w_up[...].reshape(D, ff), dpre_s[:, cols])
    yield
    norm_sums[0] += folded(dresid * unit_one)
    norm_sums[1] += folded(dresid)
    dfirst = norm_backward(dresid, unit_one, inverse_one, gain_one).astype(BF16)
    dattn[:, cols] = dfirst
    yield
    dmixed[:, cols] = dot_nn(w_out[...].reshape(D, D), dfirst).astype(BF16)


LAG = 2
MIDDLE_SIZE = 896
FF_ROWS = 512


def middle_pass(me, bundle, embed, kept, came, mixed, ff):
    tokens = mixed[0].shape[1]
    fetched = (embed, kept[0], came[0], kept[1], came[1], *mixed)
    vmem = pl.BlockSpec(memory_space=pltpu.VMEM)
    return pl.pallas_call(
        middle_kernel,
        in_specs=[pl.BlockSpec(memory_space=pltpu.SMEM)] + [ANYWHERE] * 4 + [IN_HBM] * 7,
        out_specs=[IN_HBM, IN_HBM, vmem] + [IN_HBM] * 4,
        scratch_shapes=[
            pltpu.VMEM((PARTS, ROWS, D), BF16),
            pltpu.VMEM((PARTS, ROWS, ff), BF16),
            pltpu.VMEM((PARTS, ff // PARTS, D), BF16),
            pltpu.VMEM((PARTS, ROWS, LANES), BF16),
            pltpu.VMEM((D, D), BF16),
            pltpu.VMEM((ff, D), BF16),
            pltpu.VMEM((D, ff), BF16),
            pltpu.VMEM((4, D, LANES), F32),
            pltpu.VMEM((D, tokens), BF16),
            pltpu.VMEM((ff, tokens), BF16),
            pltpu.VMEM((D, tokens), BF16),
            pltpu.VMEM((ff, tokens), BF16),
            pltpu.VMEM((D, tokens), BF16),
            pltpu.VMEM((tokens, LANES), BF16),
            pltpu.VMEM((4, D, LANES), F32),
            pltpu.VMEM((1, LANES), F32),
            pltpu.VMEM((PARTS, BUNDLE, LANES), BF16),
            pltpu.SemaphoreType.DMA((4,)),
        ]
        + [
            pltpu.VMEM(embed.shape, BF16),
            pltpu.VMEM((tokens, LANES), BF16),
            pltpu.VMEM((tokens, 2 * LANES), F32),
        ]
        + [pltpu.VMEM((D // 2, tokens), BF16)] * 2
        + [pltpu.VMEM((D, tokens), BF16)] * 2
        + [pltpu.SemaphoreType.DMA((5 + 4 * kept[0].shape[0],))],
        out_shape=[
            jax.ShapeDtypeStruct((D, tokens), BF16),
            jax.ShapeDtypeStruct((D, tokens), BF16),
            jax.ShapeDtypeStruct((8, LANES), F32),
            jax.ShapeDtypeStruct((PARTS // 2, CUT, LANES), BF16),
            jax.ShapeDtypeStruct((PARTS // 2, CUT, LANES), BF16),
            jax.ShapeDtypeStruct((PARTS // 2, BUNDLE - CUT, LANES), BF16),
            jax.ShapeDtypeStruct((PARTS // 2, BUNDLE - CUT, LANES), BF16),
        ],
        compiler_params=params(57),
        cost_estimate=cost(35e9, 20 * MIB),
        name="middle",
    )(me, *bundle, *fetched)


def last_kernel(
    me_ref, joint, dproj_a, dproj_b, dattn, kept_n, came_n, near, far, kept, leaving, *scratch
):
    joint_s, dproj_s, dattn_s, normed, packed, sems = scratch
    me = me_ref[0]
    windows, local, _ = kept_n.shape
    slots = 2 * local
    rows = near.shape[1]
    half = PARTS // 2
    copies = [pltpu.make_async_copy(joint, joint_s, sems.at[0])]
    for w in range(windows):
        cols = pl.ds(w * slots, slots)
        for source, target in (
            (dproj_a.at[:, :, cols], dproj_s.at[w, :, pl.ds(0, D // 2)]),
            (dproj_b.at[:, :, cols], dproj_s.at[w, :, pl.ds(D // 2, D // 2)]),
            (dattn.at[:, cols], dattn_s.at[w]),
            (kept_n.at[w], normed.at[w, pl.ds(0, local)]),
            (came_n.at[w], normed.at[w, pl.ds(local, local)]),
        ):
            copies.append(pltpu.make_async_copy(source, target, sems.at[len(copies)]))
    per_window = (len(copies) - 1) // windows
    for i, side in enumerate((near, far)):
        target = packed.at[pl.ds(i * half, half), pl.ds(0, rows)]
        copies.append(pltpu.make_async_copy(side, target, sems.at[len(copies)]))
    for copy in copies:
        copy.start()
    copies[0].wait()
    total = jnp.zeros((D, LANES), F32)
    for w in range(windows):
        for copy in copies[1 + w * per_window : 1 + (w + 1) * per_window]:
            copy.wait()
        dhidden = dattn_s[w].astype(F32)
        for part in range(3):
            weights = joint_s[:, :, part * D : (part + 1) * D].reshape(D, D)
            dhidden = dhidden + dot_nn(weights, dproj_s[w, part])
        total = total + dot_nn(dhidden.astype(BF16), normed[w])
    total = total.astype(BF16)
    for b in range(PARTS):
        packed[slot_of(b ^ me), rows : rows + ROWS, :] = total[b * ROWS : (b + 1) * ROWS, :]
    for copy in copies[-2:]:
        copy.wait()
    send_packed(packed, kept, leaving, sems)


def last_pass(me, joint, dprojs, dattn, kept, came, near, far, after=()):
    windows, local, _ = kept.shape
    slots = 2 * local
    height = near.shape[1] + ROWS
    return pl.pallas_call(
        ignoring(last_kernel, 9, len(after)),
        in_specs=[pl.BlockSpec(memory_space=pltpu.SMEM)]
        + [IN_HBM] * 8
        + [ANYWHERE] * len(after),
        out_specs=[IN_HBM, IN_HBM],
        out_shape=[
            jax.ShapeDtypeStruct((PARTS // 2, height, LANES), BF16),
            jax.ShapeDtypeStruct((PARTS // 2, height, LANES), BF16),
        ],
        scratch_shapes=[
            pltpu.VMEM((PARTS, ROWS, 3 * D), BF16),
            pltpu.VMEM((windows, 3, D, slots), BF16),
            pltpu.VMEM((windows, D, slots), BF16),
            pltpu.VMEM((windows, slots, LANES), BF16),
            pltpu.VMEM((PARTS, height, LANES), BF16),
            pltpu.SemaphoreType.DMA((3 + 5 * windows,)),
        ],
        compiler_params=params(26),
        cost_estimate=cost(10e9, 10 * MIB),
        name="last",
    )(me, joint, *dprojs, dattn, kept, came, near, far, *after)


def adamw(weight, mean, square, grad, count_step):
    mean_next = 0.9 * mean + 0.1 * grad
    square_next = 0.999 * square + 0.001 * grad * grad
    mean_hat = mean_next / (1.0 - 0.9**count_step)
    square_hat = square_next / (1.0 - 0.999**count_step)
    weight_next = weight - 0.1 * (mean_hat / (jnp.sqrt(square_hat) + 1e-08) + 0.1 * weight)
    return (weight_next, mean_next, square_next)


def step_second_kernel(mine_a, other_a, mine_b, other_b, counted, *refs):
    held, results = refs[:15], refs[15:]
    grad = mine_a[...].astype(F32) + other_a[...].astype(F32)
    rest = mine_b[...].astype(F32) + other_b[...].astype(F32)

    def grad_rows(at, height):
        return grad[at : at + height] if at < CUT else rest[at - CUT : at - CUT + height]

    def update(which, at, value):
        states = [held[which * 3 + j] for j in range(3)]
        news = adamw(*[state[at] for state in states], value, float(STEP_NUMBER))
        for j in range(3):
            results[which * 3 + j][at] = news[j]

    def block(c):
        return slice(c * LANES, (c + 1) * LANES)

    for c in range(4):
        base = OUT_AT + c * ROWS
        update(0, (0, slice(None), block(c)), grad[base : base + ROWS])
    for c in range(16):
        base = UP_AT + c * ROWS
        update(1, (0, slice(None), block(c)), grad[base : base + ROWS])
    for c in range(4):
        update(2, (0, slice(None), block(c)), grad_rows(DOWN_AT + c * LANES, LANES))
    horizon = held[9].shape[-1]
    head = grad_rows(HEAD_AT, ROWS)
    update(3, (slice(None), slice(None)), head[:, 0:horizon])
    norm = jnp.concatenate([head] * (LANES // ROWS), axis=0).T[96:100, 0:ROWS]
    update(4, (0, slice(None), slice(None)), norm)
    results[15][0] = norm
    losses = jnp.sum(grad_rows(LOSS_AT, 1), 1, keepdims=True)
    results[16][...] = losses / counted[0:1, 0:1]


def step_second(pair_a, pair_b, counted, states):
    shapes = [jax.ShapeDtypeStruct(a.shape, F32) for a in states]
    return pl.pallas_call(
        step_second_kernel,
        out_shape=shapes
        + [jax.ShapeDtypeStruct(states[12].shape, F32), jax.ShapeDtypeStruct((1, 1), F32)],
        compiler_params=params(20),
        cost_estimate=cost(0, 5 * MIB),
        name="step_second",
    )(*pair_a, *pair_b, counted, *states)


def step_first_kernel(mine_a, other_a, mine_b, other_b, *refs):
    held, results = refs[:6], refs[6:]
    halves = [
        mine_a[BUNDLE - CUT :, :].astype(F32) + other_a[BUNDLE - CUT :, :].astype(F32),
        mine_b[...].astype(F32) + other_b[...].astype(F32),
    ]

    def update(which, at, value):
        states = [held[which * 3 + j] for j in range(3)]
        news = adamw(*[state[at] for state in states], value, float(STEP_NUMBER))
        for j in range(3):
            results[which * 3 + j][at] = news[j]

    for part in range(3):
        for side in range(2):
            for c in range(2):
                at = (part * 2 + c) * ROWS
                start = part * D + side * (D // 2) + c * LANES
                update(0, (0, slice(None), slice(start, start + LANES)), halves[side][at : at + ROWS])
    look = held[3].shape[-1]
    update(1, (slice(None), slice(None)), halves[1][6 * ROWS : 7 * ROWS, 0:look])


def step_first(pair_a, pair_b, states):
    shapes = [jax.ShapeDtypeStruct(a.shape, F32) for a in states]
    return pl.pallas_call(
        step_first_kernel,
        out_shape=shapes,
        compiler_params=params(12),
        cost_estimate=cost(0, 2 * MIB),
        name="step_first",
    )(*pair_a, *pair_b, *states)


def whole_windows_body(
    series,
    target,
    valid_slots,
    observed,
    embed_weight,
    joint_proj,
    out_proj,
    up_proj,
    down_proj,
    head_weight,
    norm_params,
    embed_mean,
    joint_mean,
    out_mean,
    up_mean,
    down_mean,
    head_mean,
    norm_mean,
    embed_square,
    joint_square,
    out_square,
    up_square,
    down_square,
    head_square,
    norm_square,
):
    me = lax.axis_index("var").astype(jnp.int32).reshape(1)
    pos = lax.axis_index("win").astype(jnp.int32).reshape(1)
    ff = up_proj.shape[-1]
    packed = pack_first(joint_proj, embed_weight.T)
    row = sent_along_z([packed] * 3)
    turned = [array.transpose(0, 2, 1) for array in (series, target, observed)]
    prepared = prep(pos, *turned, valid_slots.reshape(1, -1), [packed])
    own = prepared[4]
    kept, came = prepared[0:4:2], [swapped(sent, "win", 1) for sent in prepared[1:4:2]]
    (plane,) = stacked([[packed, *row]], [prepared[0]])
    bundles = pack_second(
        own, came[0], out_proj, up_proj, down_proj, head_weight, norm_params, [plane]
    )
    (held,) = stacked([[plane, swapped(plane, "var", 2)]], [bundles[0]])
    qkv, hid, joint, embed = project(me, (held, swapped(held, "var", 1)), kept[0], came[0])
    count = HEADS // 2
    plane_a, bundle_b = stacked(
        [[bundles[0], *sent_along_z([bundles[0]] * 3)], [bundles[1]]], [qkv]
    )
    bundle_b = bundle_b[0]
    sides = [attend(0, count, kept[0], came[0], qkv, [plane_a, came[1]])]
    held_a, plane_b = stacked(
        [
            [plane_a, swapped(plane_a, "var", 2)],
            [bundle_b, *sent_along_z([bundle_b] * 3)],
        ],
        [sides[0][1]],
    )
    sides.append(attend(count, count, kept[0], came[0], qkv, [plane_b], [sides[0][0]]))
    (held_b,) = stacked([[plane_b, swapped(plane_b, "var", 2)]], [sides[1][1]])
    dmixed, dattn, counted, kept_a, leaving_a, kept_b, leaving_b = middle_pass(
        me,
        [held_a, swapped(held_a, "var", 1), held_b, swapped(held_b, "var", 1)],
        embed,
        kept,
        came,
        [side[1] for side in sides],
        ff,
    )

    def back(side, after):
        _, mixed, scale = sides[side]
        weights = sides[1][0]
        return unattend(me, side * count, count, weights, scale, mixed, dmixed, qkv, hid, after)

    core_a = summed([([core_terms(kept_a, leaving_a)], 2)])
    dproj_a, *joint_a = back(0, core_a[:1])
    sums = summed(
        [y_terms(*core_a), ([core_terms(kept_b, leaving_b), core_terms(*joint_a)], 2)], [dproj_a]
    )
    y_a, core_b = sums[:4], sums[4:]
    dproj_b, *joint_b = back(1, core_b[:1])
    sums = summed([z_terms(*y_a), y_terms(*core_b)], [dproj_b])
    mine_a, y_b = sums[0], sums[1:]
    leaving = last_pass(me, joint, [dproj_a, dproj_b], dattn, kept[0], came[0], *joint_b, [mine_a])
    pair_a = with_other(mine_a)
    mine_b, onward = summed([z_terms(*y_b), ([[leaving[1]]], 1)], [pair_a[1]])
    pair_b = with_other(mine_b)
    rest = summed([([core_terms(leaving[0], onward)], 2)])
    states = []
    for group in (
        (out_proj, out_mean, out_square),
        (up_proj, up_mean, up_square),
        (down_proj, down_mean, down_square),
        (head_weight, head_mean, head_square),
        (norm_params, norm_mean, norm_square),
    ):
        states.extend(group)
    new = step_second(pair_a, pair_b, counted, states)
    first_b = with_other(summed([z_terms(*summed([y_terms(*rest)]))], [new[16]])[0])
    fresh = step_first(
        pair_b,
        first_b,
        [joint_proj, joint_mean, joint_square, embed_weight.T, embed_mean.T, embed_square.T],
    )
    outs, ups, downs, heads, norms = [new[3 * i : 3 * i + 3] for i in range(5)]
    embeds = [e.T for e in fresh[3:6]]
    return (
        new[16].reshape(1),
        embeds[0],
        fresh[0],
        outs[0],
        ups[0],
        downs[0],
        heads[0],
        new[15],
        embeds[1],
        fresh[1],
        outs[1],
        ups[1],
        downs[1],
        heads[1],
        norms[1],
        embeds[2],
        fresh[2],
        outs[2],
        ups[2],
        downs[2],
        heads[2],
        norms[2],
    )


def passed_along(block, axis, distance):
    devices = range(lax.axis_size(axis))
    route = [((i - distance) % len(devices), i) for i in devices]
    return lax.ppermute(block, axis, route)


def layer_norm(resid, gain, shift):
    centre = jnp.mean(resid, -1, keepdims=True)
    offset = resid - centre
    spread = jnp.mean(offset * offset, -1, keepdims=True)
    return offset * lax.rsqrt(spread + 1e-05) * gain + shift


def to_items(matrix, windows, local, parts):
    shaped = matrix.reshape(windows, local, parts, HEADS, HEAD_SIZE).transpose(0, 3, 1, 2, 4)
    return shaped.reshape(windows * HEADS, local, parts * HEAD_SIZE)


def from_items(items, windows, local, parts):
    shaped = items.reshape(windows, HEADS, local, parts, HEAD_SIZE).transpose(0, 2, 3, 1, 4)
    return shaped.reshape(windows * local, parts * HEADS * HEAD_SIZE)


def masked_scores(query_rows, key_portion, markers, query_pos, key_pos):
    score_matrix = (
        jnp.einsum("acn,azn->acz", query_rows, key_portion, preferred_element_type=jnp.float32)
        * 0.125
    )
    allowed = (markers[None, :] > 0.5) | (query_pos[:, None] == key_pos[None, :])
    return jnp.where(allowed[None], score_matrix, -1e30)


def absorb(state, query_rows, paired_keys, markers, query_pos, key_pos):
    peak, totals, accum = state
    score_matrix = masked_scores(
        query_rows, paired_keys[..., :HEAD_SIZE], markers, query_pos, key_pos
    )
    top_new = jnp.maximum(peak, jnp.max(score_matrix, -1))
    rescale = jnp.exp(peak - top_new)
    weights = jnp.exp(score_matrix - top_new[..., None])
    totals = totals * rescale + jnp.sum(weights, -1)
    reduced_weights = weights.astype(jnp.bfloat16)
    accum = accum * rescale[..., None] + jnp.einsum(
        "zsx,zxj->zsj",
        reduced_weights,
        paired_keys[..., HEAD_SIZE:],
        preferred_element_type=jnp.float32,
    )
    return (top_new, totals, accum)


def release(
    dquery, query_rows, paired_keys, markers, query_pos, key_pos, log_total, mixed_gradient, deltas
):
    key_portion = paired_keys[..., :HEAD_SIZE]
    value_rows = paired_keys[..., HEAD_SIZE:]
    score_matrix = masked_scores(query_rows, key_portion, markers, query_pos, key_pos)
    weights = jnp.exp(score_matrix - log_total[..., None])
    weight_gradient = jnp.einsum(
        "acn,azn->acz", mixed_gradient, value_rows, preferred_element_type=jnp.float32
    )
    score_gradient = (weights * (weight_gradient - deltas[..., None])).astype(jnp.bfloat16)
    reduced_weights = weights.astype(jnp.bfloat16)
    dquery = (
        dquery
        + jnp.einsum(
            "zsx,zxj->zsj", score_gradient, key_portion, preferred_element_type=jnp.float32
        )
        * 0.125
    )
    key_gradient = (
        jnp.einsum("fov,foc->fvc", score_gradient, query_rows, preferred_element_type=jnp.float32)
        * 0.125
    )
    value_gradient = jnp.einsum(
        "fov,foc->fvc", reduced_weights, mixed_gradient, preferred_element_type=jnp.float32
    )
    return (dquery, key_gradient, value_gradient)


def empty_state(blocks, length):
    return (
        jnp.full((blocks, length), -1e30, jnp.float32),
        jnp.zeros((blocks, length), jnp.float32),
        jnp.zeros((blocks, length, HEAD_SIZE), jnp.float32),
    )


def attend_forward(items, markers, position, group, local):
    blocks = items.shape[0]
    query_rows = items[..., :HEAD_SIZE]
    paired_keys = items[..., HEAD_SIZE:]
    query_pos = position * local + jnp.arange(local, dtype=jnp.int32)
    state = absorb(
        empty_state(blocks, local), query_rows, paired_keys, markers, query_pos, query_pos
    )

    def turn(counter, carry):
        moving, moving_marks, state = carry
        moving, moving_marks = passed_along((moving, moving_marks), "win", 1)
        key_pos = (position - counter) % group * local + jnp.arange(local, dtype=jnp.int32)
        return (
            moving,
            moving_marks,
            absorb(state, query_rows, moving, moving_marks, query_pos, key_pos),
        )

    _, _, state = lax.fori_loop(1, group, turn, (paired_keys, markers, state))
    peak, totals, accum = state
    mixed_full = accum / totals[..., None]
    return (mixed_full.astype(jnp.bfloat16), (mixed_full, peak + jnp.log(totals)))


def attend_backward(items, markers, mixed_gradient, kept, position, group, local):
    blocks = items.shape[0]
    mixed_full, log_total = kept
    query_rows = items[..., :HEAD_SIZE]
    deltas = jnp.sum(mixed_gradient.astype(jnp.float32) * mixed_full, -1)
    query_pos = position * local + jnp.arange(local, dtype=jnp.int32)

    def turn(counter, carry):
        moving, moving_marks, dquery, dpairs = carry
        key_pos = (position - counter) % group * local + jnp.arange(local, dtype=jnp.int32)
        dquery, key_gradient, value_gradient = release(
            dquery,
            query_rows,
            moving,
            moving_marks,
            query_pos,
            key_pos,
            log_total,
            mixed_gradient,
            deltas,
        )
        dpairs = passed_along(
            (dpairs + jnp.concatenate([key_gradient, value_gradient], -1)).astype(jnp.bfloat16),
            "win",
            1,
        ).astype(jnp.float32)
        moving, moving_marks = passed_along((moving, moving_marks), "win", 1)
        return (moving, moving_marks, dquery, dpairs)

    start = (
        items[..., HEAD_SIZE:],
        markers,
        jnp.zeros((blocks, local, HEAD_SIZE), jnp.float32),
        jnp.zeros((blocks, local, 2 * HEAD_SIZE), jnp.float32),
    )
    _, _, dquery, dpairs = lax.fori_loop(0, group, turn, start)
    return jnp.concatenate([dquery, dpairs], -1).astype(jnp.bfloat16)


def layer_forward(hidden, layer_weights, markers, position, group, windows, local):
    joint, out_mat, up_mat, down_mat, norms = layer_weights
    hidden_low = hidden.astype(jnp.bfloat16)
    items = to_items(
        jnp.dot(hidden_low, joint, preferred_element_type=jnp.float32).astype(jnp.bfloat16),
        windows,
        local,
        3,
    )
    mixed_items, kept_attn = attend_forward(items, markers, position, group, local)
    mixed_low = from_items(mixed_items, windows, local, 1)
    resid_one = hidden + jnp.dot(mixed_low, out_mat, preferred_element_type=jnp.float32)
    middle = layer_norm(resid_one, norms[0], norms[1])
    middle_low = middle.astype(jnp.bfloat16)
    pre_gelu = jnp.dot(middle_low, up_mat, preferred_element_type=jnp.float32)
    activated = jax.nn.gelu(pre_gelu, approximate=False).astype(jnp.bfloat16)
    resid_two = middle + jnp.dot(activated, down_mat, preferred_element_type=jnp.float32)
    result = layer_norm(resid_two, norms[2], norms[3])
    return (
        result,
        (
            hidden_low,
            items,
            kept_attn,
            mixed_low,
            resid_one,
            middle_low,
            pre_gelu,
            activated,
            resid_two,
        ),
    )


def layer_backward(dresult, layer_weights, kept, markers, position, group, windows, local):
    joint, out_mat, up_mat, down_mat, norms = layer_weights
    (
        hidden_low,
        items,
        kept_attn,
        mixed_low,
        resid_one,
        middle_low,
        pre_gelu,
        activated,
        resid_two,
    ) = kept
    _, pull_two = jax.vjp(layer_norm, resid_two, norms[2], norms[3])
    dresid_two, dgain_two, dshift_two = pull_two(dresult)
    dbranch = dresid_two.astype(jnp.bfloat16)
    grad_down = jnp.dot(activated.T, dbranch, preferred_element_type=jnp.float32)
    dactive = jnp.dot(dbranch, down_mat.T, preferred_element_type=jnp.float32)
    _, pull_gelu = jax.vjp(partial(jax.nn.gelu, approximate=False), pre_gelu)
    dpre = pull_gelu(dactive)[0].astype(jnp.bfloat16)
    grad_up = jnp.dot(middle_low.T, dpre, preferred_element_type=jnp.float32)
    dmiddle = dresid_two + jnp.dot(dpre, up_mat.T, preferred_element_type=jnp.float32)
    _, pull_one = jax.vjp(layer_norm, resid_one, norms[0], norms[1])
    dresid_one, dgain_one, dshift_one = pull_one(dmiddle)
    dattn = dresid_one.astype(jnp.bfloat16)
    grad_out = jnp.dot(mixed_low.T, dattn, preferred_element_type=jnp.float32)
    mixed_gradient = jnp.dot(dattn, out_mat.T, preferred_element_type=jnp.float32).astype(
        jnp.bfloat16
    )
    ditems = attend_backward(
        items,
        markers,
        to_items(mixed_gradient, windows, local, 1),
        kept_attn,
        position,
        group,
        local,
    )
    dproj = from_items(ditems, windows, local, 3)
    grad_joint = jnp.dot(hidden_low.T, dproj, preferred_element_type=jnp.float32)
    dhidden = dresid_one + jnp.dot(dproj, joint.T, preferred_element_type=jnp.float32)
    grad_norm = jnp.stack([dgain_one, dshift_one, dgain_two, dshift_two])
    return (dhidden, (grad_joint, grad_out, grad_up, grad_down, grad_norm))


def sliced_windows_body(
    series,
    target,
    valid_slots,
    observed,
    embed_weight,
    joint_proj,
    out_proj,
    up_proj,
    down_proj,
    head_weight,
    norm_params,
    embed_mean,
    joint_mean,
    out_mean,
    up_mean,
    down_mean,
    head_mean,
    norm_mean,
    embed_square,
    joint_square,
    out_square,
    up_square,
    down_square,
    head_square,
    norm_square,
):
    windows = series.shape[0]
    local = series.shape[1]
    row_count = windows * local
    group = lax.axis_size("win")
    position = lax.axis_index("win")
    embed, joint, out_mat, up_mat, down_mat, head_mat, norms_low = (
        lax.all_gather(embed_weight.astype(jnp.bfloat16), "var", axis=1, tiled=True),
        lax.all_gather(joint_proj.astype(jnp.bfloat16), "var", axis=1, tiled=True),
        lax.all_gather(out_proj.astype(jnp.bfloat16), "var", axis=1, tiled=True),
        lax.all_gather(up_proj.astype(jnp.bfloat16), "var", axis=1, tiled=True),
        lax.all_gather(down_proj.astype(jnp.bfloat16), "var", axis=1, tiled=True),
        lax.all_gather(head_weight.astype(jnp.bfloat16), "var", axis=0, tiled=True),
        lax.all_gather(norm_params.astype(jnp.bfloat16), "var", axis=2, tiled=True),
    )
    norms = norms_low.astype(jnp.float32)
    weight_mask = observed.astype(jnp.float32) * valid_slots.astype(jnp.float32)[None, :, None]
    count = jnp.maximum(lax.psum(jnp.sum(weight_mask), ("var", "win")), 1.0)
    markers = valid_slots.astype(jnp.bfloat16)
    centre = jnp.mean(series, -1, keepdims=True)
    offset = series - centre
    spread = jnp.sqrt(jnp.mean(offset * offset, -1, keepdims=True) + 1e-05)
    normed = (offset / spread).astype(jnp.bfloat16).reshape(row_count, -1)
    hidden = jnp.dot(normed, embed, preferred_element_type=jnp.float32)
    layer = 0
    layer_weights = (joint[layer], out_mat[layer], up_mat[layer], down_mat[layer], norms[layer])
    hidden, kept = layer_forward(hidden, layer_weights, markers, position, group, windows, local)
    kept_layers = [kept]
    final_low = hidden.astype(jnp.bfloat16)
    guess = (
        jnp.dot(final_low, head_mat, preferred_element_type=jnp.float32).reshape(windows, local, -1)
        * spread
        + centre
    )
    error = guess - target
    loss_part = jnp.sum(weight_mask * error * error)
    dguess = (
        (2.0 * weight_mask * error / count * spread).reshape(row_count, -1).astype(jnp.bfloat16)
    )
    grad_head = jnp.dot(final_low.T, dguess, preferred_element_type=jnp.float32)
    dhidden = jnp.dot(dguess, head_mat.T, preferred_element_type=jnp.float32)
    layer_grads = [None] * LAYERS
    for layer in reversed(range(LAYERS)):
        layer_weights = (joint[layer], out_mat[layer], up_mat[layer], down_mat[layer], norms[layer])
        dhidden, layer_grads[layer] = layer_backward(
            dhidden, layer_weights, kept_layers[layer], markers, position, group, windows, local
        )
    grad_embed = jnp.dot(normed.T, dhidden.astype(jnp.bfloat16), preferred_element_type=jnp.float32)
    stacked = [jnp.stack([grads[i] for grads in layer_grads]) for i in range(5)]
    summed = (
        lax.psum_scatter(
            grad_embed.astype(jnp.bfloat16), "var", scatter_dimension=1, tiled=True
        ).astype(jnp.float32),
        lax.psum_scatter(
            stacked[0].astype(jnp.bfloat16), "var", scatter_dimension=1, tiled=True
        ).astype(jnp.float32),
        lax.psum_scatter(
            stacked[1].astype(jnp.bfloat16), "var", scatter_dimension=1, tiled=True
        ).astype(jnp.float32),
        lax.psum_scatter(
            stacked[2].astype(jnp.bfloat16), "var", scatter_dimension=1, tiled=True
        ).astype(jnp.float32),
        lax.psum_scatter(
            stacked[3].astype(jnp.bfloat16), "var", scatter_dimension=1, tiled=True
        ).astype(jnp.float32),
        lax.psum_scatter(
            grad_head.astype(jnp.bfloat16), "var", scatter_dimension=0, tiled=True
        ).astype(jnp.float32),
        lax.psum_scatter(
            stacked[4].astype(jnp.bfloat16), "var", scatter_dimension=2, tiled=True
        ).astype(jnp.float32),
    )
    totals = (
        lax.psum(summed[0].astype(jnp.bfloat16), "win").astype(jnp.float32),
        lax.psum(summed[1].astype(jnp.bfloat16), "win").astype(jnp.float32),
        lax.psum(summed[2].astype(jnp.bfloat16), "win").astype(jnp.float32),
        lax.psum(summed[3].astype(jnp.bfloat16), "win").astype(jnp.float32),
        lax.psum(summed[4].astype(jnp.bfloat16), "win").astype(jnp.float32),
        lax.psum(summed[5].astype(jnp.bfloat16), "win").astype(jnp.float32),
        lax.psum(summed[6].astype(jnp.bfloat16), "win").astype(jnp.float32),
    )
    loss = lax.psum(loss_part, ("var", "win")) / count
    count_step = float(STEP_NUMBER)
    weights = (embed_weight, joint_proj, out_proj, up_proj, down_proj, head_weight, norm_params)
    means = (embed_mean, joint_mean, out_mean, up_mean, down_mean, head_mean, norm_mean)
    squares = (
        embed_square,
        joint_square,
        out_square,
        up_square,
        down_square,
        head_square,
        norm_square,
    )
    results = [adamw(weights[i], means[i], squares[i], totals[i], count_step) for i in range(7)]
    return (
        loss.reshape(1),
        results[0][0],
        results[1][0],
        results[2][0],
        results[3][0],
        results[4][0],
        results[5][0],
        totals[6],
        results[0][1],
        results[1][1],
        results[2][1],
        results[3][1],
        results[4][1],
        results[5][1],
        results[6][1],
        results[0][2],
        results[1][2],
        results[2][2],
        results[3][2],
        results[4][2],
        results[5][2],
        results[6][2],
    )


def solution(mesh):
    swaps = mesh.shape["var"] == PARTS and mesh.shape["win"] == 2
    body = whole_windows_body if swaps else sliced_windows_body
    placed = (
        P("var", "win", None),
        P("var", "win", None),
        P("win"),
        P("var", "win", None),
        P(None, "var"),
        P(None, "var", None),
        P(None, "var", None),
        P(None, "var", None),
        P(None, "var", None),
        P("var", None),
        P(None, None, "var"),
        P(None, "var"),
        P(None, "var", None),
        P(None, "var", None),
        P(None, "var", None),
        P(None, "var", None),
        P("var", None),
        P(None, None, "var"),
        P(None, "var"),
        P(None, "var", None),
        P(None, "var", None),
        P(None, "var", None),
        P(None, "var", None),
        P("var", None),
        P(None, None, "var"),
    )
    return jax.shard_map(
        body,
        mesh=mesh,
        in_specs=placed,
        out_specs=(
            P(),
            P(None, "var"),
            P(None, "var", None),
            P(None, "var", None),
            P(None, "var", None),
            P(None, "var", None),
            P("var", None),
            P(None, None, "var"),
            P(None, "var"),
            P(None, "var", None),
            P(None, "var", None),
            P(None, "var", None),
            P(None, "var", None),
            P("var", None),
            P(None, None, "var"),
            P(None, "var"),
            P(None, "var", None),
            P(None, "var", None),
            P(None, "var", None),
            P(None, "var", None),
            P("var", None),
            P(None, None, "var"),
        ),
        check_vma=False,
    )
```
